512 devices in a mesh: cand: 64 (over x, z, core), mp: 8 (over y).
Axes of the slice: x: 4, y: 8, z: 8, core: 2. Of those that a mesh axis runs over, the one named last changes fastest.
Arguments:
- passages: bfloat16 [512, 64, 4096], P('cand', None, 'mp'), may hold values from -6 to 6
- norm_gain: float32 [4096], replicated, may hold values from 0.1 to 1.9
- w_qkv: bfloat16 [3, 4096, 2048], P(None, 'cand', 'mp'), as said below
- w_out: bfloat16 [2048, 4096], P('mp', 'cand'), may hold values from -0.5 to 0.5
- counts: int32 [512], P('cand'), may hold values from 1 to 63
- owners: int32 [512], P('cand'), may hold values from 0 to 63, as said below
- query_of: int32 [512], P('cand'), may hold values from 0 to 15
Outputs:
- mixed: bfloat16 [16384, 4096], P(('cand', 'mp'))
The draws below stay inside these ranges and needn't reach their ends.
Inputs may be any that keep to these rules, and one draw needn't show every extreme that they name: `owners`: A passage's owner is the device holding it or one of its two neighbours along cand, cyclically; every device hands exactly 2 passages to each neighbour; the passages of one owner hold at most 256 tokens, and some owner exactly 256. `w_qkv`: projection weights.
All inputs are finite; a program needn't handle non-finite values.
Results may differ from the reference program's by a relative error of at most 0.02.
Values may be sent and summed in bfloat16 or wider, within the bound.
No kernel may reach another device: no remote copies, remote signals or barrier semaphores. Data moves between devices by JAX's collectives and lax.ppermute only.
A program may use at most 64 MiB of HBM per device.

```python
import math
import jax
import jax.numpy as jnp
from jax import lax

D = 4096
HEADS = 16
HD = 128
L = 64
PD = 8
TCAP = 256
PASSAGES = 512
QUERIES = 16
N_CAND = 64


def spill_layout(key):
    devices = PASSAGES // PD
    kept_pairs = (PD - 8) // 2
    sub_keys = jax.random.split(key, 8)
    heat_flag = jax.random.randint(sub_keys[0], (devices,), 0, 2)
    pair_ones = jnp.ones((1, 2), jnp.int32)
    sender_heat = jnp.concatenate([jnp.roll(heat_flag, 1)[:, None] * pair_ones, jnp.roll(heat_flag, -1)[:, None] * pair_ones], axis=1)
    long_part = jax.random.randint(sub_keys[1], (devices, 4), L // 2, L)
    short_part = jax.random.randint(sub_keys[2], (devices, 4), 1, L // 4 + 1)
    recv_len = jnp.where(sender_heat == 1, long_part, short_part)
    forced = jax.random.randint(sub_keys[3], (), 0, devices)
    is_forced = (jnp.arange(devices) == forced)[:, None]
    first_col = (jnp.arange(4) == 0)[None, :]
    recv_len = jnp.where(is_forced & first_col, L - 1, recv_len)
    partner_len = jax.random.randint(sub_keys[4], (devices, 4), 1, L - recv_len + 1)
    partner_len = jnp.where(is_forced, L - recv_len, partner_len)
    pair_first = jax.random.randint(sub_keys[5], (devices, kept_pairs), 1, L)
    pair_second = jax.random.randint(sub_keys[6], (devices, kept_pairs), 1, L - pair_first + 1)
    pair_second = jnp.where(is_forced, L - pair_first, pair_second)
    pair_lengths = jnp.stack([pair_first, pair_second], axis=-1).reshape(devices, 2 * kept_pairs)
    owner_len = jnp.concatenate([recv_len[:, :2], partner_len, pair_lengths, recv_len[:, 2:]], axis=1)
    device_ids = jnp.arange(devices, dtype=jnp.int32)[:, None]
    anchor_len = jnp.concatenate([owner_len[:, 2:PD - 2], jnp.roll(owner_len, -1, axis=0)[:, :2], jnp.roll(owner_len, 1, axis=0)[:, PD - 2:]], axis=1)
    anchor_owner = jnp.concatenate([jnp.broadcast_to(device_ids, (devices, PD - 4)), jnp.broadcast_to((device_ids + 1) % devices, (devices, 2)), jnp.broadcast_to((device_ids + devices - 1) % devices, (devices, 2))], axis=1)
    shuffle_key = jax.random.randint(sub_keys[7], (devices, PD), 0, 1 << 20) * PD + jnp.arange(PD)[None, :]
    shuffle = jnp.argsort(shuffle_key, axis=1)
    counts_out = jnp.take_along_axis(anchor_len, shuffle, axis=1).reshape(-1).astype(jnp.int32)
    owners_out = jnp.take_along_axis(anchor_owner, shuffle, axis=1).reshape(-1).astype(jnp.int32)
    return (counts_out, owners_out)


def draw_counts(key, part):
    counts_out, owners_out = spill_layout(key)
    return counts_out


def draw_owners(key, part):
    counts_out, owners_out = spill_layout(key)
    return owners_out


def draw_w_qkv(key, part):
    key = jax.random.fold_in(key, 7)
    first_key = jax.random.fold_in(key, 0)
    width = HEADS * HD
    base = jax.random.normal(first_key, (3, D, width), jnp.float32) * D ** (-0.5)
    return base.astype(jnp.bfloat16)


def touch_ends(entries, key, least, largest):
    shape = entries.shape
    index_at = [jax.random.randint(jax.random.fold_in(key, axis), (), 0, shape[axis]) for axis in range(len(shape))]
    entries = entries.at[tuple(index_at)].set(least)
    longest = shape.index(max(shape))
    index_at[longest] = (index_at[longest] + 1) % shape[longest]
    return entries.at[tuple(index_at)].set(largest)


def block_levels(rng, shape, cuts, smallest, largest):
    gain = 1.0
    for dim, shards_of in cuts:
        heights = jax.random.uniform(jax.random.fold_in(jax.random.fold_in(rng, 6), dim), (shards_of,), jnp.float32, smallest / len(cuts), largest / len(cuts))
        gain = gain * jnp.repeat(jnp.exp(heights), shape[dim] // shards_of).reshape((-1,) + (1,) * (len(shape) - 1 - dim))
    return gain


def scatter_about(key, extent, scale, bound, shards=(), kind=jnp.bfloat16):
    array = jax.random.normal(key, extent, jnp.float32) * scale
    if len(shards) > 0:
        array = block_levels(key, extent, shards, -0.22, 0.18) * array
    return jnp.clip(array, min=-bound, max=bound).astype(kind)


def setup_inputs(seed: int = 0) -> dict:
    key_list = jax.random.split(jax.random.key(seed), 8)
    passages = scatter_about(key_list[0], (PASSAGES, L, D), 1.0, 6.0, ((0, 64), (2, 8)))
    norm_gain = jnp.clip(1.0 + 0.18 * jax.random.normal(key_list[1], (D,), jnp.float32), 0.1, 1.9)
    w_qkv = draw_w_qkv(jax.random.fold_in(key_list[7], 71), 0)
    w_out = scatter_about(key_list[3], (HEADS * HD, D), (HEADS * HD // 16) ** -0.5, 0.5, ((0, 8), (1, 64)))
    counts = draw_counts(jax.random.fold_in(key_list[7], 71), 0)
    owners = draw_owners(jax.random.fold_in(key_list[7], 71), 0)
    query_of = touch_ends(jax.random.randint(key_list[6], (PASSAGES,), 0, QUERIES), jax.random.fold_in(key_list[6], 1), 0, QUERIES - 1).astype(jnp.int32)
    return dict(passages=passages, norm_gain=norm_gain, w_qkv=w_qkv, w_out=w_out, counts=counts, owners=owners, query_of=query_of)


EPS = 1e-05
NEGATIVE = -1e+30

def owned_lists(owner_table, slot_count, devices):
    total = owner_table.shape[0]
    order_key = jnp.arange(total, dtype=jnp.int32)
    holder = order_key // slot_count
    target = jnp.arange(devices, dtype=jnp.int32)[:, None]
    source_rank = jnp.where(holder[None, :] == (target + devices - 1) % devices, 0, jnp.where(holder[None, :] == target, 1, 2)).astype(jnp.int32)
    sort_key = jnp.where(owner_table[None, :] == target, source_rank * total + order_key[None, :], 3 * total + order_key[None, :])
    return jnp.argsort(sort_key, axis=1)[:, :slot_count].astype(jnp.int32)

def rms_normed(flat_rows, gain_row):
    values = flat_rows.astype(jnp.float32)
    inv_scale = lax.rsqrt(lax.optimization_barrier(jnp.mean(values * values, axis=-1, keepdims=True)) + EPS)
    return (values * inv_scale * gain_row.astype(jnp.float32)).astype(jnp.bfloat16)

def pack_layout(lengths, capacity):
    slot_count = lengths.shape[0]
    slot_ends = jnp.cumsum(lengths).astype(jnp.int32)
    starts = (slot_ends - lengths).astype(jnp.int32)
    position = jnp.arange(capacity, dtype=jnp.int32)
    which_slot = jnp.minimum(lax.optimization_barrier(jnp.sum((position[:, None] >= slot_ends[None, :]).astype(jnp.int32), axis=1)).astype(jnp.int32), slot_count - 1)
    onehot = (which_slot[:, None] == jnp.arange(slot_count, dtype=jnp.int32)[None, :]).astype(jnp.int32)
    offset = (position - lax.optimization_barrier(jnp.sum(onehot * starts[None, :], axis=1))).astype(jnp.int32)
    is_valid = position < slot_ends[slot_count - 1]
    return (which_slot, offset, is_valid, starts)

def softmax_mix(queries, keys, values, inter_keys, inter_values, local_mask, inter_mask):
    inv_scale = 1.0 / math.sqrt(queries.shape[-1])
    local_scores = jnp.einsum('thd,shd->hts', queries.astype(jnp.float32), keys.astype(jnp.float32)) * inv_scale
    inter_scores = jnp.einsum('thd,phd->htp', queries.astype(jnp.float32), inter_keys.astype(jnp.float32)) * inv_scale
    scores = jnp.concatenate([local_scores, inter_scores], axis=-1)
    allowed = jnp.concatenate([local_mask, inter_mask], axis=-1)[None]
    row_peak = lax.optimization_barrier(jnp.max(jnp.where(allowed, scores, NEGATIVE), axis=-1, keepdims=True))
    raised = jnp.where(allowed, jnp.exp(scores - row_peak), 0.0)
    weights = (raised / lax.optimization_barrier(jnp.sum(raised, axis=-1, keepdims=True))).astype(jnp.bfloat16)
    split_at = keys.shape[0]
    mixed_rows = jnp.einsum('hts,shd->thd', weights[..., :split_at].astype(jnp.float32), values.astype(jnp.float32))
    mixed_rows = mixed_rows + jnp.einsum('htp,phd->thd', weights[..., split_at:].astype(jnp.float32), inter_values.astype(jnp.float32))
    return mixed_rows

def reference(passages, norm_gain, w_qkv, w_out, counts, owners, query_of):
    owner_table = owned_lists(owners, PD, N_CAND)
    first_normed = rms_normed(passages[:, 0, :], norm_gain)
    inter_keys = jnp.dot(first_normed, w_qkv[1], preferred_element_type=jnp.float32).astype(jnp.bfloat16).reshape(PASSAGES, HEADS, HD)
    inter_values = jnp.dot(first_normed, w_qkv[2], preferred_element_type=jnp.float32).astype(jnp.bfloat16).reshape(PASSAGES, HEADS, HD)
    inter_ids = jnp.arange(PASSAGES, dtype=jnp.int32)

    def owner_block(my_ids):
        lengths = jnp.take(counts, my_ids)
        which_slot, offset, is_valid, starts = pack_layout(lengths, TCAP)
        flat_rows = jnp.take(passages, my_ids, axis=0).reshape(PD * L, D)
        source_row = which_slot * L + jnp.where(is_valid, offset, 0)
        packed = jnp.where(is_valid[:, None], jnp.take(flat_rows, source_row, axis=0), jnp.zeros((), jnp.bfloat16))
        normed = rms_normed(packed, norm_gain)
        queries = jnp.dot(normed, w_qkv[0], preferred_element_type=jnp.float32).astype(jnp.bfloat16).reshape(TCAP, HEADS, HD)
        keys = jnp.dot(normed, w_qkv[1], preferred_element_type=jnp.float32).astype(jnp.bfloat16).reshape(TCAP, HEADS, HD)
        values = jnp.dot(normed, w_qkv[2], preferred_element_type=jnp.float32).astype(jnp.bfloat16).reshape(TCAP, HEADS, HD)
        row_ids = jnp.take(my_ids, which_slot)
        row_query = jnp.take(query_of, row_ids)
        same_slot = which_slot[:, None] == which_slot[None, :]
        local_mask = same_slot & is_valid[:, None] & is_valid[None, :] | jnp.eye(TCAP, dtype=bool)
        inter_mask = (row_query[:, None] == query_of[None, :]) & (row_ids[:, None] != inter_ids[None, :])
        attended = softmax_mix(queries, keys, values, inter_keys, inter_values, local_mask, inter_mask)
        attended = jnp.where(is_valid[:, None], attended.reshape(TCAP, HEADS * HD), 0.0).astype(jnp.bfloat16)
        projected = jnp.dot(attended, w_out, preferred_element_type=jnp.float32)
        return (packed.astype(jnp.float32) + projected).astype(jnp.bfloat16)
    blocks = lax.map(owner_block, owner_table)
    return blocks.reshape(N_CAND * TCAP, D)
```

```python
import math

import jax
import jax.numpy as jnp
from jax import lax
from jax.experimental import pallas as pl
from jax.experimental.pallas import tpu as pltpu
from jax.sharding import PartitionSpec as P

HD = 128
EPS = 1e-05
NEGATIVE = -1e30
VMEM_LIMIT = 48 * 1024 * 1024
F32 = jnp.float32
BF16 = jnp.bfloat16
NT = (((1,), (1,)), ((), ()))


def along(shard, axis, by):
    length = lax.axis_size(axis)
    return lax.ppermute(shard, axis, [(i, (i + by) % length) for i in range(length)])


def to_sibling(shard):
    length = lax.axis_size("cand")
    return lax.ppermute(shard, "cand", [(i, i ^ 1) for i in range(length)])


def same_core_groups():
    length = lax.axis_size("cand")
    return [list(range(core, length, 2)) for core in range(2)]


def pick_kernel(owners, counts, query_of, passages, right, left, kept):
    me = lax.axis_index("cand")
    devices = lax.axis_size("cand")
    slots, length, width = passages.shape
    row = lax.broadcasted_iota(jnp.int32, (16, width), 0)
    lane = lax.broadcasted_iota(jnp.int32, (16, width), 1)
    number = [jnp.int32(0)] * 3
    targets = (right, left, kept)
    for slot in range(slots):
        ahead = lax.rem(owners[slot] - me + devices, devices)
        facts = jnp.where(lane < width // 2, counts[slot], query_of[slot]).astype(F32)
        tail = passages[slot, length - 16 :, :].astype(F32)
        tail = jnp.where(row == 15, facts, tail).astype(BF16)
        for which, wanted in enumerate((1, devices - 1, 0)):
            target = targets[which]
            hit = ahead == wanted
            place = jnp.minimum(number[which], target.shape[0] - 1)

            @pl.when(hit)
            def _():
                target[place, : length - 16, :] = passages[slot, : length - 16, :]
                target[place, length - 16 :, :] = tail

            number[which] = number[which] + hit.astype(jnp.int32)


def pick(owners, counts, query_of, passages):
    slots, length, width = passages.shape
    smem = pl.BlockSpec(memory_space=pltpu.SMEM)
    vmem = pl.BlockSpec(memory_space=pltpu.VMEM)
    shape = lambda n: jax.ShapeDtypeStruct((n, length, width), BF16)
    return pl.pallas_call(
        pick_kernel,
        out_shape=(shape(2), shape(2), shape(slots - 4)),
        in_specs=[smem, smem, smem, vmem],
        out_specs=(vmem, vmem, vmem),
        compiler_params=pltpu.CompilerParams(vmem_limit_bytes=VMEM_LIMIT),
    )(owners, counts, query_of, passages)


def pack_kernel(from_left, kept, from_right, packed, facts):
    rows = packed.shape[0]
    length = kept.shape[1]
    blocks = (
        [from_left[i] for i in range(from_left.shape[0])]
        + [kept[i] for i in range(kept.shape[0])]
        + [from_right[i] for i in range(from_right.shape[0])]
    )
    position = lax.broadcasted_iota(jnp.int32, (rows, length), 0)
    offset = lax.broadcasted_iota(jnp.int32, (rows, length), 1)
    start = jnp.zeros((1, length), jnp.int32)
    total = jnp.zeros(packed.shape, F32)
    for slot, block in enumerate(blocks):
        fact = block[length - 16 :, :].astype(F32)[15:16, :]
        facts[slot : slot + 1, :] = fact
        count = fact[:, :length].astype(jnp.int32)
        chosen = (position == start + offset) & (offset < count)
        total = total + jnp.dot(
            chosen.astype(F32).astype(BF16), block, preferred_element_type=F32
        )
        start = start + count
    packed[...] = total.astype(BF16)


def pack(from_left, kept, from_right):
    slots = from_left.shape[0] + kept.shape[0] + from_right.shape[0]
    length, width = kept.shape[1:]
    vmem = pl.BlockSpec(memory_space=pltpu.VMEM)
    return pl.pallas_call(
        pack_kernel,
        out_shape=(
            jax.ShapeDtypeStruct((slots * length // 2, width), BF16),
            jax.ShapeDtypeStruct((slots, width), F32),
        ),
        in_specs=[vmem] * 3,
        out_specs=(vmem, vmem),
        compiler_params=pltpu.CompilerParams(vmem_limit_bytes=VMEM_LIMIT),
    )(from_left, kept, from_right)


def project_kernel(order, *refs):
    pieces, (gain, weights, facts, queries, keys, values, residual, sent, rows_in, total, squares) = (
        refs[:9],
        refs[9:],
    )
    step = pl.program_id(0)
    rows, width = rows_in.shape
    for number in range(7):

        @pl.when(step == number)
        def _():
            rows_in[...] = pieces[number][...]

    @pl.when(step == 7)
    def _():
        rows_in[: rows // 2, :] = pieces[7][...]
        rows_in[rows // 2 :, :] = pieces[8][...]

    @pl.when(step == 0)
    def _():
        total[...] = jnp.zeros_like(total)
        squares[...] = jnp.zeros_like(squares)

    share = residual.shape[0]
    residual[...] = rows_in[pl.ds(pl.multiple_of(order[0] * share, share), share), :]
    x = rows_in[...].astype(F32)
    squares[...] += jnp.sum(x * x, axis=1, keepdims=True)
    scaled = (x * gain[0]).astype(BF16)
    columns = weights.shape[2]
    depth = weights.shape[1] // 3
    for part in range(3):
        block = weights[:, part * depth : (part + 1) * depth, :].reshape(-1, columns)
        total[:, part * columns : (part + 1) * columns] += jnp.dot(
            scaled, block, preferred_element_type=F32
        )

    @pl.when(step == 7)
    def _():
        inverse = lax.rsqrt(squares[...] / (8 * width) + EPS)
        done = [
            (total[:, part * columns : (part + 1) * columns] * inverse).astype(BF16)
            for part in range(3)
        ]
        queries[...], keys[...], values[...] = done
        slots = facts.shape[0]
        slot_of = lax.broadcasted_iota(jnp.int32, (2 * slots, rows), 0) % slots
        place = lax.broadcasted_iota(jnp.int32, (2 * slots, rows), 1)
        start = jnp.zeros((1, rows), jnp.int32)
        first = jnp.zeros((2 * slots, rows), jnp.int32)
        asked = jnp.zeros((2 * slots, HD), jnp.int32)
        for slot in range(slots):
            here = slot_of == slot
            first = jnp.where(here, start, first)
            asked = jnp.where(
                here[:, :HD], facts[slot : slot + 1, width // 2 : width // 2 + HD].astype(jnp.int32), asked
            )
            start = start + facts[slot : slot + 1, :rows].astype(jnp.int32)
        chosen = (first == place).astype(F32).astype(BF16)
        mark = (asked == place[:, :HD]).astype(F32).astype(BF16)
        key_rows = jnp.dot(chosen, done[1], preferred_element_type=F32).astype(BF16)
        value_rows = jnp.dot(chosen, done[2], preferred_element_type=F32).astype(BF16)
        for copy in range(sent.shape[0] // (2 * slots)):
            there = slice(copy * 2 * slots, (copy + 1) * 2 * slots)
            sent[there, :columns] = key_rows
            sent[there, columns : 2 * columns] = value_rows
            sent[there, 2 * columns :] = mark


def project(order, pieces, gain, weights, facts, copies):
    rows, width = pieces[0].shape
    columns = weights.shape[2]
    slots = facts.shape[0]
    whole = lambda array: pl.BlockSpec(array.shape, lambda r, order: (0,) * array.ndim)
    out = lambda *shape: (
        jax.ShapeDtypeStruct(shape, BF16),
        pl.BlockSpec(shape, lambda r, order: (0, 0)),
    )
    outs = [out(rows, columns)] * 3
    outs.append(
        (
            jax.ShapeDtypeStruct((rows // 8, 8 * width), BF16),
            pl.BlockSpec((rows // 8, width), lambda r, order: (0, order[r])),
        )
    )
    outs.append(out(copies * slots, 2 * columns + HD))
    return pl.pallas_call(
        project_kernel,
        out_shape=tuple(o[0] for o in outs),
        grid_spec=pltpu.PrefetchScalarGridSpec(
            num_scalar_prefetch=1,
            grid=(8,),
            in_specs=[whole(piece) for piece in pieces]
            + [
                pl.BlockSpec((1, 1, width), lambda r, order: (order[r], 0, 0)),
                pl.BlockSpec((8, 192, columns), lambda r, order: (order[r], 0, 0)),
                whole(facts),
            ],
            out_specs=tuple(o[1] for o in outs),
            scratch_shapes=[
                pltpu.VMEM((rows, width), BF16),
                pltpu.VMEM((rows, 3 * columns), F32),
                pltpu.VMEM((rows, 1), F32),
            ],
        ),
        compiler_params=pltpu.CompilerParams(vmem_limit_bytes=VMEM_LIMIT),
    )(order, *pieces, gain, weights, facts)


def attend_kernel(queries, keys, values, near, far, facts, weights, out):
    rows, columns = queries.shape
    slots = facts.shape[0]
    half = facts.shape[1] // 2
    here = lax.axis_index("cand") // 2 * slots
    down = lax.broadcasted_iota(jnp.int32, (rows, rows), 0)
    across = lax.broadcasted_iota(jnp.int32, (rows, rows), 1)
    slot_down = jnp.zeros((rows, rows), jnp.int32)
    slot_across = jnp.zeros((rows, rows), jnp.int32)
    end = jnp.zeros((1, rows), jnp.int32)
    for slot in range(slots):
        end = end + facts[slot : slot + 1, :rows].astype(jnp.int32)
        if slot < slots - 1:
            slot_down = slot_down + (down >= end).astype(jnp.int32)
            slot_across = slot_across + (across >= end).astype(jnp.int32)
    asked = jnp.zeros((rows, HD), jnp.int32)
    for slot in range(slots):
        asked = jnp.where(
            slot_down[:, :HD] == slot,
            facts[slot : slot + 1, half : half + HD].astype(jnp.int32),
            asked,
        )
    local = ((slot_down == slot_across) & (down < end) & (across < end)) | (down == across)
    mark = (asked == across[:, :HD]).astype(F32).astype(BF16)
    same = lambda other: lax.dot_general(
        mark, other[:, 2 * columns :], NT, preferred_element_type=F32
    ) > 0.5
    masks = [local, same(near) & (across != here + slot_down), same(far)]
    scale = 1.0 / math.sqrt(HD)
    heads = []
    for head in range(columns // HD):
        lanes = slice(head * HD, (head + 1) * HD)
        value_lanes = slice(columns + head * HD, columns + (head + 1) * HD)
        query = queries[:, lanes]
        scores = [
            jnp.where(
                mask,
                lax.dot_general(query, key, NT, preferred_element_type=F32) * scale,
                NEGATIVE,
            )
            for mask, key in zip(masks, (keys[:, lanes], near[:, lanes], far[:, lanes]))
        ]
        peak = jnp.maximum(jnp.maximum(scores[0], scores[1]), scores[2])
        peak = jnp.max(peak, axis=1, keepdims=True)
        raised = [jnp.exp(score - peak) for score in scores]
        bottom = jnp.sum(raised[0] + raised[1] + raised[2], axis=1, keepdims=True)
        top = jnp.zeros((rows, HD), F32)
        for part, value in zip(raised, (values[:, lanes], near[:, value_lanes], far[:, value_lanes])):
            top = top + jnp.dot(part.astype(BF16), value, preferred_element_type=F32)
        heads.append(jnp.where(down[:, :HD] < end[:, :HD], top / bottom, 0.0).astype(BF16))
    attended = jnp.concatenate(heads, axis=1)
    chunk = 8
    for first in range(0, weights.shape[0], chunk):
        block = weights[first : first + chunk].reshape(-1, columns)
        width = block.shape[0]
        at = first * weights.shape[1]
        out[:, at : at + width] = lax.dot_general(
            attended, block, NT, preferred_element_type=F32
        ).astype(BF16)


def attend(queries, keys, values, near, far, facts, weights):
    rows, columns = queries.shape
    vmem = pl.BlockSpec(memory_space=pltpu.VMEM)
    whole = lambda array: pl.BlockSpec(array.shape, lambda i: (0,) * array.ndim)
    depth = weights.shape[1] // 4
    width = weights.shape[0] * depth
    small = (queries, keys, values, near, far, facts)
    return pl.pallas_call(
        attend_kernel,
        out_shape=jax.ShapeDtypeStruct((rows, width), BF16),
        grid=(1,),
        in_specs=[whole(array) for array in small]
        + [pl.BlockSpec((weights.shape[0], depth, columns), lambda i: (0, 3, 0))],
        out_specs=pl.BlockSpec((rows, width), lambda i: (0, 0)),
        compiler_params=pltpu.CompilerParams(vmem_limit_bytes=VMEM_LIMIT),
    )(*small, weights)


def shards(passages, norm_gain, w_qkv, w_out, counts, owners, query_of):
    devices = lax.axis_size("cand")
    parts = lax.axis_size("mp")
    me = lax.axis_index("mp")
    columns = w_qkv.shape[2]
    with jax.named_scope("weights_gathered"):
        own_weights = jnp.concatenate([w_qkv.reshape(-1, columns), w_out.T], axis=0)
        weights = lax.all_gather(own_weights, "cand", axis=0, tiled=False)
    with jax.named_scope("passages_handed_over"):
        right, left, kept = pick(owners, counts, query_of, passages)
        from_left = along(right, "cand", 1)
        from_right = along(left, "cand", -1)
        packed, facts = pack(from_left, kept, from_right)
    with jax.named_scope("features_gathered"):
        half = packed.shape[0] // 2
        up, down = [packed], [packed]
        for _ in range(3):
            up.append(along(up[-1], "mp", 1))
            down.append(along(down[-1], "mp", -1))
        last = [along(up[3][:half], "mp", 1), along(down[3][half:], "mp", -1)]
        pieces = [packed, up[1], down[1], up[2], down[2], up[3], down[3]] + last
    order = lax.rem(me + jnp.array([0, 7, 1, 6, 2, 5, 3, 4], jnp.int32), parts)
    gain = norm_gain.reshape(parts, 1, -1)
    queries, keys, values, residual, sent = project(
        order, pieces, gain, weights, facts, devices // 2
    )
    with jax.named_scope("interaction_gathered"):
        near = lax.all_to_all(
            sent, "cand", 0, 0, tiled=True, axis_index_groups=same_core_groups()
        )
        far = to_sibling(near)
    partial = attend(queries, keys, values, near, far, facts, weights)
    with jax.named_scope("heads_summed"):
        summed = lax.psum_scatter(partial, "mp", scatter_dimension=0, tiled=True)
    return (residual.astype(F32) + summed.astype(F32)).astype(BF16)


def solution(mesh):
    in_specs = (
        P("cand", None, "mp"),
        P(),
        P(None, "cand", "mp"),
        P("mp", "cand"),
        P("cand"),
        P("cand"),
        P("cand"),
    )
    out_specs = P(("cand", "mp"), None)
    return jax.shard_map(shards, mesh=mesh, in_specs=in_specs, out_specs=out_specs, check_vma=False)
```

```python
import math

import jax
import jax.numpy as jnp
from jax import lax
from jax.experimental import pallas as pl
from jax.experimental.pallas import tpu as pltpu
from jax.sharding import PartitionSpec as P

HD = 128
EPS = 1e-05
NEGATIVE = -1e30
VMEM_LIMIT = 48 * 1024 * 1024
F32 = jnp.float32
BF16 = jnp.bfloat16
NT = (((1,), (1,)), ((), ()))


def along(shard, axis, by):
    length = lax.axis_size(axis)
    return lax.ppermute(shard, axis, [(i, (i + by) % length) for i in range(length)])


def to_sibling(shard):
    length = lax.axis_size("cand")
    return lax.ppermute(shard, "cand", [(i, i ^ 1) for i in range(length)])


def same_core_groups():
    length = lax.axis_size("cand")
    return [list(range(core, length, 2)) for core in range(2)]


ALONG_Z = 8


def x_groups():
    length = lax.axis_size("cand")
    step = 2 * ALONG_Z
    return [
        [x + 2 * z + core for x in range(0, length, step) for core in range(2)]
        for z in range(ALONG_Z)
    ]


def z_groups():
    length = lax.axis_size("cand")
    step = 2 * ALONG_Z
    return [
        [x + 2 * z + core for z in range(ALONG_Z)]
        for x in range(0, length, step)
        for core in range(2)
    ]


def one_way(shard):
    chips, parts = lax.axis_size("cand"), lax.axis_size("mp")
    pairs = []
    for device in range(chips):
        by = 1 if device % 2 == 0 else parts - 1
        for part in range(parts):
            pairs.append((device * parts + part, device * parts + (part + by) % parts))
    return lax.ppermute(shard, ("cand", "mp"), pairs)


def pick_kernel(owners, counts, query_of, passages, right, left, kept):
    me = lax.axis_index("cand")
    devices = lax.axis_size("cand")
    slots, length, width = passages.shape
    row = lax.broadcasted_iota(jnp.int32, (16, width), 0)
    lane = lax.broadcasted_iota(jnp.int32, (16, width), 1)
    number = [jnp.int32(0)] * 3
    targets = (right, left, kept)
    for slot in range(slots):
        ahead = lax.rem(owners[slot] - me + devices, devices)
        facts = jnp.where(lane < width // 2, counts[slot], query_of[slot]).astype(F32)
        tail = passages[slot, length - 16 :, :].astype(F32)
        tail = jnp.where(row == 15, facts, tail).astype(BF16)
        for which, wanted in enumerate((1, devices - 1, 0)):
            target = targets[which]
            hit = ahead == wanted
            place = jnp.minimum(number[which], target.shape[0] - 1)

            @pl.when(hit)
            def _():
                target[place, : length - 16, :] = passages[slot, : length - 16, :]
                target[place, length - 16 :, :] = tail

            number[which] = number[which] + hit.astype(jnp.int32)


def pick(owners, counts, query_of, passages):
    slots, length, width = passages.shape
    smem = pl.BlockSpec(memory_space=pltpu.SMEM)
    vmem = pl.BlockSpec(memory_space=pltpu.VMEM)
    shape = lambda n: jax.ShapeDtypeStruct((n, length, width), BF16)
    return pl.pallas_call(
        pick_kernel,
        out_shape=(shape(2), shape(2), shape(slots - 4)),
        in_specs=[smem, smem, smem, vmem],
        out_specs=(vmem, vmem, vmem),
        compiler_params=pltpu.CompilerParams(vmem_limit_bytes=VMEM_LIMIT),
    )(owners, counts, query_of, passages)


def pack_kernel(from_left, kept, from_right, packed):
    length = kept.shape[1]
    blocks = (
        [from_left[i] for i in range(from_left.shape[0])]
        + [kept[i] for i in range(kept.shape[0])]
        + [from_right[i] for i in range(from_right.shape[0])]
    )
    rows = len(blocks) * length // 2
    position = lax.broadcasted_iota(jnp.int32, (rows, length), 0)
    offset = lax.broadcasted_iota(jnp.int32, (rows, length), 1)
    width = packed.shape[1]
    slot_of = lax.broadcasted_iota(jnp.int32, (16, width), 0)
    start = jnp.zeros((1, length), jnp.int32)
    total = jnp.zeros((rows, width), F32)
    facts = jnp.zeros((16, width), F32)
    for slot, block in enumerate(blocks):
        fact = block[length - 16 :, :].astype(F32)[15:16, :]
        facts = jnp.where(slot_of == slot, fact, facts)
        count = fact[:, :length].astype(jnp.int32)
        chosen = (position == start + offset) & (offset < count)
        total = total + jnp.dot(
            chosen.astype(F32).astype(BF16), block, preferred_element_type=F32
        )
        start = start + count
    packed[:rows, :] = total.astype(BF16)
    packed[rows:, :] = facts.astype(BF16)


def pack(from_left, kept, from_right):
    slots = from_left.shape[0] + kept.shape[0] + from_right.shape[0]
    length, width = kept.shape[1:]
    vmem = pl.BlockSpec(memory_space=pltpu.VMEM)
    return pl.pallas_call(
        pack_kernel,
        out_shape=jax.ShapeDtypeStruct((slots * length // 2 + 16, width), BF16),
        in_specs=[vmem] * 3,
        out_specs=vmem,
        compiler_params=pltpu.CompilerParams(vmem_limit_bytes=VMEM_LIMIT),
    )(from_left, kept, from_right)


def project_kernel(order, *refs):
    mine, theirs, *pieces = refs[:10]
    gain, weights, queries, keys, values, residual, sent, rows_in, total, squares = refs[10:]
    step = pl.program_id(0)
    rows, width = rows_in.shape
    half = rows // 2

    @pl.when(step == 0)
    def _():
        rows_in[:half, :] = mine[:half, :]
        rows_in[half:, :] = theirs[:half, :]
        total[...] = jnp.zeros_like(total)
        squares[...] = jnp.zeros_like(squares)

    for number in range(3):

        @pl.when(step == 1 + 2 * number)
        def _():
            rows_in[...] = pieces[2 * number][...]

        @pl.when(step == 2 + 2 * number)
        def _():
            rows_in[:half, :] = pieces[2 * number + 1][half:, :]
            rows_in[half:, :] = pieces[2 * number + 1][:half, :]

    @pl.when(step == 7)
    def _():
        rows_in[:half, :] = pieces[6][...]
        rows_in[half:, :] = pieces[7][...]

    share = residual.shape[0]
    row = pl.multiple_of(order[8] * share, share)
    residual[...] = rows_in[pl.ds(row, share), :]
    x = rows_in[...].astype(F32)
    squares[...] += jnp.sum(x * x, axis=1, keepdims=True)
    scaled = (x * gain[0]).astype(BF16)
    depth = weights.shape[3] // 3
    block = jnp.concatenate(
        [
            weights[:, 0, :, part * depth : (part + 1) * depth, :].reshape(-1, HD)
            for part in range(3)
        ],
        axis=1,
    )
    total[...] += jnp.dot(scaled, block, preferred_element_type=F32)

    @pl.when(step == 7)
    def _():
        inverse = lax.rsqrt(squares[...] / (8 * width) + EPS)
        done = [
            (total[:, part * HD : (part + 1) * HD] * inverse).astype(BF16) for part in range(3)
        ]
        queries[...], keys[...], values[...] = done
        slots = 8
        slot_of = lax.broadcasted_iota(jnp.int32, (2 * slots, rows), 0)
        place = lax.broadcasted_iota(jnp.int32, (2 * slots, rows), 1)
        first = jnp.zeros((2 * slots, rows), jnp.int32)
        asked = jnp.zeros((2 * slots, HD), jnp.int32)
        for side, source in enumerate((mine, theirs)):
            facts = source[half:, :].astype(F32).astype(jnp.int32)
            start = jnp.full((1, HD), side * half, jnp.int32)
            for slot in range(slots):
                here = slot_of == side * slots + slot
                first = jnp.where(here, jnp.concatenate([start] * (rows // HD), axis=1), first)
                asked = jnp.where(
                    here[:, :HD], facts[slot : slot + 1, width // 2 : width // 2 + HD], asked
                )
                start = start + facts[slot : slot + 1, :HD]
        chosen = (first == place).astype(F32).astype(BF16)
        mark = (asked == place[:, :HD]).astype(F32).astype(BF16)
        key_rows = jnp.dot(chosen, done[1], preferred_element_type=F32).astype(BF16)
        value_rows = jnp.dot(chosen, done[2], preferred_element_type=F32).astype(BF16)
        for copy in range(sent.shape[0] // (2 * slots)):
            there = slice(copy * 2 * slots, (copy + 1) * 2 * slots)
            sent[there, :HD] = key_rows
            sent[there, HD : 2 * HD] = value_rows
            sent[there, 2 * HD :] = mark


def project(order, mine, theirs, pieces, gain, weights, copies):
    rows, width = pieces[0].shape
    along_z, along_x = weights.shape[:2]
    whole = lambda array: pl.BlockSpec(array.shape, lambda r, order: (0,) * array.ndim)
    out = lambda *shape: (
        jax.ShapeDtypeStruct(shape, BF16),
        pl.BlockSpec(shape, lambda r, order: (0, 0)),
    )
    outs = [out(rows, HD)] * 3
    outs.append(
        (
            jax.ShapeDtypeStruct((rows // 16, 8 * width), BF16),
            pl.BlockSpec((rows // 16, width), lambda r, order: (0, order[r])),
        )
    )
    outs.append(out(copies * 16, 3 * HD))
    return pl.pallas_call(
        project_kernel,
        out_shape=tuple(o[0] for o in outs),
        grid_spec=pltpu.PrefetchScalarGridSpec(
            num_scalar_prefetch=1,
            grid=(8,),
            in_specs=[whole(mine), whole(theirs)]
            + [whole(piece) for piece in pieces]
            + [
                pl.BlockSpec((1, 1, width), lambda r, order: (order[r], 0, 0)),
                pl.BlockSpec(
                    (along_z // 2, 1, 2, 192, HD),
                    lambda r, order: (lax.rem(order[r], 2), order[r] // 2, 0, 0, 0),
                ),
            ],
            out_specs=tuple(o[1] for o in outs),
            scratch_shapes=[
                pltpu.VMEM((rows, width), BF16),
                pltpu.VMEM((rows, 3 * HD), F32),
                pltpu.VMEM((rows, 1), F32),
            ],
        ),
        compiler_params=pltpu.CompilerParams(vmem_limit_bytes=VMEM_LIMIT),
    )(order, mine, theirs, *pieces, gain, weights)


def attend_kernel(queries, keys, values, others, mine, theirs, own_out, other_out):
    slots = 8
    rows = own_out.shape[0]
    half = mine.shape[1] // 2
    count = others.shape[0]
    here = lax.axis_index("cand") // 2 * (2 * slots)
    down = lax.broadcasted_iota(jnp.int32, (rows, rows), 0)
    across = lax.broadcasted_iota(jnp.int32, (rows, rows), 1)
    far_across = lax.broadcasted_iota(jnp.int32, (rows, count), 1)
    scale = 1.0 / math.sqrt(HD)
    for side, (source, out) in enumerate(((mine, own_out), (theirs, other_out))):
        facts = source[rows:, :].astype(F32).astype(jnp.int32)
        slot_down = jnp.zeros((rows, rows), jnp.int32)
        slot_across = jnp.zeros((rows, rows), jnp.int32)
        end = jnp.zeros((1, rows), jnp.int32)
        for slot in range(slots):
            end = end + facts[slot : slot + 1, :rows]
            if slot < slots - 1:
                slot_down = slot_down + (down >= end).astype(jnp.int32)
                slot_across = slot_across + (across >= end).astype(jnp.int32)
        asked = jnp.zeros((rows, HD), jnp.int32)
        for slot in range(slots):
            asked = jnp.where(
                slot_down[:, :HD] == slot, facts[slot : slot + 1, half : half + HD], asked
            )
        local = ((slot_down == slot_across) & (down < end) & (across < end)) | (down == across)
        mark = (asked == across[:, :HD]).astype(F32).astype(BF16)
        same = lax.dot_general(mark, others[:, 2 * HD :], NT, preferred_element_type=F32) > 0.5
        itself = here + side * slots + jnp.concatenate([slot_down] * (count // rows), axis=1)
        seen = same & (far_across != itself)
        there = slice(side * rows, (side + 1) * rows)
        query = queries[there, :]
        near_scores = jnp.where(
            local,
            lax.dot_general(query, keys[there, :], NT, preferred_element_type=F32) * scale,
            NEGATIVE,
        )
        far_scores = jnp.where(
            seen,
            lax.dot_general(query, others[:, :HD], NT, preferred_element_type=F32) * scale,
            NEGATIVE,
        )
        peak = jnp.maximum(
            jnp.max(near_scores, axis=1, keepdims=True), jnp.max(far_scores, axis=1, keepdims=True)
        )
        near_raised = jnp.exp(near_scores - peak)
        far_raised = jnp.exp(far_scores - peak)
        bottom = jnp.sum(near_raised, axis=1, keepdims=True) + jnp.sum(
            far_raised, axis=1, keepdims=True
        )
        top = jnp.dot(near_raised.astype(BF16), values[there, :], preferred_element_type=F32)
        top = top + jnp.dot(
            far_raised.astype(BF16), others[:, HD : 2 * HD], preferred_element_type=F32
        )
        out[...] = jnp.where(down[:, :HD] < end[:, :HD], top / bottom, 0.0).astype(BF16)


def attend(queries, keys, values, others, mine, theirs):
    vmem = pl.BlockSpec(memory_space=pltpu.VMEM)
    shape = jax.ShapeDtypeStruct((queries.shape[0] // 2, HD), BF16)
    return pl.pallas_call(
        attend_kernel,
        out_shape=(shape, shape),
        in_specs=[vmem] * 6,
        out_specs=(vmem, vmem),
        compiler_params=pltpu.CompilerParams(vmem_limit_bytes=VMEM_LIMIT),
    )(queries, keys, values, others, mine, theirs)


def mix_kernel(own, sibling, own_weights, sibling_weights, out):
    along_z, along_x, _, depth, _ = own_weights.shape
    attended = jnp.concatenate([own[...], sibling[...]], axis=1)
    width = 2 * depth
    for x in range(along_x):
        for z in range(along_z):
            block = jnp.concatenate(
                [
                    own_weights[z, x].reshape(width, HD),
                    sibling_weights[z, x].reshape(width, HD),
                ],
                axis=1,
            )
            at = (x * along_z + z) * width
            out[:, at : at + width] = lax.dot_general(
                attended, block, NT, preferred_element_type=F32
            ).astype(BF16)


def mix(own, sibling, own_weights, sibling_weights):
    along_z, along_x, cores, depth, _ = sibling_weights.shape
    rows, width = own.shape[0], along_z * along_x * cores * depth
    whole = lambda array: pl.BlockSpec(array.shape, lambda i: (0,) * array.ndim)
    return pl.pallas_call(
        mix_kernel,
        out_shape=jax.ShapeDtypeStruct((rows, width), BF16),
        grid=(1,),
        in_specs=[
            whole(own),
            whole(sibling),
            pl.BlockSpec(sibling_weights.shape, lambda i: (0, 0, 0, 3, 0)),
            whole(sibling_weights),
        ],
        out_specs=pl.BlockSpec((rows, width), lambda i: (0, 0)),
        compiler_params=pltpu.CompilerParams(vmem_limit_bytes=VMEM_LIMIT),
    )(own, sibling, own_weights, sibling_weights)


def shards(passages, norm_gain, w_qkv, w_out, counts, owners, query_of):
    devices = lax.axis_size("cand")
    parts = lax.axis_size("mp")
    me = lax.axis_index("mp")
    core = lax.rem(lax.axis_index("cand"), 2)
    columns = w_qkv.shape[2]
    along_x = devices // (2 * ALONG_Z)
    with jax.named_scope("weights_gathered"):
        own_weights = jnp.concatenate([w_qkv.reshape(-1, columns), w_out.T], axis=0)
        by_head = own_weights.reshape(-1, 2, HD).transpose(1, 0, 2)
        copies = jnp.broadcast_to(by_head[None], (along_x,) + by_head.shape)
        depth = by_head.shape[1]
        from_x = lax.all_to_all(
            copies.reshape(-1, HD), "cand", 0, 0, tiled=True, axis_index_groups=x_groups()
        )
        weights = lax.all_gather(from_x, "cand", axis=0, tiled=False, axis_index_groups=z_groups())
        weights = weights.reshape(ALONG_Z, along_x, 2, depth, HD)
    with jax.named_scope("passages_handed_over"):
        right, left, kept = pick(owners, counts, query_of, passages)
        from_left = along(right, "cand", 1)
        from_right = along(left, "cand", -1)
        mine = pack(from_left, kept, from_right)
    with jax.named_scope("features_gathered"):
        theirs = to_sibling(mine)
        half = mine.shape[0] - 16
        travelling = jnp.concatenate([mine[:half], theirs[:half]], axis=0)
        pieces = []
        for step in range(4):
            if step == 3:
                travelling = travelling[:half]
            travelling = one_way(travelling)
            pieces += [travelling, to_sibling(travelling)]
    way = 1 - 2 * core
    offsets = jnp.array([0, -1, 1, -2, 2, -3, 3, 4], jnp.int32)
    order = lax.rem(me + parts + way * offsets, parts)
    order = jnp.concatenate([order, me[None]]).astype(jnp.int32)
    gain = norm_gain.reshape(parts, 1, -1)
    queries, keys, values, residual, sent = project(
        order, mine, theirs, pieces, gain, weights, devices // 2
    )
    with jax.named_scope("interaction_gathered"):
        others = lax.all_to_all(
            sent, "cand", 0, 0, tiled=True, axis_index_groups=same_core_groups()
        )
    own, other = attend(queries, keys, values, others, mine, theirs)
    with jax.named_scope("heads_summed"):
        sibling_weights = to_sibling(weights[:, :, :, 192:])
        sibling = to_sibling(other)
        partial = mix(own, sibling, weights, sibling_weights)
        summed = lax.psum_scatter(partial, "mp", scatter_dimension=0, tiled=True)
    return (residual.astype(F32) + summed.astype(F32)).astype(BF16)


def solution(mesh):
    in_specs = (
        P("cand", None, "mp"),
        P(),
        P(None, "cand", "mp"),
        P("mp", "cand"),
        P("cand"),
        P("cand"),
        P("cand"),
    )
    out_specs = P(("cand", "mp"), None)
    return jax.shard_map(shards, mesh=mesh, in_specs=in_specs, out_specs=out_specs, check_vma=False)
```

```python
import math

import jax
import jax.numpy as jnp
from jax import lax
from jax.experimental import pallas as pl
from jax.experimental.pallas import tpu as pltpu
from jax.sharding import PartitionSpec as P

HD = 128
EPS = 1e-05
NEGATIVE = -1e30
VMEM_LIMIT = 48 * 1024 * 1024
F32 = jnp.float32
BF16 = jnp.bfloat16
NT = (((1,), (1,)), ((), ()))


def along(shard, axis, by):
    length = lax.axis_size(axis)
    return lax.ppermute(shard, axis, [(i, (i + by) % length) for i in range(length)])


def to_sibling(shard):
    length = lax.axis_size("cand")
    return lax.ppermute(shard, "cand", [(i, i ^ 1) for i in range(length)])


def same_core_groups():
    length = lax.axis_size("cand")
    return [list(range(core, length, 2)) for core in range(2)]


ALONG_Z = 8


def x_groups():
    length = lax.axis_size("cand")
    step = 2 * ALONG_Z
    return [
        [x + 2 * z + core for x in range(0, length, step) for core in range(2)]
        for z in range(ALONG_Z)
    ]


def z_groups():
    length = lax.axis_size("cand")
    step = 2 * ALONG_Z
    return [
        [x + 2 * z + core for z in range(ALONG_Z)]
        for x in range(0, length, step)
        for core in range(2)
    ]


def opposed(shard, by):
    chips, parts = lax.axis_size("cand"), lax.axis_size("mp")
    pairs = []
    for device in range(chips):
        signed = by if device % 2 == 0 else -by
        for part in range(parts):
            pairs.append((device * parts + part, device * parts + (part + signed) % parts))
    return lax.ppermute(shard, ("cand", "mp"), pairs)


def pick_kernel(owners, counts, query_of, passages, right, left, kept):
    me = lax.axis_index("cand")
    devices = lax.axis_size("cand")
    slots, length, width = passages.shape
    row = lax.broadcasted_iota(jnp.int32, (16, width), 0)
    lane = lax.broadcasted_iota(jnp.int32, (16, width), 1)
    number = [jnp.int32(0)] * 3
    targets = (right, left, kept)
    for slot in range(slots):
        ahead = lax.rem(owners[slot] - me + devices, devices)
        facts = jnp.where(lane < width // 2, counts[slot], query_of[slot]).astype(F32)
        tail = passages[slot, length - 16 :, :].astype(F32)
        tail = jnp.where(row == 15, facts, tail).astype(BF16)
        for which, wanted in enumerate((1, devices - 1, 0)):
            target = targets[which]
            hit = ahead == wanted
            place = jnp.minimum(number[which], target.shape[0] - 1)

            @pl.when(hit)
            def _():
                target[place, : length - 16, :] = passages[slot, : length - 16, :]
                target[place, length - 16 :, :] = tail

            number[which] = number[which] + hit.astype(jnp.int32)


def pick(owners, counts, query_of, passages):
    slots, length, width = passages.shape
    smem = pl.BlockSpec(memory_space=pltpu.SMEM)
    vmem = pl.BlockSpec(memory_space=pltpu.VMEM)
    shape = lambda n: jax.ShapeDtypeStruct((n, length, width), BF16)
    return pl.pallas_call(
        pick_kernel,
        out_shape=(shape(2), shape(2), shape(slots - 4)),
        in_specs=[smem, smem, smem, vmem],
        out_specs=(vmem, vmem, vmem),
        compiler_params=pltpu.CompilerParams(vmem_limit_bytes=VMEM_LIMIT),
    )(owners, counts, query_of, passages)


def pack_kernel(from_left, kept, from_right, packed, facts):
    rows = packed.shape[0]
    length = kept.shape[1]
    blocks = (
        [from_left[i] for i in range(from_left.shape[0])]
        + [kept[i] for i in range(kept.shape[0])]
        + [from_right[i] for i in range(from_right.shape[0])]
    )
    position = lax.broadcasted_iota(jnp.int32, (rows, length), 0)
    offset = lax.broadcasted_iota(jnp.int32, (rows, length), 1)
    start = jnp.zeros((1, length), jnp.int32)
    total = jnp.zeros(packed.shape, F32)
    for slot, block in enumerate(blocks):
        fact = block[length - 16 :, :].astype(F32)[15:16, :]
        facts[slot : slot + 1, :] = fact
        count = fact[:, :length].astype(jnp.int32)
        chosen = (position == start + offset) & (offset < count)
        total = total + jnp.dot(
            chosen.astype(F32).astype(BF16), block, preferred_element_type=F32
        )
        start = start + count
    packed[...] = total.astype(BF16)


def pack(from_left, kept, from_right):
    slots = from_left.shape[0] + kept.shape[0] + from_right.shape[0]
    length, width = kept.shape[1:]
    vmem = pl.BlockSpec(memory_space=pltpu.VMEM)
    return pl.pallas_call(
        pack_kernel,
        out_shape=(
            jax.ShapeDtypeStruct((slots * length // 2, width), BF16),
            jax.ShapeDtypeStruct((slots, width), F32),
        ),
        in_specs=[vmem] * 3,
        out_specs=(vmem, vmem),
        compiler_params=pltpu.CompilerParams(vmem_limit_bytes=VMEM_LIMIT),
    )(from_left, kept, from_right)


def project_kernel(place, *refs):
    pieces, gain, own_weights, sibling_weights, facts = refs[:9], *refs[9:13]
    queries, keys, values, residual, sent, rows_in, total, squares = refs[13:]
    step = pl.program_id(0)
    rows = rows_in.shape[0]
    width = rows_in.shape[1] // 2
    half = rows // 2
    for side in range(2):
        lanes = slice(side * width, (side + 1) * width)
        wanted = place[2 * step + side]
        for number in range(7):

            @pl.when(wanted == number)
            def _():
                rows_in[:, lanes] = pieces[number][...]

        @pl.when(wanted == 7)
        def _():
            rows_in[:half, lanes] = pieces[7][...]
            rows_in[half:, lanes] = pieces[8][...]

    share = residual.shape[0]
    residual[...] = rows_in[pl.ds(pl.multiple_of(place[8] * share, share), share), :]
    x = rows_in[...].astype(F32)
    square = jnp.sum(x * x, axis=1, keepdims=True)
    scaled = (x * gain[0]).astype(BF16)
    depth = own_weights.shape[3] // 3
    block = jnp.concatenate(
        [
            source[:, 0, :, part * depth : (part + 1) * depth, :].reshape(-1, HD)
            for part in range(3)
            for source in (own_weights, sibling_weights)
        ],
        axis=1,
    )
    product = jnp.dot(scaled, block, preferred_element_type=F32)

    @pl.when(step == 0)
    def _():
        total[...] = product
        squares[...] = square

    @pl.when(step > 0)
    def _():
        total[...] += product
        squares[...] += square

    @pl.when(step == 3)
    def _():
        inverse = lax.rsqrt(squares[...] / (8 * width) + EPS)
        columns = 2 * HD
        done = [
            (total[:, part * columns : (part + 1) * columns] * inverse).astype(BF16)
            for part in range(3)
        ]
        queries[...], keys[...], values[...] = done
        slots = facts.shape[0]
        slot_of = lax.broadcasted_iota(jnp.int32, (2 * slots, rows), 0) % slots
        position = lax.broadcasted_iota(jnp.int32, (2 * slots, rows), 1)
        start = jnp.zeros((1, rows), jnp.int32)
        first = jnp.zeros((2 * slots, rows), jnp.int32)
        asked = jnp.zeros((2 * slots, HD), jnp.int32)
        for slot in range(slots):
            here = slot_of == slot
            first = jnp.where(here, start, first)
            asked = jnp.where(
                here[:, :HD],
                facts[slot : slot + 1, width // 2 : width // 2 + HD].astype(jnp.int32),
                asked,
            )
            start = start + facts[slot : slot + 1, :rows].astype(jnp.int32)
        chosen = (first == position).astype(F32).astype(BF16)
        mark = (asked == position[:, :HD]).astype(F32).astype(BF16)
        key_rows = jnp.dot(chosen, done[1], preferred_element_type=F32).astype(BF16)
        value_rows = jnp.dot(chosen, done[2], preferred_element_type=F32).astype(BF16)
        for copy in range(sent.shape[0] // (2 * slots)):
            there = slice(copy * 2 * slots, (copy + 1) * 2 * slots)
            sent[there, :columns] = key_rows
            sent[there, columns : 2 * columns] = value_rows
            sent[there, 2 * columns :] = mark


def project(place, pieces, gain, own_weights, sibling_weights, facts, copies):
    rows, width = pieces[0].shape
    along_z, along_x, cores, depth, _ = own_weights.shape
    columns = 2 * HD
    whole = lambda array: pl.BlockSpec(array.shape, lambda r, place: (0,) * array.ndim)
    out = lambda *shape: (
        jax.ShapeDtypeStruct(shape, BF16),
        pl.BlockSpec(shape, lambda r, place: (0, 0)),
    )
    outs = [out(rows, columns)] * 3
    outs.append(
        (
            jax.ShapeDtypeStruct((rows // 8, 8 * width), BF16),
            pl.BlockSpec((rows // 8, 2 * width), lambda r, place: (0, r)),
        )
    )
    outs.append(out(copies * facts.shape[0], 2 * columns + HD))
    weight = pl.BlockSpec((along_z, 1, cores, depth, HD), lambda r, place: (0, r, 0, 0, 0))
    return pl.pallas_call(
        project_kernel,
        out_shape=tuple(o[0] for o in outs),
        grid_spec=pltpu.PrefetchScalarGridSpec(
            num_scalar_prefetch=1,
            grid=(along_x,),
            in_specs=[whole(piece) for piece in pieces]
            + [
                pl.BlockSpec((1, 1, 2 * width), lambda r, place: (r, 0, 0)),
                weight,
                weight,
                whole(facts),
            ],
            out_specs=tuple(o[1] for o in outs),
            scratch_shapes=[
                pltpu.VMEM((rows, 2 * width), BF16),
                pltpu.VMEM((rows, 3 * columns), F32),
                pltpu.VMEM((rows, 1), F32),
            ],
        ),
        compiler_params=pltpu.CompilerParams(vmem_limit_bytes=VMEM_LIMIT),
    )(place, *pieces, gain, own_weights, sibling_weights, facts)


def attend_kernel(queries, keys, values, near, far, facts, own_weights, sibling_weights, out):
    rows, columns = queries.shape
    slots = facts.shape[0]
    half = facts.shape[1] // 2
    here = lax.axis_index("cand") // 2 * slots
    down = lax.broadcasted_iota(jnp.int32, (rows, rows), 0)
    across = lax.broadcasted_iota(jnp.int32, (rows, rows), 1)
    slot_down = jnp.zeros((rows, rows), jnp.int32)
    slot_across = jnp.zeros((rows, rows), jnp.int32)
    end = jnp.zeros((1, rows), jnp.int32)
    for slot in range(slots):
        end = end + facts[slot : slot + 1, :rows].astype(jnp.int32)
        if slot < slots - 1:
            slot_down = slot_down + (down >= end).astype(jnp.int32)
            slot_across = slot_across + (across >= end).astype(jnp.int32)
    asked = jnp.zeros((rows, HD), jnp.int32)
    for slot in range(slots):
        asked = jnp.where(
            slot_down[:, :HD] == slot,
            facts[slot : slot + 1, half : half + HD].astype(jnp.int32),
            asked,
        )
    local = ((slot_down == slot_across) & (down < end) & (across < end)) | (down == across)
    mark = (asked == across[:, :HD]).astype(F32).astype(BF16)
    same = lambda other: lax.dot_general(
        mark, other[:, 2 * columns :], NT, preferred_element_type=F32
    ) > 0.5
    masks = [local, same(near) & (across != here + slot_down), same(far)]
    scale = 1.0 / math.sqrt(HD)
    heads = []
    for head in range(columns // HD):
        lanes = slice(head * HD, (head + 1) * HD)
        value_lanes = slice(columns + head * HD, columns + (head + 1) * HD)
        swapped = columns - HD * (1 + head)
        far_lanes = slice(swapped, swapped + HD)
        far_value_lanes = slice(columns + swapped, columns + swapped + HD)
        query = queries[:, lanes]
        scores = [
            jnp.where(
                mask,
                lax.dot_general(query, key, NT, preferred_element_type=F32) * scale,
                NEGATIVE,
            )
            for mask, key in zip(masks, (keys[:, lanes], near[:, lanes], far[:, far_lanes]))
        ]
        peak = jnp.maximum(jnp.maximum(scores[0], scores[1]), scores[2])
        peak = jnp.max(peak, axis=1, keepdims=True)
        raised = [jnp.exp(score - peak) for score in scores]
        bottom = jnp.sum(raised[0] + raised[1] + raised[2], axis=1, keepdims=True)
        top = jnp.zeros((rows, HD), F32)
        for part, value in zip(
            raised, (values[:, lanes], near[:, value_lanes], far[:, far_value_lanes])
        ):
            top = top + jnp.dot(part.astype(BF16), value, preferred_element_type=F32)
        heads.append(jnp.where(down[:, :HD] < end[:, :HD], top / bottom, 0.0).astype(BF16))
    attended = jnp.concatenate(heads, axis=1)
    along_z, along_x, cores, depth, _ = own_weights.shape
    width = cores * depth
    for x in range(along_x):
        for z in range(0, along_z, 2):
            block = jnp.concatenate(
                [
                    source[z : z + 2, x].reshape(2 * width, HD)
                    for source in (own_weights, sibling_weights)
                ],
                axis=1,
            )
            at = (x * along_z + z) * width
            out[:, at : at + 2 * width] = lax.dot_general(
                attended, block, NT, preferred_element_type=F32
            ).astype(BF16)


def attend(queries, keys, values, near, far, facts, own_weights, sibling_weights):
    rows = queries.shape[0]
    along_z, along_x, cores, depth, _ = own_weights.shape
    vmem = pl.BlockSpec(memory_space=pltpu.VMEM)
    return pl.pallas_call(
        attend_kernel,
        out_shape=jax.ShapeDtypeStruct((rows, along_z * along_x * cores * depth), BF16),
        in_specs=[vmem] * 8,
        out_specs=vmem,
        compiler_params=pltpu.CompilerParams(vmem_limit_bytes=VMEM_LIMIT),
    )(queries, keys, values, near, far, facts, own_weights, sibling_weights)


def shards(passages, norm_gain, w_qkv, w_out, counts, owners, query_of):
    devices = lax.axis_size("cand")
    parts = lax.axis_size("mp")
    me = lax.axis_index("mp")
    core = lax.rem(lax.axis_index("cand"), 2)
    columns = w_qkv.shape[2]
    along_x = devices // (2 * ALONG_Z)
    with jax.named_scope("weights_gathered"):
        own_weights = jnp.concatenate([w_qkv.reshape(-1, columns), w_out.T], axis=0)
        by_head = own_weights.reshape(-1, 2, HD).transpose(1, 0, 2)
        copies = jnp.broadcast_to(by_head[None], (along_x,) + by_head.shape)
        from_x = lax.all_to_all(
            copies.reshape(-1, HD), "cand", 0, 0, tiled=True, axis_index_groups=x_groups()
        ).reshape(along_x, 2, -1, HD)
        split = w_qkv.shape[0] * w_qkv.shape[1]
        along_z = lambda shard: lax.all_gather(shard, "cand", axis_index_groups=z_groups())
        project_weights = along_z(from_x[:, :, :split])
        mix_weights = along_z(from_x[:, :, split:])
        sibling_project = to_sibling(project_weights)
        sibling_mix = to_sibling(mix_weights)
    with jax.named_scope("passages_handed_over"):
        right, left, kept = pick(owners, counts, query_of, passages)
        from_left = along(right, "cand", 1)
        from_right = along(left, "cand", -1)
        packed, facts = pack(from_left, kept, from_right)
    with jax.named_scope("features_gathered"):
        half = packed.shape[0] // 2
        first, second = opposed(packed, 1), opposed(packed, -1)
        third, fourth = opposed(packed, 2), opposed(packed, -2)
        fifth, sixth = opposed(third, 1), opposed(fourth, -1)
        last = [opposed(third[:half], 2), opposed(fourth[half:], -2)]
        pieces = [packed, first, second, third, fourth, fifth, sixth] + last
    away = (jnp.arange(parts, dtype=jnp.int32) - me) * (1 - 2 * core)
    away = lax.rem(away + parts, parts)
    place = jnp.where(away < parts // 2, 2 * away, 2 * parts - 1 - 2 * away)
    place = jnp.concatenate([place, me[None]]).astype(jnp.int32)
    gain = norm_gain.reshape(along_x, 1, -1)
    queries, keys, values, residual, sent = project(
        place, pieces, gain, project_weights, sibling_project, facts, devices // 2
    )
    with jax.named_scope("interaction_gathered"):
        near = lax.all_to_all(
            sent, "cand", 0, 0, tiled=True, axis_index_groups=same_core_groups()
        )
        far = to_sibling(near)
    partial = attend(queries, keys, values, near, far, facts, mix_weights, sibling_mix)
    with jax.named_scope("heads_summed"):
        summed = lax.psum_scatter(partial, "mp", scatter_dimension=0, tiled=True)
    return (residual.astype(F32) + summed.astype(F32)).astype(BF16)


def solution(mesh):
    in_specs = (
        P("cand", None, "mp"),
        P(),
        P(None, "cand", "mp"),
        P("mp", "cand"),
        P("cand"),
        P("cand"),
        P("cand"),
    )
    out_specs = P(("cand", "mp"), None)
    return jax.shard_map(shards, mesh=mesh, in_specs=in_specs, out_specs=out_specs, check_vma=False)
```

```python
import math

import jax
import jax.numpy as jnp
from jax import lax
from jax.experimental import pallas as pl
from jax.experimental.pallas import tpu as pltpu
from jax.sharding import PartitionSpec as P

HD = 128
EPS = 1e-05
NEGATIVE = -1e30
VMEM_LIMIT = 48 * 1024 * 1024
F32 = jnp.float32
BF16 = jnp.bfloat16
NT = (((1,), (1,)), ((), ()))


def along(shard, axis, by):
    length = lax.axis_size(axis)
    return lax.ppermute(shard, axis, [(i, (i + by) % length) for i in range(length)])


def to_sibling(shard):
    length = lax.axis_size("cand")
    return lax.ppermute(shard, "cand", [(i, i ^ 1) for i in range(length)])


def same_core_groups():
    length = lax.axis_size("cand")
    return [list(range(core, length, 2)) for core in range(2)]


ALONG_Z = 8


def x_groups():
    length = lax.axis_size("cand")
    step = 2 * ALONG_Z
    return [
        [x + 2 * z + core for x in range(0, length, step) for core in range(2)]
        for z in range(ALONG_Z)
    ]


def z_groups():
    length = lax.axis_size("cand")
    step = 2 * ALONG_Z
    return [
        [x + 2 * z + core for z in range(ALONG_Z)]
        for x in range(0, length, step)
        for core in range(2)
    ]


def opposed(shard, by):
    chips, parts = lax.axis_size("cand"), lax.axis_size("mp")
    pairs = []
    for device in range(chips):
        signed = by if device % 2 == 0 else -by
        for part in range(parts):
            pairs.append((device * parts + part, device * parts + (part + signed) % parts))
    return lax.ppermute(shard, ("cand", "mp"), pairs)


def pick_kernel(owners, counts, query_of, passages, right, left, kept):
    me = lax.axis_index("cand")
    devices = lax.axis_size("cand")
    slots, length, width = passages.shape
    row = lax.broadcasted_iota(jnp.int32, (16, width), 0)
    lane = lax.broadcasted_iota(jnp.int32, (16, width), 1)
    number = [jnp.int32(0)] * 3
    targets = (right, left, kept)
    for slot in range(slots):
        ahead = lax.rem(owners[slot] - me + devices, devices)
        facts = jnp.where(lane < width // 2, counts[slot], query_of[slot]).astype(F32)
        tail = passages[slot, length - 16 :, :].astype(F32)
        tail = jnp.where(row == 15, facts, tail).astype(BF16)
        for which, wanted in enumerate((1, devices - 1, 0)):
            target = targets[which]
            hit = ahead == wanted
            place = jnp.minimum(number[which], target.shape[0] - 1)

            @pl.when(hit)
            def _():
                target[place, : length - 16, :] = passages[slot, : length - 16, :]
                target[place, length - 16 :, :] = tail

            number[which] = number[which] + hit.astype(jnp.int32)


def pick(owners, counts, query_of, passages):
    slots, length, width = passages.shape
    smem = pl.BlockSpec(memory_space=pltpu.SMEM)
    vmem = pl.BlockSpec(memory_space=pltpu.VMEM)
    shape = lambda n: jax.ShapeDtypeStruct((n, length, width), BF16)
    return pl.pallas_call(
        pick_kernel,
        out_shape=(shape(2), shape(2), shape(slots - 4)),
        in_specs=[smem, smem, smem, vmem],
        out_specs=(vmem, vmem, vmem),
        compiler_params=pltpu.CompilerParams(vmem_limit_bytes=VMEM_LIMIT),
    )(owners, counts, query_of, passages)


def pack_kernel(from_left, kept, from_right, packed, facts):
    rows = packed.shape[0]
    length = kept.shape[1]
    blocks = (
        [from_left[i] for i in range(from_left.shape[0])]
        + [kept[i] for i in range(kept.shape[0])]
        + [from_right[i] for i in range(from_right.shape[0])]
    )
    position = lax.broadcasted_iota(jnp.int32, (rows, length), 0)
    offset = lax.broadcasted_iota(jnp.int32, (rows, length), 1)
    start = jnp.zeros((1, length), jnp.int32)
    total = jnp.zeros(packed.shape, F32)
    for slot, block in enumerate(blocks):
        fact = block[length - 16 :, :].astype(F32)[15:16, :]
        facts[slot : slot + 1, :] = fact
        count = fact[:, :length].astype(jnp.int32)
        chosen = (position == start + offset) & (offset < count)
        total = total + jnp.dot(
            chosen.astype(F32).astype(BF16), block, preferred_element_type=F32
        )
        start = start + count
    packed[...] = total.astype(BF16)


def pack(from_left, kept, from_right):
    slots = from_left.shape[0] + kept.shape[0] + from_right.shape[0]
    length, width = kept.shape[1:]
    vmem = pl.BlockSpec(memory_space=pltpu.VMEM)
    return pl.pallas_call(
        pack_kernel,
        out_shape=(
            jax.ShapeDtypeStruct((slots * length // 2, width), BF16),
            jax.ShapeDtypeStruct((slots, width), F32),
        ),
        in_specs=[vmem] * 3,
        out_specs=(vmem, vmem),
        compiler_params=pltpu.CompilerParams(vmem_limit_bytes=VMEM_LIMIT),
    )(from_left, kept, from_right)


def project_kernel(place, *refs):
    pieces, gain, own_weights, sibling_weights, facts = refs[:9], *refs[9:13]
    queries, keys, values, residual, sent, rows_in, total, squares = refs[13:]
    step = pl.program_id(0)
    rows = rows_in.shape[0]
    width = rows_in.shape[1] // 2
    half = rows // 2
    for side in range(2):
        lanes = slice(side * width, (side + 1) * width)
        wanted = place[2 * step + side]
        for number in range(7):

            @pl.when(wanted == number)
            def _():
                rows_in[:, lanes] = pieces[number][...]

        @pl.when(wanted == 7)
        def _():
            rows_in[:half, lanes] = pieces[7][...]
            rows_in[half:, lanes] = pieces[8][...]

    share = residual.shape[0]
    residual[...] = rows_in[pl.ds(pl.multiple_of(place[8] * share, share), share), :]
    x = rows_in[...].astype(F32)
    square = jnp.sum(x * x, axis=1, keepdims=True)
    scaled = (x * gain[0]).astype(BF16)
    depth = own_weights.shape[3] // 3
    block = jnp.concatenate(
        [
            source[:, 0, :, part * depth : (part + 1) * depth, :].reshape(-1, HD)
            for part in range(3)
            for source in (own_weights, sibling_weights)
        ],
        axis=1,
    )
    product = jnp.dot(scaled, block, preferred_element_type=F32)

    @pl.when(step == 0)
    def _():
        total[...] = product
        squares[...] = square

    @pl.when(step > 0)
    def _():
        total[...] += product
        squares[...] += square

    @pl.when(step == 3)
    def _():
        inverse = lax.rsqrt(squares[...] / (8 * width) + EPS)
        columns = 2 * HD
        done = [
            (total[:, part * columns : (part + 1) * columns] * inverse).astype(BF16)
            for part in range(3)
        ]
        queries[...], keys[...], values[...] = done
        slots = facts.shape[0]
        slot_of = lax.broadcasted_iota(jnp.int32, (2 * slots, rows), 0) % slots
        position = lax.broadcasted_iota(jnp.int32, (2 * slots, rows), 1)
        start = jnp.zeros((1, rows), jnp.int32)
        first = jnp.zeros((2 * slots, rows), jnp.int32)
        asked = jnp.zeros((2 * slots, HD), jnp.int32)
        for slot in range(slots):
            here = slot_of == slot
            first = jnp.where(here, start, first)
            asked = jnp.where(
                here[:, :HD],
                facts[slot : slot + 1, width // 2 : width // 2 + HD].astype(jnp.int32),
                asked,
            )
            start = start + facts[slot : slot + 1, :rows].astype(jnp.int32)
        chosen = (first == position).astype(F32).astype(BF16)
        mark = (asked == position[:, :HD]).astype(F32).astype(BF16)
        key_rows = jnp.dot(chosen, done[1], preferred_element_type=F32).astype(BF16)
        value_rows = jnp.dot(chosen, done[2], preferred_element_type=F32).astype(BF16)
        for copy in range(sent.shape[0] // (2 * slots)):
            there = slice(copy * 2 * slots, (copy + 1) * 2 * slots)
            sent[there, :columns] = key_rows
            sent[there, columns : 2 * columns] = value_rows
            sent[there, 2 * columns :] = mark


def project(place, pieces, gain, own_weights, sibling_weights, facts, copies):
    rows, width = pieces[0].shape
    along_z, along_x, cores, depth, _ = own_weights.shape
    columns = 2 * HD
    whole = lambda array: pl.BlockSpec(array.shape, lambda r, place: (0,) * array.ndim)
    out = lambda *shape: (
        jax.ShapeDtypeStruct(shape, BF16),
        pl.BlockSpec(shape, lambda r, place: (0, 0)),
    )
    outs = [out(rows, columns)] * 3
    outs.append(
        (
            jax.ShapeDtypeStruct((rows // 8, 8 * width), BF16),
            pl.BlockSpec((rows // 8, 2 * width), lambda r, place: (0, r)),
        )
    )
    outs.append(out(copies * facts.shape[0], 2 * columns + HD))
    weight = pl.BlockSpec((along_z, 1, cores, depth, HD), lambda r, place: (0, r, 0, 0, 0))
    return pl.pallas_call(
        project_kernel,
        out_shape=tuple(o[0] for o in outs),
        grid_spec=pltpu.PrefetchScalarGridSpec(
            num_scalar_prefetch=1,
            grid=(along_x,),
            in_specs=[whole(piece) for piece in pieces]
            + [
                pl.BlockSpec((1, 1, 2 * width), lambda r, place: (r, 0, 0)),
                weight,
                weight,
                whole(facts),
            ],
            out_specs=tuple(o[1] for o in outs),
            scratch_shapes=[
                pltpu.VMEM((rows, 2 * width), BF16),
                pltpu.VMEM((rows, 3 * columns), F32),
                pltpu.VMEM((rows, 1), F32),
            ],
        ),
        compiler_params=pltpu.CompilerParams(vmem_limit_bytes=VMEM_LIMIT),
    )(place, *pieces, gain, own_weights, sibling_weights, facts)


def attend_kernel(queries, keys, values, near, far, facts, own_weights, sibling_weights, out):
    rows, columns = queries.shape
    slots = facts.shape[0]
    half = facts.shape[1] // 2
    here = lax.axis_index("cand") // 2 * slots
    down = lax.broadcasted_iota(jnp.int32, (rows, rows), 0)
    across = lax.broadcasted_iota(jnp.int32, (rows, rows), 1)
    slot_down = jnp.zeros((rows, rows), jnp.int32)
    slot_across = jnp.zeros((rows, rows), jnp.int32)
    end = jnp.zeros((1, rows), jnp.int32)
    for slot in range(slots):
        end = end + facts[slot : slot + 1, :rows].astype(jnp.int32)
        if slot < slots - 1:
            slot_down = slot_down + (down >= end).astype(jnp.int32)
            slot_across = slot_across + (across >= end).astype(jnp.int32)
    asked = jnp.zeros((rows, HD), jnp.int32)
    for slot in range(slots):
        asked = jnp.where(
            slot_down[:, :HD] == slot,
            facts[slot : slot + 1, half : half + HD].astype(jnp.int32),
            asked,
        )
    local = ((slot_down == slot_across) & (down < end) & (across < end)) | (down == across)
    mark = (asked == across[:, :HD]).astype(F32).astype(BF16)
    same = lambda other: lax.dot_general(
        mark, other[:, 2 * columns :], NT, preferred_element_type=F32
    ) > 0.5
    masks = [local, same(near) & (across != here + slot_down), same(far)]
    scale = 1.0 / math.sqrt(HD)
    heads = []
    for head in range(columns // HD):
        lanes = slice(head * HD, (head + 1) * HD)
        value_lanes = slice(columns + head * HD, columns + (head + 1) * HD)
        swapped = columns - HD * (1 + head)
        far_lanes = slice(swapped, swapped + HD)
        far_value_lanes = slice(columns + swapped, columns + swapped + HD)
        query = queries[:, lanes]
        scores = [
            jnp.where(
                mask,
                lax.dot_general(query, key, NT, preferred_element_type=F32) * scale,
                NEGATIVE,
            )
            for mask, key in zip(masks, (keys[:, lanes], near[:, lanes], far[:, far_lanes]))
        ]
        peak = jnp.maximum(jnp.maximum(scores[0], scores[1]), scores[2])
        peak = jnp.max(peak, axis=1, keepdims=True)
        raised = [jnp.exp(score - peak) for score in scores]
        bottom = jnp.sum(raised[0] + raised[1] + raised[2], axis=1, keepdims=True)
        top = jnp.zeros((rows, HD), F32)
        for part, value in zip(
            raised, (values[:, lanes], near[:, value_lanes], far[:, far_value_lanes])
        ):
            top = top + jnp.dot(part.astype(BF16), value, preferred_element_type=F32)
        heads.append(jnp.where(down[:, :HD] < end[:, :HD], top / bottom, 0.0).astype(BF16))
    attended = jnp.concatenate(heads, axis=1)
    along_z, along_x, cores, depth, _ = own_weights.shape
    width = cores * depth
    for x in range(along_x):
        for z in range(0, along_z, 2):
            block = jnp.concatenate(
                [
                    source[z : z + 2, x].reshape(2 * width, HD)
                    for source in (own_weights, sibling_weights)
                ],
                axis=1,
            )
            at = (x * along_z + z) * width
            out[:, at : at + 2 * width] = lax.dot_general(
                attended, block, NT, preferred_element_type=F32
            ).astype(BF16)


def attend(queries, keys, values, near, far, facts, own_weights, sibling_weights):
    rows = queries.shape[0]
    along_z, along_x, cores, depth, _ = own_weights.shape
    vmem = pl.BlockSpec(memory_space=pltpu.VMEM)
    return pl.pallas_call(
        attend_kernel,
        out_shape=jax.ShapeDtypeStruct((rows, along_z * along_x * cores * depth), BF16),
        in_specs=[vmem] * 8,
        out_specs=vmem,
        compiler_params=pltpu.CompilerParams(vmem_limit_bytes=VMEM_LIMIT),
    )(queries, keys, values, near, far, facts, own_weights, sibling_weights)


def shards(passages, norm_gain, w_qkv, w_out, counts, owners, query_of):
    devices = lax.axis_size("cand")
    parts = lax.axis_size("mp")
    me = lax.axis_index("mp")
    core = lax.rem(lax.axis_index("cand"), 2)
    columns = w_qkv.shape[2]
    along_x = devices // (2 * ALONG_Z)
    with jax.named_scope("weights_gathered"):
        own_weights = jnp.concatenate([w_qkv.reshape(-1, columns), w_out.T], axis=0)
        by_head = own_weights.reshape(-1, 2, HD).transpose(1, 0, 2)
        copies = jnp.broadcast_to(by_head[None], (along_x,) + by_head.shape)
        from_x = lax.all_to_all(
            copies.reshape(-1, HD), "cand", 0, 0, tiled=True, axis_index_groups=x_groups()
        ).reshape(along_x, 2, -1, HD)
        split = w_qkv.shape[0] * w_qkv.shape[1]
        along_z = lambda shard: lax.all_gather(shard, "cand", axis_index_groups=z_groups())
        project_weights = along_z(from_x[:, :, :split])
        mix_weights = along_z(from_x[:, :, split:])
    with jax.named_scope("passages_handed_over"):
        right, left, kept = pick(owners, counts, query_of, passages)
        from_left = along(right, "cand", 1)
        from_right = along(left, "cand", -1)
        packed, facts = pack(from_left, kept, from_right)
    with jax.named_scope("features_gathered"):
        half = packed.shape[0] // 2
        third, fourth = opposed(packed, 2), opposed(packed, -2)
        first, second = opposed(packed, 1), opposed(packed, -1)
        first, second, third, fourth = lax.optimization_barrier((first, second, third, fourth))
        sixth = opposed(fourth, -1)
        last = (opposed(third[:half], 2), opposed(fourth[half:], -2))
        project_weights, third, sixth, last = lax.optimization_barrier(
            (project_weights, third, sixth, last)
        )
        fifth = opposed(third, 1)
        pieces = [packed, first, second, third, fourth, fifth, sixth, *last]
    with jax.named_scope("weights_swapped"):
        sibling_project = to_sibling(project_weights)
    away = (jnp.arange(parts, dtype=jnp.int32) - me) * (1 - 2 * core)
    away = lax.rem(away + parts, parts)
    place = jnp.where(away < parts // 2, 2 * away, 2 * parts - 1 - 2 * away)
    place = jnp.concatenate([place, me[None]]).astype(jnp.int32)
    gain = norm_gain.reshape(along_x, 1, -1)
    queries, keys, values, residual, sent = project(
        place, pieces, gain, project_weights, sibling_project, facts, devices // 2
    )
    with jax.named_scope("interaction_gathered"):
        near = lax.all_to_all(
            sent, "cand", 0, 0, tiled=True, axis_index_groups=same_core_groups()
        )
        far = to_sibling(near)
    with jax.named_scope("weights_swapped"):
        mix_weights, _ = lax.optimization_barrier((mix_weights, near))
        sibling_mix = to_sibling(mix_weights)
    partial = attend(queries, keys, values, near, far, facts, mix_weights, sibling_mix)
    with jax.named_scope("heads_summed"):
        summed = lax.psum_scatter(partial, "mp", scatter_dimension=0, tiled=True)
    return (residual.astype(F32) + summed.astype(F32)).astype(BF16)


def solution(mesh):
    in_specs = (
        P("cand", None, "mp"),
        P(),
        P(None, "cand", "mp"),
        P("mp", "cand"),
        P("cand"),
        P("cand"),
        P("cand"),
    )
    out_specs = P(("cand", "mp"), None)
    return jax.shard_map(shards, mesh=mesh, in_specs=in_specs, out_specs=out_specs, check_vma=False)
```

```python
import math

import jax
import jax.numpy as jnp
from jax import lax
from jax.experimental import pallas as pl
from jax.experimental.pallas import tpu as pltpu
from jax.sharding import PartitionSpec as P

HD = 128
EPS = 1e-05
NEGATIVE = -1e30
VMEM_LIMIT = 48 * 1024 * 1024
F32 = jnp.float32
BF16 = jnp.bfloat16
NT = (((1,), (1,)), ((), ()))


def along(shard, axis, by):
    length = lax.axis_size(axis)
    return lax.ppermute(shard, axis, [(i, (i + by) % length) for i in range(length)])


def to_sibling(shard):
    length = lax.axis_size("cand")
    return lax.ppermute(shard, "cand", [(i, i ^ 1) for i in range(length)])


def same_core_groups():
    length = lax.axis_size("cand")
    return [list(range(core, length, 2)) for core in range(2)]


ALONG_Z = 8


def x_groups():
    length = lax.axis_size("cand")
    step = 2 * ALONG_Z
    return [
        [x + 2 * z + core for x in range(0, length, step) for core in range(2)]
        for z in range(ALONG_Z)
    ]


def z_groups():
    length = lax.axis_size("cand")
    step = 2 * ALONG_Z
    return [
        [x + 2 * z + core for z in range(ALONG_Z)]
        for x in range(0, length, step)
        for core in range(2)
    ]


def opposed(shard, by):
    chips, parts = lax.axis_size("cand"), lax.axis_size("mp")
    pairs = []
    for device in range(chips):
        signed = by if device % 2 == 0 else -by
        for part in range(parts):
            pairs.append((device * parts + part, device * parts + (part + signed) % parts))
    return lax.ppermute(shard, ("cand", "mp"), pairs)


def pick_kernel(table, passages, right, left, kept):
    me = lax.axis_index("cand")
    devices = lax.axis_size("cand")
    slots, length, width = passages.shape
    row = lax.broadcasted_iota(jnp.int32, (16, width), 0)
    lane = lax.broadcasted_iota(jnp.int32, (16, width), 1)
    number = [jnp.int32(0)] * 3
    targets = (right, left, kept)
    for slot in range(slots):
        ahead = lax.rem(table[0, slot] - me + devices, devices)
        facts = jnp.where(lane < width // 2, table[1, slot], table[2, slot]).astype(F32)
        tail = passages[slot, length - 16 :, :].astype(F32)
        tail = jnp.where(row == 15, facts, tail).astype(BF16)
        for which, wanted in enumerate((1, devices - 1, 0)):
            target = targets[which]
            hit = ahead == wanted
            place = jnp.minimum(number[which], target.shape[0] - 1)

            @pl.when(hit)
            def _():
                target[place, : length - 16, :] = passages[slot, : length - 16, :]
                target[place, length - 16 :, :] = tail

            number[which] = number[which] + hit.astype(jnp.int32)


def pick(facts, passages):
    slots, length, width = passages.shape
    smem = pl.BlockSpec(memory_space=pltpu.SMEM)
    vmem = pl.BlockSpec(memory_space=pltpu.VMEM)
    shape = lambda n: jax.ShapeDtypeStruct((n, length, width), BF16)
    return pl.pallas_call(
        pick_kernel,
        out_shape=(shape(2), shape(2), shape(slots - 4)),
        in_specs=[smem, vmem],
        out_specs=(vmem, vmem, vmem),
        compiler_params=pltpu.CompilerParams(vmem_limit_bytes=VMEM_LIMIT),
    )(facts, passages)


def pack_kernel(from_left, kept, from_right, packed, facts):
    rows = packed.shape[0]
    length = kept.shape[1]
    blocks = (
        [from_left[i] for i in range(from_left.shape[0])]
        + [kept[i] for i in range(kept.shape[0])]
        + [from_right[i] for i in range(from_right.shape[0])]
    )
    position = lax.broadcasted_iota(jnp.int32, (rows, length), 0)
    offset = lax.broadcasted_iota(jnp.int32, (rows, length), 1)
    start = jnp.zeros((1, length), jnp.int32)
    total = jnp.zeros(packed.shape, F32)
    for slot, block in enumerate(blocks):
        fact = block[length - 16 :, :].astype(F32)[15:16, :]
        facts[slot : slot + 1, :] = fact
        count = fact[:, :length].astype(jnp.int32)
        chosen = (position == start + offset) & (offset < count)
        total = total + jnp.dot(
            chosen.astype(F32).astype(BF16), block, preferred_element_type=F32
        )
        start = start + count
    packed[...] = total.astype(BF16)


def pack(from_left, kept, from_right):
    slots = from_left.shape[0] + kept.shape[0] + from_right.shape[0]
    length, width = kept.shape[1:]
    vmem = pl.BlockSpec(memory_space=pltpu.VMEM)
    return pl.pallas_call(
        pack_kernel,
        out_shape=(
            jax.ShapeDtypeStruct((slots * length // 2, width), BF16),
            jax.ShapeDtypeStruct((slots, width), F32),
        ),
        in_specs=[vmem] * 3,
        out_specs=(vmem, vmem),
        compiler_params=pltpu.CompilerParams(vmem_limit_bytes=VMEM_LIMIT),
    )(from_left, kept, from_right)


def norm_kernel(place, *refs):
    pieces, (gain, facts, normed, residual, rows_in, squares) = refs[:9], refs[9:]
    stage, step = pl.program_id(0), pl.program_id(1)
    rows = rows_in.shape[1]
    width = gain.shape[2]
    half = rows // 2
    share = residual.shape[0]

    @pl.when(stage == 0)
    def _():
        wanted = place[step]
        for number in range(7):

            @pl.when(wanted == number)
            def _():
                rows_in[step] = pieces[number][...]

        @pl.when(wanted == 7)
        def _():
            rows_in[step, :half, :] = pieces[7][...]
            rows_in[step, half:, :] = pieces[8][...]

        x = rows_in[step].astype(F32)
        square = jnp.sum(x * x, axis=1, keepdims=True)

        @pl.when(step == 0)
        def _():
            squares[...] = square

        @pl.when(step > 0)
        def _():
            squares[...] += square

    @pl.when(stage == 1)
    def _():
        x = rows_in[step].astype(F32)
        inverse = lax.rsqrt(squares[...] / (8 * width) + EPS)
        normed[:rows, :] = (x * inverse * gain[0]).astype(BF16)
        told = jnp.concatenate([facts[...], jnp.zeros_like(facts)], axis=0)
        normed[rows:, :] = told.astype(BF16)
        residual[...] = rows_in[step, pl.ds(pl.multiple_of(place[8] * share, share), share), :]


def norm(place, pieces, gain, facts):
    rows, width = pieces[0].shape
    whole = lambda array: pl.BlockSpec(array.shape, lambda s, r, place: (0,) * array.ndim)
    return pl.pallas_call(
        norm_kernel,
        out_shape=(
            jax.ShapeDtypeStruct((rows + 16, 8 * width), BF16),
            jax.ShapeDtypeStruct((rows // 8, 8 * width), BF16),
        ),
        grid_spec=pltpu.PrefetchScalarGridSpec(
            num_scalar_prefetch=1,
            grid=(2, 8),
            in_specs=[whole(piece) for piece in pieces]
            + [pl.BlockSpec((1, 1, width), lambda s, r, place: (s * r, 0, 0)), whole(facts)],
            out_specs=(
                pl.BlockSpec((rows + 16, width), lambda s, r, place: (0, s * r)),
                pl.BlockSpec((rows // 8, width), lambda s, r, place: (0, s * r)),
            ),
            scratch_shapes=[pltpu.VMEM((8, rows, width), BF16), pltpu.VMEM((rows, 1), F32)],
        ),
        compiler_params=pltpu.CompilerParams(vmem_limit_bytes=VMEM_LIMIT),
    )(place, *pieces, gain, facts)


def project_kernel(mine, theirs, weights, facts, other_facts, queries, keys, values, sent, total):
    step = pl.program_id(0)
    rows = mine.shape[0] - 16
    depth = weights.shape[3] // 3
    block = jnp.concatenate(
        [
            weights[:, 0, :, part * depth : (part + 1) * depth, :].reshape(-1, HD)
            for part in range(3)
        ],
        axis=1,
    )
    for side, source in enumerate((mine, theirs)):
        there = slice(side * rows, (side + 1) * rows)
        product = jnp.dot(source[:rows, :], block, preferred_element_type=F32)

        @pl.when(step == 0)
        def _():
            total[there, :] = product

        @pl.when(step > 0)
        def _():
            total[there, :] += product

    @pl.when(step == pl.num_programs(0) - 1)
    def _():
        done = [total[:, part * HD : (part + 1) * HD].astype(BF16) for part in range(3)]
        queries[...], keys[...], values[...] = done
        slots = 8
        slot_of = lax.broadcasted_iota(jnp.int32, (2 * slots, 2 * rows), 0)
        position = lax.broadcasted_iota(jnp.int32, (2 * slots, 2 * rows), 1)
        first = jnp.zeros((2 * slots, 2 * rows), jnp.int32)
        asked = jnp.zeros((2 * slots, HD), jnp.int32)
        half = facts.shape[1] // 2
        for side, source in enumerate((facts, other_facts)):
            told = source[...].astype(F32).astype(jnp.int32)
            start = jnp.full((1, HD), side * rows, jnp.int32)
            for slot in range(slots):
                here = slot_of == side * slots + slot
                first = jnp.where(here, jnp.concatenate([start] * (2 * rows // HD), axis=1), first)
                asked = jnp.where(here[:, :HD], told[slot : slot + 1, half : half + HD], asked)
                start = start + told[slot : slot + 1, :HD]
        chosen = (first == position).astype(F32).astype(BF16)
        mark = (asked == position[:, :HD]).astype(F32).astype(BF16)
        key_rows = jnp.dot(chosen, done[1], preferred_element_type=F32).astype(BF16)
        value_rows = jnp.dot(chosen, done[2], preferred_element_type=F32).astype(BF16)
        for copy in range(sent.shape[0] // (2 * slots)):
            there = slice(copy * 2 * slots, (copy + 1) * 2 * slots)
            sent[there, :HD] = key_rows
            sent[there, HD : 2 * HD] = value_rows
            sent[there, 2 * HD :] = mark


def facts_spec(array, width):
    last = array.shape[0] // 16 - 1
    return pl.BlockSpec((16, width), lambda i: (last, 0))


def project(mine, theirs, weights, copies, width):
    rows = mine.shape[0] - 16
    along_z, along_x, cores = weights.shape[:3]
    out = lambda *shape: (
        jax.ShapeDtypeStruct(shape, BF16),
        pl.BlockSpec(shape, lambda i: (0, 0)),
    )
    outs = [out(2 * rows, HD)] * 3 + [out(copies * 16, 3 * HD)]
    x = pl.BlockSpec((mine.shape[0], mine.shape[1] // along_x), lambda i: (0, i))
    return pl.pallas_call(
        project_kernel,
        out_shape=tuple(o[0] for o in outs),
        grid=(along_x,),
        in_specs=[
            x,
            x,
            pl.BlockSpec((along_z, 1, cores, 192, HD), lambda i: (0, i, 0, 0, 0)),
            facts_spec(mine, width),
            facts_spec(theirs, width),
        ],
        out_specs=tuple(o[1] for o in outs),
        scratch_shapes=[pltpu.VMEM((2 * rows, 3 * HD), F32)],
        compiler_params=pltpu.CompilerParams(vmem_limit_bytes=VMEM_LIMIT),
    )(mine, theirs, weights, mine, theirs)


def attend_kernel(queries, keys, values, others, mine, theirs, own_out, other_out):
    slots = 8
    rows = own_out.shape[0]
    half = mine.shape[1] // 2
    count = others.shape[0]
    here = lax.axis_index("cand") // 2 * (2 * slots)
    down = lax.broadcasted_iota(jnp.int32, (rows, rows), 0)
    across = lax.broadcasted_iota(jnp.int32, (rows, rows), 1)
    far_across = lax.broadcasted_iota(jnp.int32, (rows, count), 1)
    scale = 1.0 / math.sqrt(HD)
    for side, (source, out) in enumerate(((mine, own_out), (theirs, other_out))):
        facts = source[...].astype(F32).astype(jnp.int32)
        slot_down = jnp.zeros((rows, rows), jnp.int32)
        slot_across = jnp.zeros((rows, rows), jnp.int32)
        end = jnp.zeros((1, rows), jnp.int32)
        for slot in range(slots):
            end = end + facts[slot : slot + 1, :rows]
            if slot < slots - 1:
                slot_down = slot_down + (down >= end).astype(jnp.int32)
                slot_across = slot_across + (across >= end).astype(jnp.int32)
        asked = jnp.zeros((rows, HD), jnp.int32)
        for slot in range(slots):
            asked = jnp.where(
                slot_down[:, :HD] == slot, facts[slot : slot + 1, half : half + HD], asked
            )
        local = ((slot_down == slot_across) & (down < end) & (across < end)) | (down == across)
        mark = (asked == across[:, :HD]).astype(F32).astype(BF16)
        same = lax.dot_general(mark, others[:, 2 * HD :], NT, preferred_element_type=F32) > 0.5
        itself = here + side * slots + jnp.concatenate([slot_down] * (count // rows), axis=1)
        seen = same & (far_across != itself)
        there = slice(side * rows, (side + 1) * rows)
        query = queries[there, :]
        near_scores = jnp.where(
            local,
            lax.dot_general(query, keys[there, :], NT, preferred_element_type=F32) * scale,
            NEGATIVE,
        )
        far_scores = jnp.where(
            seen,
            lax.dot_general(query, others[:, :HD], NT, preferred_element_type=F32) * scale,
            NEGATIVE,
        )
        peak = jnp.maximum(
            jnp.max(near_scores, axis=1, keepdims=True), jnp.max(far_scores, axis=1, keepdims=True)
        )
        near_raised = jnp.exp(near_scores - peak)
        far_raised = jnp.exp(far_scores - peak)
        bottom = jnp.sum(near_raised, axis=1, keepdims=True) + jnp.sum(
            far_raised, axis=1, keepdims=True
        )
        top = jnp.dot(near_raised.astype(BF16), values[there, :], preferred_element_type=F32)
        top = top + jnp.dot(
            far_raised.astype(BF16), others[:, HD : 2 * HD], preferred_element_type=F32
        )
        out[...] = jnp.where(down[:, :HD] < end[:, :HD], top / bottom, 0.0).astype(BF16)


def attend(queries, keys, values, others, mine, theirs, width):
    whole = lambda array: pl.BlockSpec(array.shape, lambda i: (0, 0))
    rows = queries.shape[0] // 2
    shape = jax.ShapeDtypeStruct((rows, HD), BF16)
    spec = pl.BlockSpec((rows, HD), lambda i: (0, 0))
    return pl.pallas_call(
        attend_kernel,
        out_shape=(shape, shape),
        grid=(1,),
        in_specs=[whole(array) for array in (queries, keys, values, others)]
        + [facts_spec(mine, width), facts_spec(theirs, width)],
        out_specs=(spec, spec),
        compiler_params=pltpu.CompilerParams(vmem_limit_bytes=VMEM_LIMIT),
    )(queries, keys, values, others, mine, theirs)


def mix_kernel(own, sibling, own_weights, sibling_weights, out):
    along_z, along_x, _, depth, _ = own_weights.shape
    attended = jnp.concatenate([own[...], sibling[...]], axis=1)
    width = 2 * depth
    for x in range(along_x):
        for z in range(0, along_z, 2):
            block = jnp.concatenate(
                [
                    own_weights[z : z + 2, x].reshape(2 * width, HD),
                    sibling_weights[z : z + 2, x].reshape(2 * width, HD),
                ],
                axis=1,
            )
            at = (x * along_z + z) * width
            out[:, at : at + 2 * width] = lax.dot_general(
                attended, block, NT, preferred_element_type=F32
            ).astype(BF16)


def mix(own, sibling, own_weights, sibling_weights):
    along_z, along_x, cores, depth, _ = sibling_weights.shape
    rows, width = own.shape[0], along_z * along_x * cores * depth
    whole = lambda array: pl.BlockSpec(array.shape, lambda i: (0,) * array.ndim)
    return pl.pallas_call(
        mix_kernel,
        out_shape=jax.ShapeDtypeStruct((rows, width), BF16),
        grid=(1,),
        in_specs=[
            whole(own),
            whole(sibling),
            pl.BlockSpec(sibling_weights.shape, lambda i: (0, 0, 0, 3, 0)),
            whole(sibling_weights),
        ],
        out_specs=pl.BlockSpec((rows, width), lambda i: (0, 0)),
        compiler_params=pltpu.CompilerParams(vmem_limit_bytes=VMEM_LIMIT),
    )(own, sibling, own_weights, sibling_weights)


def shards(passages, norm_gain, w_qkv, w_out, counts, owners, query_of):
    devices = lax.axis_size("cand")
    parts = lax.axis_size("mp")
    me = lax.axis_index("mp")
    core = lax.rem(lax.axis_index("cand"), 2)
    columns = w_qkv.shape[2]
    along_x = devices // (2 * ALONG_Z)
    with jax.named_scope("weights_gathered"):
        own_weights = jnp.concatenate([w_qkv.reshape(-1, columns), w_out.T], axis=0)
        by_head = own_weights.reshape(-1, 2, HD).transpose(1, 0, 2)
        copies = jnp.broadcast_to(by_head[None], (along_x,) + by_head.shape)
        from_x = lax.all_to_all(
            copies.reshape(-1, HD), "cand", 0, 0, tiled=True, axis_index_groups=x_groups()
        ).reshape(along_x, 2, -1, HD)
    with jax.named_scope("passages_handed_over"):
        right, left, kept = pick(jnp.stack([owners, counts, query_of]), passages)
        from_left = along(right, "cand", 1)
        from_right = along(left, "cand", -1)
        from_x, from_left, from_right = lax.optimization_barrier((from_x, from_left, from_right))
        packed, facts = pack(from_left, kept, from_right)
    with jax.named_scope("weights_gathered"):
        weights = lax.all_gather(from_x, "cand", axis_index_groups=z_groups())
    with jax.named_scope("features_gathered"):
        half = packed.shape[0] // 2
        third, fourth = opposed(packed, 2), opposed(packed, -2)
        first, second = opposed(packed, 1), opposed(packed, -1)
        first, second, third, fourth = lax.optimization_barrier((first, second, third, fourth))
        fifth, sixth = opposed(third, 1), opposed(fourth, -1)
        last = (opposed(third[:half], 2), opposed(fourth[half:], -2))
        pieces = [packed, first, second, third, fourth, fifth, sixth, *last]
    away = (jnp.arange(parts, dtype=jnp.int32) - me) * (1 - 2 * core)
    away = lax.rem(away + parts, parts)
    place = jnp.where(away < parts // 2, 2 * away, 2 * parts - 1 - 2 * away)
    place = jnp.concatenate([place, me[None]]).astype(jnp.int32)
    normed, residual = norm(place, pieces, norm_gain.reshape(parts, 1, -1), facts)
    with jax.named_scope("normed_swapped"):
        sibling_normed = to_sibling(normed)
        weights, sibling_normed = lax.optimization_barrier((weights, sibling_normed))
    width = packed.shape[1]
    queries, keys, values, sent = project(normed, sibling_normed, weights, devices // 2, width)
    with jax.named_scope("interaction_gathered"):
        sibling_weights = to_sibling(weights[:, :, :, 192:])
        others = lax.all_to_all(
            sent, "cand", 0, 0, tiled=True, axis_index_groups=same_core_groups()
        )
    own, other = attend(queries, keys, values, others, normed, sibling_normed, width)
    with jax.named_scope("heads_summed"):
        sibling = to_sibling(other)
        partial = mix(own, sibling, weights, sibling_weights)
        summed = lax.psum_scatter(partial, "mp", scatter_dimension=0, tiled=True)
    return (residual.astype(F32) + summed.astype(F32)).astype(BF16)


def solution(mesh):
    in_specs = (
        P("cand", None, "mp"),
        P(),
        P(None, "cand", "mp"),
        P("mp", "cand"),
        P("cand"),
        P("cand"),
        P("cand"),
    )
    out_specs = P(("cand", "mp"), None)
    return jax.shard_map(shards, mesh=mesh, in_specs=in_specs, out_specs=out_specs, check_vma=False)
```

```python
import math

import jax
import jax.numpy as jnp
from jax import lax
from jax.experimental import pallas as pl
from jax.experimental.pallas import tpu as pltpu
from jax.sharding import PartitionSpec as P

HD = 128
EPS = 1e-05
NEGATIVE = -1e30
VMEM_LIMIT = 20 * 1024 * 1024
F32 = jnp.float32
BF16 = jnp.bfloat16
NT = (((1,), (1,)), ((), ()))


def along(shard, axis, by):
    length = lax.axis_size(axis)
    return lax.ppermute(shard, axis, [(i, (i + by) % length) for i in range(length)])


def to_sibling(shard):
    length = lax.axis_size("cand")
    return lax.ppermute(shard, "cand", [(i, i ^ 1) for i in range(length)])


def same_core_groups():
    length = lax.axis_size("cand")
    return [list(range(core, length, 2)) for core in range(2)]


ALONG_Z = 8


def x_groups():
    length = lax.axis_size("cand")
    step = 2 * ALONG_Z
    return [
        [x + 2 * z + core for x in range(0, length, step) for core in range(2)]
        for z in range(ALONG_Z)
    ]


def z_groups():
    length = lax.axis_size("cand")
    step = 2 * ALONG_Z
    return [
        [x + 2 * z + core for z in range(ALONG_Z)]
        for x in range(0, length, step)
        for core in range(2)
    ]


def to_outer(shard):
    length = lax.axis_size("cand")
    pairs = [(i, (i + (1 if i % 2 else length - 1)) % length) for i in range(length)]
    return lax.ppermute(shard, "cand", pairs)


def paired(shard, turn):
    length = lax.axis_size("mp")
    pairs = []
    for part in range(length):
        by = 1 if (part + turn) % 2 == 0 else length - 1
        pairs.append((part, (part + by) % length))
    return lax.ppermute(shard, "mp", pairs)


def opposed(shard, by):
    chips, parts = lax.axis_size("cand"), lax.axis_size("mp")
    pairs = []
    for device in range(chips):
        signed = by if device % 2 == 0 else -by
        for part in range(parts):
            pairs.append((device * parts + part, device * parts + (part + signed) % parts))
    return lax.ppermute(shard, ("cand", "mp"), pairs)


def prepare_kernel(table, passages, w_qkv, w_out, inner, outer, kept, copies):
    me = lax.axis_index("cand")
    devices = lax.axis_size("cand")
    slots, length, width = passages.shape
    turned = w_out[...].astype(F32).T.astype(BF16)
    depth = w_qkv.shape[1]
    for head in range(2):
        lanes = slice(head * HD, (head + 1) * HD)
        for copy in range(head, copies.shape[0], 2):
            for part in range(3):
                copies[copy, part * depth : (part + 1) * depth, :] = w_qkv[part, :, lanes]
            copies[copy, 3 * depth :, :] = turned[:, lanes]
    row = lax.broadcasted_iota(jnp.int32, (16, width), 0)
    lane = lax.broadcasted_iota(jnp.int32, (16, width), 1)
    number = [jnp.int32(0)] * 3
    core = lax.rem(me, 2)
    inward = jnp.where(core == 0, 1, devices - 1)
    outward = jnp.where(core == 0, devices - 1, 1)
    for slot in range(slots):
        ahead = lax.rem(table[0, slot] - me + devices, devices)
        facts = jnp.where(lane < width // 2, table[1, slot], table[2, slot]).astype(F32)
        tail = passages[slot, length - 16 :, :].astype(F32)
        tail = jnp.where(row == 15, facts, tail).astype(BF16)
        for which, (wanted, target) in enumerate(((inward, inner), (outward, outer), (0, kept))):
            hit = ahead == wanted
            place = jnp.minimum(number[which], target.shape[0] - 1)

            @pl.when(hit)
            def _():
                target[place, : length - 16, :] = passages[slot, : length - 16, :]
                target[place, length - 16 :, :] = tail

            number[which] = number[which] + hit.astype(jnp.int32)


def prepare(table, passages, w_qkv, w_out):
    slots, length, width = passages.shape
    smem = pl.BlockSpec(memory_space=pltpu.SMEM)
    vmem = pl.BlockSpec(memory_space=pltpu.VMEM)
    shape = lambda n: jax.ShapeDtypeStruct((n, length, width), BF16)
    depth = 3 * w_qkv.shape[1] + w_out.shape[1]
    return pl.pallas_call(
        prepare_kernel,
        out_shape=(shape(2), shape(2), shape(slots - 4), jax.ShapeDtypeStruct((8, depth, HD), BF16)),
        in_specs=[smem, vmem, vmem, vmem],
        out_specs=(vmem, vmem, vmem, vmem),
        compiler_params=pltpu.CompilerParams(vmem_limit_bytes=VMEM_LIMIT),
    )(table, passages, w_qkv, w_out)


def pack_kernel(inner, kept, outer, packed, facts):
    rows = packed.shape[0]
    length = kept.shape[1]
    first = lax.rem(lax.axis_index("cand"), 2) == 0
    blocks = (
        [jnp.where(first, outer[i], inner[i]) for i in range(outer.shape[0])]
        + [kept[i] for i in range(kept.shape[0])]
        + [jnp.where(first, inner[i], outer[i]) for i in range(inner.shape[0])]
    )
    position = lax.broadcasted_iota(jnp.int32, (rows, length), 0)
    offset = lax.broadcasted_iota(jnp.int32, (rows, length), 1)
    start = jnp.zeros((1, length), jnp.int32)
    total = jnp.zeros(packed.shape, F32)
    for slot, block in enumerate(blocks):
        fact = block[length - 16 :, :].astype(F32)[15:16, :]
        facts[slot : slot + 1, :] = fact
        count = fact[:, :length].astype(jnp.int32)
        chosen = (position == start + offset) & (offset < count)
        total = total + jnp.dot(
            chosen.astype(F32).astype(BF16), block, preferred_element_type=F32
        )
        start = start + count
    packed[...] = total.astype(BF16)


def pack(inner, kept, outer):
    slots = inner.shape[0] + kept.shape[0] + outer.shape[0]
    length, width = kept.shape[1:]
    vmem = pl.BlockSpec(memory_space=pltpu.VMEM)
    return pl.pallas_call(
        pack_kernel,
        out_shape=(
            jax.ShapeDtypeStruct((slots * length // 2, width), BF16),
            jax.ShapeDtypeStruct((slots, width), F32),
        ),
        in_specs=[vmem] * 3,
        out_specs=(vmem, vmem),
        compiler_params=pltpu.CompilerParams(vmem_limit_bytes=VMEM_LIMIT),
    )(inner, kept, outer)


def norm_kernel(place, *refs):
    pieces, (gain, facts, normed, residual, rows_in, squares) = refs[:9], refs[9:]
    stage, step = pl.program_id(0), pl.program_id(1)
    rows = rows_in.shape[1]
    width = gain.shape[2]
    half = rows // 2
    share = residual.shape[0]

    @pl.when(stage == 0)
    def _():
        wanted = place[step]
        for number in range(7):

            @pl.when(wanted == number)
            def _():
                rows_in[step] = pieces[number][...]

        @pl.when(wanted == 7)
        def _():
            rows_in[step, :half, :] = pieces[7][...]
            rows_in[step, half:, :] = pieces[8][...]

        x = rows_in[step].astype(F32)
        square = jnp.sum(x * x, axis=1, keepdims=True)

        @pl.when(step == 0)
        def _():
            squares[...] = square

        @pl.when(step > 0)
        def _():
            squares[...] += square

    @pl.when(stage == 1)
    def _():
        x = rows_in[step].astype(F32)
        inverse = lax.rsqrt(squares[...] / (8 * width) + EPS)
        normed[:rows, :] = (x * inverse * gain[0]).astype(BF16)
        told = jnp.concatenate([facts[...], jnp.zeros_like(facts)], axis=0)
        normed[rows:, :] = told.astype(BF16)
        residual[...] = rows_in[step, pl.ds(pl.multiple_of(place[8] * share, share), share), :]


def norm(place, pieces, gain, facts):
    rows, width = pieces[0].shape
    whole = lambda array: pl.BlockSpec(array.shape, lambda s, r, place: (0,) * array.ndim)
    return pl.pallas_call(
        norm_kernel,
        out_shape=(
            jax.ShapeDtypeStruct((rows + 16, 8 * width), BF16),
            jax.ShapeDtypeStruct((rows // 8, 8 * width), BF16),
        ),
        grid_spec=pltpu.PrefetchScalarGridSpec(
            num_scalar_prefetch=1,
            grid=(2, 8),
            in_specs=[whole(piece) for piece in pieces]
            + [pl.BlockSpec((1, 1, width), lambda s, r, place: (s * r, 0, 0)), whole(facts)],
            out_specs=(
                pl.BlockSpec((rows + 16, width), lambda s, r, place: (0, s * r)),
                pl.BlockSpec((rows // 8, width), lambda s, r, place: (0, s * r)),
            ),
            scratch_shapes=[pltpu.VMEM((8, rows, width), BF16), pltpu.VMEM((rows, 1), F32)],
        ),
        compiler_params=pltpu.CompilerParams(vmem_limit_bytes=VMEM_LIMIT),
    )(place, *pieces, gain, facts)


def project_kernel(mine, theirs, weights, facts, other_facts, queries, keys, values, sent, total):
    step = pl.program_id(0)
    rows = mine.shape[0] - 16
    depth = weights.shape[3] // 3
    block = jnp.concatenate(
        [
            weights[:, 0, :, part * depth : (part + 1) * depth, :].reshape(-1, HD)
            for part in range(3)
        ],
        axis=1,
    )
    for side, source in enumerate((mine, theirs)):
        there = slice(side * rows, (side + 1) * rows)
        product = jnp.dot(source[:rows, :], block, preferred_element_type=F32)

        @pl.when(step == 0)
        def _():
            total[there, :] = product

        @pl.when(step > 0)
        def _():
            total[there, :] += product

    @pl.when(step == pl.num_programs(0) - 1)
    def _():
        done = [total[:, part * HD : (part + 1) * HD].astype(BF16) for part in range(3)]
        queries[...], keys[...], values[...] = done
        slots = 8
        slot_of = lax.broadcasted_iota(jnp.int32, (2 * slots, 2 * rows), 0)
        position = lax.broadcasted_iota(jnp.int32, (2 * slots, 2 * rows), 1)
        first = jnp.zeros((2 * slots, 2 * rows), jnp.int32)
        asked = jnp.zeros((2 * slots, HD), jnp.int32)
        half = facts.shape[1] // 2
        for side, source in enumerate((facts, other_facts)):
            told = source[...].astype(F32).astype(jnp.int32)
            start = jnp.full((1, HD), side * rows, jnp.int32)
            for slot in range(slots):
                here = slot_of == side * slots + slot
                first = jnp.where(here, jnp.concatenate([start] * (2 * rows // HD), axis=1), first)
                asked = jnp.where(here[:, :HD], told[slot : slot + 1, half : half + HD], asked)
                start = start + told[slot : slot + 1, :HD]
        chosen = (first == position).astype(F32).astype(BF16)
        mark = (asked == position[:, :HD]).astype(F32).astype(BF16)
        key_rows = jnp.dot(chosen, done[1], preferred_element_type=F32).astype(BF16)
        value_rows = jnp.dot(chosen, done[2], preferred_element_type=F32).astype(BF16)
        for copy in range(sent.shape[0] // (2 * slots)):
            there = slice(copy * 2 * slots, (copy + 1) * 2 * slots)
            sent[there, :HD] = key_rows
            sent[there, HD : 2 * HD] = value_rows
            sent[there, 2 * HD :] = mark


def facts_spec(array, width):
    last = array.shape[0] // 16 - 1
    return pl.BlockSpec((16, width), lambda i: (last, 0))


def project(mine, theirs, weights, copies, width):
    rows = mine.shape[0] - 16
    along_z, along_x, cores = weights.shape[:3]
    out = lambda *shape: (
        jax.ShapeDtypeStruct(shape, BF16),
        pl.BlockSpec(shape, lambda i: (0, 0)),
    )
    outs = [out(2 * rows, HD)] * 3 + [out(copies * 16, 3 * HD)]
    x = pl.BlockSpec((mine.shape[0], mine.shape[1] // along_x), lambda i: (0, i))
    return pl.pallas_call(
        project_kernel,
        out_shape=tuple(o[0] for o in outs),
        grid=(along_x,),
        in_specs=[
            x,
            x,
            pl.BlockSpec((along_z, 1, cores, 192, HD), lambda i: (0, i, 0, 0, 0)),
            facts_spec(mine, width),
            facts_spec(theirs, width),
        ],
        out_specs=tuple(o[1] for o in outs),
        scratch_shapes=[pltpu.VMEM((2 * rows, 3 * HD), F32)],
        compiler_params=pltpu.CompilerParams(vmem_limit_bytes=VMEM_LIMIT),
    )(mine, theirs, weights, mine, theirs)


def attend_kernel(queries, keys, values, others, mine, theirs, own_out, other_out):
    slots = 8
    rows = own_out.shape[0]
    half = mine.shape[1] // 2
    count = others.shape[0]
    here = lax.axis_index("cand") // 2 * (2 * slots)
    down = lax.broadcasted_iota(jnp.int32, (rows, rows), 0)
    across = lax.broadcasted_iota(jnp.int32, (rows, rows), 1)
    far_across = lax.broadcasted_iota(jnp.int32, (rows, count), 1)
    scale = 1.0 / math.sqrt(HD)
    for side, (source, out) in enumerate(((mine, own_out), (theirs, other_out))):
        facts = source[...].astype(F32).astype(jnp.int32)
        slot_down = jnp.zeros((rows, rows), jnp.int32)
        slot_across = jnp.zeros((rows, rows), jnp.int32)
        end = jnp.zeros((1, rows), jnp.int32)
        for slot in range(slots):
            end = end + facts[slot : slot + 1, :rows]
            if slot < slots - 1:
                slot_down = slot_down + (down >= end).astype(jnp.int32)
                slot_across = slot_across + (across >= end).astype(jnp.int32)
        asked = jnp.zeros((rows, HD), jnp.int32)
        for slot in range(slots):
            asked = jnp.where(
                slot_down[:, :HD] == slot, facts[slot : slot + 1, half : half + HD], asked
            )
        local = ((slot_down == slot_across) & (down < end) & (across < end)) | (down == across)
        mark = (asked == across[:, :HD]).astype(F32).astype(BF16)
        same = lax.dot_general(mark, others[:, 2 * HD :], NT, preferred_element_type=F32) > 0.5
        itself = here + side * slots + jnp.concatenate([slot_down] * (count // rows), axis=1)
        seen = same & (far_across != itself)
        there = slice(side * rows, (side + 1) * rows)
        query = queries[there, :]
        near_scores = jnp.where(
            local,
            lax.dot_general(query, keys[there, :], NT, preferred_element_type=F32) * scale,
            NEGATIVE,
        )
        far_scores = jnp.where(
            seen,
            lax.dot_general(query, others[:, :HD], NT, preferred_element_type=F32) * scale,
            NEGATIVE,
        )
        peak = jnp.maximum(
            jnp.max(near_scores, axis=1, keepdims=True), jnp.max(far_scores, axis=1, keepdims=True)
        )
        near_raised = jnp.exp(near_scores - peak)
        far_raised = jnp.exp(far_scores - peak)
        bottom = jnp.sum(near_raised, axis=1, keepdims=True) + jnp.sum(
            far_raised, axis=1, keepdims=True
        )
        top = jnp.dot(near_raised.astype(BF16), values[there, :], preferred_element_type=F32)
        top = top + jnp.dot(
            far_raised.astype(BF16), others[:, HD : 2 * HD], preferred_element_type=F32
        )
        out[...] = jnp.where(down[:, :HD] < end[:, :HD], top / bottom, 0.0).astype(BF16)


def attend(queries, keys, values, others, mine, theirs, width):
    whole = lambda array: pl.BlockSpec(array.shape, lambda i: (0, 0))
    rows = queries.shape[0] // 2
    shape = jax.ShapeDtypeStruct((rows, HD), BF16)
    spec = pl.BlockSpec((rows, HD), lambda i: (0, 0))
    return pl.pallas_call(
        attend_kernel,
        out_shape=(shape, shape),
        grid=(1,),
        in_specs=[whole(array) for array in (queries, keys, values, others)]
        + [facts_spec(mine, width), facts_spec(theirs, width)],
        out_specs=(spec, spec),
        compiler_params=pltpu.CompilerParams(vmem_limit_bytes=VMEM_LIMIT),
    )(queries, keys, values, others, mine, theirs)


def mix_kernel(turn, pairs, own, sibling, own_weights, sibling_weights, *refs):
    outs, attended = refs[:4], refs[4]
    along_z, along_x, _, depth, _ = own_weights.shape
    share = outs[0].shape[0]
    both = jnp.concatenate([own[...], sibling[...]], axis=1)
    if turn:
        both = jnp.concatenate([both[share // 2 :], both[: share // 2]], axis=0)
    attended[...] = both
    rows = jnp.concatenate(
        [attended[pl.ds(pl.multiple_of(pairs[i] * share, share), share), :] for i in range(4)],
        axis=0,
    )
    width = 2 * depth
    for x in range(along_x):
        for z in range(0, along_z, 2):
            block = jnp.concatenate(
                [
                    source[z : z + 2, x].reshape(2 * width, HD)
                    for source in (own_weights, sibling_weights)
                ],
                axis=1,
            )
            at = (x * along_z + z) * width
            done = lax.dot_general(rows, block, NT, preferred_element_type=F32).astype(BF16)
            for i in range(4):
                outs[i][:, at : at + 2 * width] = done[i * share : (i + 1) * share]


def mix(turn, pairs, own, sibling, own_weights, sibling_weights):
    along_z, along_x, cores, depth, _ = sibling_weights.shape
    rows, width = own.shape[0], along_z * along_x * cores * depth // 2
    whole = lambda array: pl.BlockSpec(array.shape, lambda i, pairs: (0,) * array.ndim)
    columns = (along_z, along_x // 2, cores, depth, HD)
    return pl.pallas_call(
        lambda *refs: mix_kernel(turn, *refs),
        out_shape=(jax.ShapeDtypeStruct((rows // 4, width), BF16),) * 4,
        grid_spec=pltpu.PrefetchScalarGridSpec(
            num_scalar_prefetch=1,
            grid=(1,),
            in_specs=[
                whole(own),
                whole(sibling),
                pl.BlockSpec(columns, lambda i, pairs: (0, turn, 0, 3, 0)),
                pl.BlockSpec(columns, lambda i, pairs: (0, turn, 0, 0, 0)),
            ],
            out_specs=(pl.BlockSpec((rows // 4, width), lambda i, pairs: (0, 0)),) * 4,
            scratch_shapes=[pltpu.VMEM((rows, 2 * HD), BF16)],
        ),
        compiler_params=pltpu.CompilerParams(vmem_limit_bytes=VMEM_LIMIT),
    )(pairs, own, sibling, own_weights, sibling_weights)


def plus(first, second):
    return (first.astype(F32) + second.astype(F32)).astype(BF16)


def heads_summed(turn, blocks, odd):
    farthest, far, near, mine = blocks
    far = plus(far, paired(farthest, 1 - turn))
    near = plus(near, paired(far, turn))
    mine = plus(mine, paired(near, 1 - turn))
    half = mine.shape[0] // 2
    kept = jnp.where(odd, mine[half:], mine[:half])
    sent = jnp.where(odd, mine[:half], mine[half:])
    return kept.astype(F32) + paired(sent, turn).astype(F32)


def shards(passages, norm_gain, w_qkv, w_out, counts, owners, query_of):
    devices = lax.axis_size("cand")
    parts = lax.axis_size("mp")
    me = lax.axis_index("mp")
    core = lax.rem(lax.axis_index("cand"), 2)
    along_x = devices // (2 * ALONG_Z)
    with jax.named_scope("prepared"):
        table = jnp.stack([owners, counts, query_of])
        inner, outer, kept, copies = prepare(table, passages, w_qkv, w_out)
    with jax.named_scope("passages_handed_over"):
        inner, outer = to_sibling(inner), to_outer(outer)
    with jax.named_scope("weights_gathered"):
        from_x = lax.all_to_all(
            copies.reshape(-1, HD), "cand", 0, 0, tiled=True, axis_index_groups=x_groups()
        ).reshape(along_x, 2, -1, HD)
        from_x, inner, outer = lax.optimization_barrier((from_x, inner, outer))
        weights = lax.all_gather(from_x, "cand", axis_index_groups=z_groups())
    with jax.named_scope("passages_packed"):
        packed, facts = pack(inner, kept, outer)
    with jax.named_scope("features_gathered"):
        half = packed.shape[0] // 2
        third, fourth = opposed(packed, 2), opposed(packed, -2)
        first, second = opposed(packed, 1), opposed(packed, -1)
        first, second, third, fourth = lax.optimization_barrier((first, second, third, fourth))
        fifth, sixth = opposed(third, 1), opposed(fourth, -1)
        last = (opposed(third[:half], 2), opposed(fourth[half:], -2))
        pieces = [packed, first, second, third, fourth, fifth, sixth, *last]
    away = (jnp.arange(parts, dtype=jnp.int32) - me) * (1 - 2 * core)
    away = lax.rem(away + parts, parts)
    place = jnp.where(away < parts // 2, 2 * away, 2 * parts - 1 - 2 * away)
    place = jnp.concatenate([place, me[None]]).astype(jnp.int32)
    normed, residual = norm(place, pieces, norm_gain.reshape(parts, 1, -1), facts)
    with jax.named_scope("normed_swapped"):
        sibling_normed = to_sibling(normed)
        weights, sibling_normed = lax.optimization_barrier((weights, sibling_normed))
    width = packed.shape[1]
    queries, keys, values, sent = project(normed, sibling_normed, weights, devices // 2, width)
    with jax.named_scope("interaction_gathered"):
        others = lax.all_to_all(
            sent, "cand", 0, 0, tiled=True, axis_index_groups=same_core_groups()
        )
        weights, queries = lax.optimization_barrier((weights, queries))
        sibling_weights = to_sibling(weights[:, :, :, 192:])
    own, other = attend(queries, keys, values, others, normed, sibling_normed, width)
    with jax.named_scope("heads_summed"):
        sibling = to_sibling(other)
        sums = []
        for turn in range(2):
            part = lax.rem(me + parts - turn, parts)
            odd = lax.rem(part, 2)
            away = jnp.where(odd == 0, jnp.array([2, 1, 3, 0]), jnp.array([2, 3, 1, 0]))
            pairs = lax.rem(part // 2 + away, parts // 2).astype(jnp.int32)
            blocks = mix(turn, pairs, own, sibling, weights, sibling_weights)
            sums.append(heads_summed(turn, blocks, odd == 1))
    return (residual.astype(F32) + jnp.concatenate(sums, axis=1)).astype(BF16)


def solution(mesh):
    in_specs = (
        P("cand", None, "mp"),
        P(),
        P(None, "cand", "mp"),
        P("mp", "cand"),
        P("cand"),
        P("cand"),
        P("cand"),
    )
    out_specs = P(("cand", "mp"), None)
    return jax.shard_map(shards, mesh=mesh, in_specs=in_specs, out_specs=out_specs, check_vma=False)
```

```python
import math

import jax
import jax.numpy as jnp
from jax import lax
from jax.experimental import pallas as pl
from jax.experimental.pallas import tpu as pltpu
from jax.sharding import PartitionSpec as P

HD = 128
EPS = 1e-05
NEGATIVE = -1e30
VMEM_LIMIT = 48 * 1024 * 1024
F32 = jnp.float32
BF16 = jnp.bfloat16
NT = (((1,), (1,)), ((), ()))


def along(shard, axis, by):
    length = lax.axis_size(axis)
    return lax.ppermute(shard, axis, [(i, (i + by) % length) for i in range(length)])


def to_sibling(shard):
    length = lax.axis_size("cand")
    return lax.ppermute(shard, "cand", [(i, i ^ 1) for i in range(length)])


def same_core_groups():
    length = lax.axis_size("cand")
    return [list(range(core, length, 2)) for core in range(2)]


ALONG_Z = 8


def x_groups():
    length = lax.axis_size("cand")
    step = 2 * ALONG_Z
    return [
        [x + 2 * z + core for x in range(0, length, step) for core in range(2)]
        for z in range(ALONG_Z)
    ]


def z_groups():
    length = lax.axis_size("cand")
    step = 2 * ALONG_Z
    return [
        [x + 2 * z + core for z in range(ALONG_Z)]
        for x in range(0, length, step)
        for core in range(2)
    ]


def to_outer(shard):
    length = lax.axis_size("cand")
    pairs = [(i, (i + (1 if i % 2 else length - 1)) % length) for i in range(length)]
    return lax.ppermute(shard, "cand", pairs)


def opposed(shard, by):
    chips, parts = lax.axis_size("cand"), lax.axis_size("mp")
    pairs = []
    for device in range(chips):
        signed = by if device % 2 == 0 else -by
        for part in range(parts):
            pairs.append((device * parts + part, device * parts + (part + signed) % parts))
    return lax.ppermute(shard, ("cand", "mp"), pairs)


def pick_kernel(table, passages, inner, outer, kept):
    me = lax.axis_index("cand")
    devices = lax.axis_size("cand")
    slots, length, width = passages.shape
    row = lax.broadcasted_iota(jnp.int32, (16, width), 0)
    lane = lax.broadcasted_iota(jnp.int32, (16, width), 1)
    number = [jnp.int32(0)] * 3
    core = lax.rem(me, 2)
    inward = jnp.where(core == 0, 1, devices - 1)
    outward = jnp.where(core == 0, devices - 1, 1)
    for slot in range(slots):
        ahead = lax.rem(table[0, slot] - me + devices, devices)
        facts = jnp.where(lane < width // 2, table[1, slot], table[2, slot]).astype(F32)
        tail = passages[slot, length - 16 :, :].astype(F32)
        tail = jnp.where(row == 15, facts, tail).astype(BF16)
        for which, (wanted, target) in enumerate(((inward, inner), (outward, outer), (0, kept))):
            hit = ahead == wanted
            place = jnp.minimum(number[which], target.shape[0] - 1)

            @pl.when(hit)
            def _():
                target[place, : length - 16, :] = passages[slot, : length - 16, :]
                target[place, length - 16 :, :] = tail

            number[which] = number[which] + hit.astype(jnp.int32)


def pick(table, passages):
    slots, length, width = passages.shape
    smem = pl.BlockSpec(memory_space=pltpu.SMEM)
    vmem = pl.BlockSpec(memory_space=pltpu.VMEM)
    shape = lambda n: jax.ShapeDtypeStruct((n, length, width), BF16)
    return pl.pallas_call(
        pick_kernel,
        out_shape=(shape(2), shape(2), shape(slots - 4)),
        in_specs=[smem, vmem],
        out_specs=(vmem, vmem, vmem),
        compiler_params=pltpu.CompilerParams(vmem_limit_bytes=VMEM_LIMIT),
    )(table, passages)


def copy_kernel(w_qkv, w_out, copies):
    depth = w_qkv.shape[1]
    for copy in range(copies.shape[0]):
        lanes = slice(copy % 2 * HD, (copy % 2 + 1) * HD)
        for part in range(3):
            copies[copy, part * depth : (part + 1) * depth, :] = w_qkv[part, :, lanes]
        copies[copy, 3 * depth :, :] = w_out[:, lanes]


def copies_by_head(w_qkv, w_out, number):
    vmem = pl.BlockSpec(memory_space=pltpu.VMEM)
    depth = 3 * w_qkv.shape[1] + w_out.shape[0]
    return pl.pallas_call(
        copy_kernel,
        out_shape=jax.ShapeDtypeStruct((number, depth, HD), BF16),
        in_specs=[vmem, vmem],
        out_specs=vmem,
        compiler_params=pltpu.CompilerParams(vmem_limit_bytes=VMEM_LIMIT),
    )(w_qkv, w_out)


def pack_kernel(inner, kept, outer, packed, facts):
    rows = packed.shape[0]
    length = kept.shape[1]
    first = lax.rem(lax.axis_index("cand"), 2) == 0
    blocks = (
        [jnp.where(first, outer[i], inner[i]) for i in range(outer.shape[0])]
        + [kept[i] for i in range(kept.shape[0])]
        + [jnp.where(first, inner[i], outer[i]) for i in range(inner.shape[0])]
    )
    position = lax.broadcasted_iota(jnp.int32, (rows, length), 0)
    offset = lax.broadcasted_iota(jnp.int32, (rows, length), 1)
    start = jnp.zeros((1, length), jnp.int32)
    total = jnp.zeros(packed.shape, F32)
    for slot, block in enumerate(blocks):
        fact = block[length - 16 :, :].astype(F32)[15:16, :]
        facts[slot : slot + 1, :] = fact
        count = fact[:, :length].astype(jnp.int32)
        chosen = (position == start + offset) & (offset < count)
        total = total + jnp.dot(
            chosen.astype(F32).astype(BF16), block, preferred_element_type=F32
        )
        start = start + count
    packed[...] = total.astype(BF16)


def pack(inner, kept, outer):
    slots = inner.shape[0] + kept.shape[0] + outer.shape[0]
    length, width = kept.shape[1:]
    vmem = pl.BlockSpec(memory_space=pltpu.VMEM)
    return pl.pallas_call(
        pack_kernel,
        out_shape=(
            jax.ShapeDtypeStruct((slots * length // 2, width), BF16),
            jax.ShapeDtypeStruct((slots, width), F32),
        ),
        in_specs=[vmem] * 3,
        out_specs=(vmem, vmem),
        compiler_params=pltpu.CompilerParams(vmem_limit_bytes=VMEM_LIMIT),
    )(inner, kept, outer)


def norm_kernel(place, *refs):
    pieces, (gain, facts, normed, residual, rows_in) = refs[:9], refs[9:]
    rows, width = pieces[0].shape
    parts = rows_in.shape[0]
    half = rows // 2
    share = residual.shape[0]
    row = pl.multiple_of(place[8] * share, share)
    square = jnp.zeros((rows, HD), F32)
    for number in range(8):
        if number < 7:
            block = pieces[number][...]
        else:
            block = jnp.concatenate([pieces[7][...], pieces[8][...]], axis=0)
        rows_in[place[number]] = block
        x = block.astype(F32)
        x = x * x
        for lane in range(0, width, HD):
            square = square + x[:, lane : lane + HD]
    inverse = lax.rsqrt(jnp.sum(square, axis=1, keepdims=True) / (parts * width) + EPS)
    for part in range(parts):
        lanes = slice(part * width, (part + 1) * width)
        x = rows_in[part].astype(F32)
        normed[:rows, lanes] = (x * inverse * gain[part]).astype(BF16)
        residual[:, lanes] = rows_in[part, pl.ds(row, share), :]
    normed[rows:, :width] = jnp.concatenate(
        [facts[...], jnp.zeros_like(facts)], axis=0
    ).astype(BF16)
    normed[rows:, width:] = jnp.zeros((16, (parts - 1) * width), BF16)


def norm(place, pieces, gain, facts):
    rows, width = pieces[0].shape
    smem = pl.BlockSpec(memory_space=pltpu.SMEM)
    vmem = pl.BlockSpec(memory_space=pltpu.VMEM)
    return pl.pallas_call(
        norm_kernel,
        out_shape=(
            jax.ShapeDtypeStruct((rows + 16, 8 * width), BF16),
            jax.ShapeDtypeStruct((rows // 8, 8 * width), BF16),
        ),
        in_specs=[smem] + [vmem] * 11,
        out_specs=(vmem, vmem),
        scratch_shapes=[pltpu.VMEM((8, rows, width), BF16)],
        compiler_params=pltpu.CompilerParams(vmem_limit_bytes=VMEM_LIMIT),
    )(place, *pieces, gain, facts)


def project_kernel(mine, theirs, weights, facts, other_facts, queries, keys, values, sent, total):
    step = pl.program_id(0)
    rows = mine.shape[0] - 16
    depth = weights.shape[3] // 3
    block = jnp.concatenate(
        [
            weights[:, 0, :, part * depth : (part + 1) * depth, :].reshape(-1, HD)
            for part in range(3)
        ],
        axis=1,
    )
    for side, source in enumerate((mine, theirs)):
        there = slice(side * rows, (side + 1) * rows)
        product = jnp.dot(source[:rows, :], block, preferred_element_type=F32)

        @pl.when(step == 0)
        def _():
            total[there, :] = product

        @pl.when(step > 0)
        def _():
            total[there, :] += product

    @pl.when(step == pl.num_programs(0) - 1)
    def _():
        done = [total[:, part * HD : (part + 1) * HD].astype(BF16) for part in range(3)]
        queries[...], keys[...], values[...] = done
        slots = 8
        slot_of = lax.broadcasted_iota(jnp.int32, (2 * slots, 2 * rows), 0)
        position = lax.broadcasted_iota(jnp.int32, (2 * slots, 2 * rows), 1)
        first = jnp.zeros((2 * slots, 2 * rows), jnp.int32)
        asked = jnp.zeros((2 * slots, HD), jnp.int32)
        half = facts.shape[1] // 2
        for side, source in enumerate((facts, other_facts)):
            told = source[...].astype(F32).astype(jnp.int32)
            start = jnp.full((1, HD), side * rows, jnp.int32)
            for slot in range(slots):
                here = slot_of == side * slots + slot
                first = jnp.where(here, jnp.concatenate([start] * (2 * rows // HD), axis=1), first)
                asked = jnp.where(here[:, :HD], told[slot : slot + 1, half : half + HD], asked)
                start = start + told[slot : slot + 1, :HD]
        chosen = (first == position).astype(F32).astype(BF16)
        mark = (asked == position[:, :HD]).astype(F32).astype(BF16)
        key_rows = jnp.dot(chosen, done[1], preferred_element_type=F32).astype(BF16)
        value_rows = jnp.dot(chosen, done[2], preferred_element_type=F32).astype(BF16)
        for copy in range(sent.shape[0] // (2 * slots)):
            there = slice(copy * 2 * slots, (copy + 1) * 2 * slots)
            sent[there, :HD] = key_rows
            sent[there, HD : 2 * HD] = value_rows
            sent[there, 2 * HD :] = mark


def facts_spec(array, width):
    last = array.shape[0] // 16 - 1
    return pl.BlockSpec((16, width), lambda i: (last, 0))


def project(mine, theirs, weights, copies, width):
    rows = mine.shape[0] - 16
    along_z, along_x, cores = weights.shape[:3]
    out = lambda *shape: (
        jax.ShapeDtypeStruct(shape, BF16),
        pl.BlockSpec(shape, lambda i: (0, 0)),
    )
    outs = [out(2 * rows, HD)] * 3 + [out(copies * 16, 3 * HD)]
    x = pl.BlockSpec((mine.shape[0], mine.shape[1] // along_x), lambda i: (0, i))
    return pl.pallas_call(
        project_kernel,
        out_shape=tuple(o[0] for o in outs),
        grid=(along_x,),
        in_specs=[
            x,
            x,
            pl.BlockSpec((along_z, 1, cores, 192, HD), lambda i: (0, i, 0, 0, 0)),
            facts_spec(mine, width),
            facts_spec(theirs, width),
        ],
        out_specs=tuple(o[1] for o in outs),
        scratch_shapes=[pltpu.VMEM((2 * rows, 3 * HD), F32)],
        compiler_params=pltpu.CompilerParams(vmem_limit_bytes=VMEM_LIMIT),
    )(mine, theirs, weights, mine, theirs)


def attend_kernel(queries, keys, values, others, mine, theirs, own_out, other_out):
    slots = 8
    rows = own_out.shape[0]
    half = mine.shape[1] // 2
    count = others.shape[0]
    here = lax.axis_index("cand") // 2 * (2 * slots)
    down = lax.broadcasted_iota(jnp.int32, (rows, rows), 0)
    across = lax.broadcasted_iota(jnp.int32, (rows, rows), 1)
    far_across = lax.broadcasted_iota(jnp.int32, (rows, count), 1)
    scale = 1.0 / math.sqrt(HD)
    for side, (source, out) in enumerate(((mine, own_out), (theirs, other_out))):
        facts = source[...].astype(F32).astype(jnp.int32)
        slot_down = jnp.zeros((rows, rows), jnp.int32)
        slot_across = jnp.zeros((rows, rows), jnp.int32)
        end = jnp.zeros((1, rows), jnp.int32)
        for slot in range(slots):
            end = end + facts[slot : slot + 1, :rows]
            if slot < slots - 1:
                slot_down = slot_down + (down >= end).astype(jnp.int32)
                slot_across = slot_across + (across >= end).astype(jnp.int32)
        asked = jnp.zeros((rows, HD), jnp.int32)
        for slot in range(slots):
            asked = jnp.where(
                slot_down[:, :HD] == slot, facts[slot : slot + 1, half : half + HD], asked
            )
        local = ((slot_down == slot_across) & (down < end) & (across < end)) | (down == across)
        mark = (asked == across[:, :HD]).astype(F32).astype(BF16)
        same = lax.dot_general(mark, others[:, 2 * HD :], NT, preferred_element_type=F32) > 0.5
        itself = here + side * slots + jnp.concatenate([slot_down] * (count // rows), axis=1)
        seen = same & (far_across != itself)
        there = slice(side * rows, (side + 1) * rows)
        query = queries[there, :]
        near_scores = jnp.where(
            local,
            lax.dot_general(query, keys[there, :], NT, preferred_element_type=F32) * scale,
            NEGATIVE,
        )
        far_scores = jnp.where(
            seen,
            lax.dot_general(query, others[:, :HD], NT, preferred_element_type=F32) * scale,
            NEGATIVE,
        )
        peak = jnp.maximum(
            jnp.max(near_scores, axis=1, keepdims=True), jnp.max(far_scores, axis=1, keepdims=True)
        )
        near_raised = jnp.exp(near_scores - peak)
        far_raised = jnp.exp(far_scores - peak)
        bottom = jnp.sum(near_raised, axis=1, keepdims=True) + jnp.sum(
            far_raised, axis=1, keepdims=True
        )
        top = jnp.dot(near_raised.astype(BF16), values[there, :], preferred_element_type=F32)
        top = top + jnp.dot(
            far_raised.astype(BF16), others[:, HD : 2 * HD], preferred_element_type=F32
        )
        out[...] = jnp.where(down[:, :HD] < end[:, :HD], top / bottom, 0.0).astype(BF16)


def attend(queries, keys, values, others, mine, theirs, width):
    whole = lambda array: pl.BlockSpec(array.shape, lambda i: (0, 0))
    rows = queries.shape[0] // 2
    shape = jax.ShapeDtypeStruct((rows, HD), BF16)
    spec = pl.BlockSpec((rows, HD), lambda i: (0, 0))
    return pl.pallas_call(
        attend_kernel,
        out_shape=(shape, shape),
        grid=(1,),
        in_specs=[whole(array) for array in (queries, keys, values, others)]
        + [facts_spec(mine, width), facts_spec(theirs, width)],
        out_specs=(spec, spec),
        compiler_params=pltpu.CompilerParams(vmem_limit_bytes=VMEM_LIMIT),
    )(queries, keys, values, others, mine, theirs)


def mix_kernel(own, sibling, own_weights, sibling_weights, out):
    along_z, along_x, _, depth, _ = own_weights.shape
    attended = jnp.concatenate([own[...], sibling[...]], axis=1)
    width = 2 * depth
    for x in range(along_x):
        for z in range(0, along_z, 2):
            block = jnp.concatenate(
                [
                    own_weights[z : z + 2, x].reshape(2 * width, HD),
                    sibling_weights[z : z + 2, x].reshape(2 * width, HD),
                ],
                axis=1,
            )
            at = (x * along_z + z) * width
            out[:, at : at + 2 * width] = lax.dot_general(
                attended, block, NT, preferred_element_type=F32
            ).astype(BF16)


def mix(own, sibling, own_weights, sibling_weights):
    along_z, along_x, cores, depth, _ = sibling_weights.shape
    rows, width = own.shape[0], along_z * along_x * cores * depth
    whole = lambda array: pl.BlockSpec(array.shape, lambda i: (0,) * array.ndim)
    return pl.pallas_call(
        mix_kernel,
        out_shape=jax.ShapeDtypeStruct((rows, width), BF16),
        grid=(1,),
        in_specs=[
            whole(own),
            whole(sibling),
            pl.BlockSpec(sibling_weights.shape, lambda i: (0, 0, 0, 3, 0)),
            whole(sibling_weights),
        ],
        out_specs=pl.BlockSpec((rows, width), lambda i: (0, 0)),
        compiler_params=pltpu.CompilerParams(vmem_limit_bytes=VMEM_LIMIT),
    )(own, sibling, own_weights, sibling_weights)


def shards(passages, norm_gain, w_qkv, w_out, counts, owners, query_of):
    devices = lax.axis_size("cand")
    parts = lax.axis_size("mp")
    me = lax.axis_index("mp")
    core = lax.rem(lax.axis_index("cand"), 2)
    along_x = devices // (2 * ALONG_Z)
    with jax.named_scope("weights_gathered"):
        copies = copies_by_head(w_qkv, w_out.T, 2 * along_x)
        from_x = lax.all_to_all(
            copies.reshape(-1, HD), "cand", 0, 0, tiled=True, axis_index_groups=x_groups()
        ).reshape(along_x, 2, -1, HD)
        weights = lax.all_gather(from_x, "cand", axis_index_groups=z_groups())
    with jax.named_scope("passages_handed_over"):
        inner, outer, kept = pick(jnp.stack([owners, counts, query_of]), passages)
        from_x, inner, outer = lax.optimization_barrier((from_x, inner, outer))
        inner, outer = to_sibling(inner), to_outer(outer)
    with jax.named_scope("passages_packed"):
        packed, facts = pack(inner, kept, outer)
    with jax.named_scope("features_gathered"):
        half = packed.shape[0] // 2
        third, fourth = opposed(packed, 2), opposed(packed, -2)
        first, second = opposed(packed, 1), opposed(packed, -1)
        first, second, third, fourth = lax.optimization_barrier((first, second, third, fourth))
        fifth, sixth = opposed(third, 1), opposed(fourth, -1)
        last = (opposed(third[:half], 2), opposed(fourth[half:], -2))
        pieces = [packed, first, second, third, fourth, fifth, sixth, *last]
    away = jnp.array([0, -1, 1, -2, 2, -3, 3, 4, 0], jnp.int32)
    place = lax.rem(me + parts + away * (1 - 2 * core), parts).astype(jnp.int32)
    normed, residual = norm(place, pieces, norm_gain.reshape(parts, 1, -1), facts)
    with jax.named_scope("normed_swapped"):
        sibling_normed = to_sibling(normed)
        weights, sibling_normed = lax.optimization_barrier((weights, sibling_normed))
    width = packed.shape[1]
    queries, keys, values, sent = project(normed, sibling_normed, weights, devices // 2, width)
    with jax.named_scope("interaction_gathered"):
        others = lax.all_to_all(
            sent, "cand", 0, 0, tiled=True, axis_index_groups=same_core_groups()
        )
        weights, queries = lax.optimization_barrier((weights, queries))
        sibling_weights = to_sibling(weights[:, :, :, 192:])
    own, other = attend(queries, keys, values, others, normed, sibling_normed, width)
    with jax.named_scope("heads_summed"):
        sibling = to_sibling(other)
        partial = mix(own, sibling, weights, sibling_weights)
        summed = lax.psum_scatter(partial, "mp", scatter_dimension=0, tiled=True)
    return (residual.astype(F32) + summed.astype(F32)).astype(BF16)


def solution(mesh):
    in_specs = (
        P("cand", None, "mp"),
        P(),
        P(None, "cand", "mp"),
        P("mp", "cand"),
        P("cand"),
        P("cand"),
        P("cand"),
    )
    out_specs = P(("cand", "mp"), None)
    return jax.shard_map(shards, mesh=mesh, in_specs=in_specs, out_specs=out_specs, check_vma=False)
```

```python
import math

import jax
import jax.numpy as jnp
from jax import lax
from jax.experimental import pallas as pl
from jax.experimental.pallas import tpu as pltpu
from jax.sharding import PartitionSpec as P

HD = 128
EPS = 1e-05
NEGATIVE = -1e30
VMEM_LIMIT = 48 * 1024 * 1024
F32 = jnp.float32
BF16 = jnp.bfloat16
NT = (((1,), (1,)), ((), ()))


def along(shard, axis, by):
    length = lax.axis_size(axis)
    return lax.ppermute(shard, axis, [(i, (i + by) % length) for i in range(length)])


def to_sibling(shard):
    length = lax.axis_size("cand")
    return lax.ppermute(shard, "cand", [(i, i ^ 1) for i in range(length)])


def same_core_groups():
    length = lax.axis_size("cand")
    return [list(range(core, length, 2)) for core in range(2)]


ALONG_Z = 8


def x_groups():
    length = lax.axis_size("cand")
    step = 2 * ALONG_Z
    return [
        [x + 2 * z + core for x in range(0, length, step) for core in range(2)]
        for z in range(ALONG_Z)
    ]


def z_groups():
    length = lax.axis_size("cand")
    step = 2 * ALONG_Z
    return [
        [x + 2 * z + core for z in range(ALONG_Z)]
        for x in range(0, length, step)
        for core in range(2)
    ]


def to_outer(shard):
    length = lax.axis_size("cand")
    pairs = [(i, (i + (1 if i % 2 else length - 1)) % length) for i in range(length)]
    return lax.ppermute(shard, "cand", pairs)


def opposed(shard, by):
    chips, parts = lax.axis_size("cand"), lax.axis_size("mp")
    pairs = []
    for device in range(chips):
        signed = by if device % 2 == 0 else -by
        for part in range(parts):
            pairs.append((device * parts + part, device * parts + (part + signed) % parts))
    return lax.ppermute(shard, ("cand", "mp"), pairs)


def pick_kernel(table, passages, inner, outer, kept):
    me = lax.axis_index("cand")
    devices = lax.axis_size("cand")
    slots, length, width = passages.shape
    row = lax.broadcasted_iota(jnp.int32, (16, width), 0)
    lane = lax.broadcasted_iota(jnp.int32, (16, width), 1)
    number = [jnp.int32(0)] * 3
    core = lax.rem(me, 2)
    inward = jnp.where(core == 0, 1, devices - 1)
    outward = jnp.where(core == 0, devices - 1, 1)
    for slot in range(slots):
        ahead = lax.rem(table[0, slot] - me + devices, devices)
        facts = jnp.where(lane < width // 2, table[1, slot], table[2, slot]).astype(F32)
        tail = passages[slot, length - 16 :, :].astype(F32)
        tail = jnp.where(row == 15, facts, tail).astype(BF16)
        for which, (wanted, target) in enumerate(((inward, inner), (outward, outer), (0, kept))):
            hit = ahead == wanted
            place = jnp.minimum(number[which], target.shape[0] - 1)

            @pl.when(hit)
            def _():
                target[place, : length - 16, :] = passages[slot, : length - 16, :]
                target[place, length - 16 :, :] = tail

            number[which] = number[which] + hit.astype(jnp.int32)


def pick(table, passages):
    slots, length, width = passages.shape
    smem = pl.BlockSpec(memory_space=pltpu.SMEM)
    vmem = pl.BlockSpec(memory_space=pltpu.VMEM)
    shape = lambda n: jax.ShapeDtypeStruct((n, length, width), BF16)
    return pl.pallas_call(
        pick_kernel,
        out_shape=(shape(2), shape(2), shape(slots - 4)),
        in_specs=[smem, vmem],
        out_specs=(vmem, vmem, vmem),
        compiler_params=pltpu.CompilerParams(vmem_limit_bytes=VMEM_LIMIT),
    )(table, passages)


def copy_kernel(w_qkv, w_out, copies):
    depth = w_qkv.shape[1]
    for copy in range(copies.shape[0]):
        lanes = slice(copy % 2 * HD, (copy % 2 + 1) * HD)
        for part in range(3):
            copies[copy, part * depth : (part + 1) * depth, :] = w_qkv[part, :, lanes]
        copies[copy, 3 * depth :, :] = w_out[:, lanes]


def copies_by_head(w_qkv, w_out, number):
    vmem = pl.BlockSpec(memory_space=pltpu.VMEM)
    depth = 3 * w_qkv.shape[1] + w_out.shape[0]
    return pl.pallas_call(
        copy_kernel,
        out_shape=jax.ShapeDtypeStruct((number, depth, HD), BF16),
        in_specs=[vmem, vmem],
        out_specs=vmem,
        compiler_params=pltpu.CompilerParams(vmem_limit_bytes=VMEM_LIMIT),
    )(w_qkv, w_out)


def pack_kernel(inner, kept, outer, packed, facts):
    rows = packed.shape[0]
    length = kept.shape[1]
    first = lax.rem(lax.axis_index("cand"), 2) == 0
    blocks = (
        [jnp.where(first, outer[i], inner[i]) for i in range(outer.shape[0])]
        + [kept[i] for i in range(kept.shape[0])]
        + [jnp.where(first, inner[i], outer[i]) for i in range(inner.shape[0])]
    )
    position = lax.broadcasted_iota(jnp.int32, (rows, length), 0)
    offset = lax.broadcasted_iota(jnp.int32, (rows, length), 1)
    start = jnp.zeros((1, length), jnp.int32)
    total = jnp.zeros(packed.shape, F32)
    for slot, block in enumerate(blocks):
        fact = block[length - 16 :, :].astype(F32)[15:16, :]
        facts[slot : slot + 1, :] = fact
        count = fact[:, :length].astype(jnp.int32)
        chosen = (position == start + offset) & (offset < count)
        total = total + jnp.dot(
            chosen.astype(F32).astype(BF16), block, preferred_element_type=F32
        )
        start = start + count
    packed[...] = total.astype(BF16)


def pack(inner, kept, outer):
    slots = inner.shape[0] + kept.shape[0] + outer.shape[0]
    length, width = kept.shape[1:]
    vmem = pl.BlockSpec(memory_space=pltpu.VMEM)
    return pl.pallas_call(
        pack_kernel,
        out_shape=(
            jax.ShapeDtypeStruct((slots * length // 2, width), BF16),
            jax.ShapeDtypeStruct((slots, width), F32),
        ),
        in_specs=[vmem] * 3,
        out_specs=(vmem, vmem),
        compiler_params=pltpu.CompilerParams(vmem_limit_bytes=VMEM_LIMIT),
    )(inner, kept, outer)


def norm_kernel(place, *refs):
    pieces, (gain, normed, residual, rows_in) = refs[:9], refs[9:]
    rows, width = pieces[0].shape
    parts = rows_in.shape[0]
    half = rows // 2
    share = residual.shape[0]
    row = pl.multiple_of(place[8] * share, share)
    square = jnp.zeros((rows, HD), F32)
    for number in range(8):
        if number < 7:
            block = pieces[number][...]
        else:
            block = jnp.concatenate([pieces[7][...], pieces[8][...]], axis=0)
        rows_in[place[number]] = block
        x = block.astype(F32)
        x = x * x
        for lane in range(0, width, HD):
            square = square + x[:, lane : lane + HD]
    inverse = lax.rsqrt(jnp.sum(square, axis=1, keepdims=True) / (parts * width) + EPS)
    for part in range(parts):
        lanes = slice(part * width, (part + 1) * width)
        x = rows_in[part].astype(F32)
        normed[:, lanes] = (x * inverse * gain[part]).astype(BF16)
        residual[:, lanes] = rows_in[part, pl.ds(row, share), :]


def norm(place, pieces, gain):
    rows, width = pieces[0].shape
    smem = pl.BlockSpec(memory_space=pltpu.SMEM)
    vmem = pl.BlockSpec(memory_space=pltpu.VMEM)
    return pl.pallas_call(
        norm_kernel,
        out_shape=(
            jax.ShapeDtypeStruct((rows, 8 * width), BF16),
            jax.ShapeDtypeStruct((rows // 8, 8 * width), BF16),
        ),
        in_specs=[smem] + [vmem] * 10,
        out_specs=(vmem, vmem),
        scratch_shapes=[pltpu.VMEM((8, rows, width), BF16)],
        compiler_params=pltpu.CompilerParams(vmem_limit_bytes=VMEM_LIMIT),
    )(place, *pieces, gain)


def project_kernel(x, own_weights, sibling_weights, facts, queries, keys, values, sent, total):
    step = pl.program_id(0)
    rows = x.shape[0]
    columns = 2 * HD
    depth = own_weights.shape[3] // 3
    block = jnp.concatenate(
        [
            source[:, 0, :, part * depth : (part + 1) * depth, :].reshape(-1, HD)
            for part in range(3)
            for source in (own_weights, sibling_weights)
        ],
        axis=1,
    )
    product = jnp.dot(x[...], block, preferred_element_type=F32)

    @pl.when(step == 0)
    def _():
        total[...] = product

    @pl.when(step > 0)
    def _():
        total[...] += product

    @pl.when(step == pl.num_programs(0) - 1)
    def _():
        done = [
            total[:, part * columns : (part + 1) * columns].astype(BF16) for part in range(3)
        ]
        queries[...], keys[...], values[...] = done
        slots = facts.shape[0]
        half = facts.shape[1] // 2
        slot_of = lax.broadcasted_iota(jnp.int32, (2 * slots, rows), 0) % slots
        position = lax.broadcasted_iota(jnp.int32, (2 * slots, rows), 1)
        start = jnp.zeros((1, rows), jnp.int32)
        first = jnp.zeros((2 * slots, rows), jnp.int32)
        asked = jnp.zeros((2 * slots, HD), jnp.int32)
        for slot in range(slots):
            here = slot_of == slot
            first = jnp.where(here, start, first)
            asked = jnp.where(
                here[:, :HD], facts[slot : slot + 1, half : half + HD].astype(jnp.int32), asked
            )
            start = start + facts[slot : slot + 1, :rows].astype(jnp.int32)
        chosen = (first == position).astype(F32).astype(BF16)
        mark = (asked == position[:, :HD]).astype(F32).astype(BF16)
        key_rows = jnp.dot(chosen, done[1], preferred_element_type=F32).astype(BF16)
        value_rows = jnp.dot(chosen, done[2], preferred_element_type=F32).astype(BF16)
        for copy in range(sent.shape[0] // (2 * slots)):
            there = slice(copy * 2 * slots, (copy + 1) * 2 * slots)
            sent[there, :columns] = key_rows
            sent[there, columns : 2 * columns] = value_rows
            sent[there, 2 * columns :] = mark


def project(normed, own_weights, sibling_weights, facts, copies):
    rows, features = normed.shape
    along_z, along_x, cores = own_weights.shape[:3]
    columns = 2 * HD
    out = lambda *shape: (
        jax.ShapeDtypeStruct(shape, BF16),
        pl.BlockSpec(shape, lambda i: (0, 0)),
    )
    outs = [out(rows, columns)] * 3 + [out(copies * facts.shape[0], 2 * columns + HD)]
    weight = pl.BlockSpec((along_z, 1, cores, 192, HD), lambda i: (0, i, 0, 0, 0))
    return pl.pallas_call(
        project_kernel,
        out_shape=tuple(o[0] for o in outs),
        grid=(along_x,),
        in_specs=[
            pl.BlockSpec((rows, features // along_x), lambda i: (0, i)),
            weight,
            weight,
            pl.BlockSpec(facts.shape, lambda i: (0, 0)),
        ],
        out_specs=tuple(o[1] for o in outs),
        scratch_shapes=[pltpu.VMEM((rows, 3 * columns), F32)],
        compiler_params=pltpu.CompilerParams(vmem_limit_bytes=VMEM_LIMIT),
    )(normed, own_weights, sibling_weights, facts)


def attend_kernel(queries, keys, values, near, far, facts, own_weights, sibling_weights, out):
    rows, columns = queries.shape
    slots = facts.shape[0]
    half = facts.shape[1] // 2
    here = lax.axis_index("cand") // 2 * slots
    down = lax.broadcasted_iota(jnp.int32, (rows, rows), 0)
    across = lax.broadcasted_iota(jnp.int32, (rows, rows), 1)
    slot_down = jnp.zeros((rows, rows), jnp.int32)
    slot_across = jnp.zeros((rows, rows), jnp.int32)
    end = jnp.zeros((1, rows), jnp.int32)
    for slot in range(slots):
        end = end + facts[slot : slot + 1, :rows].astype(jnp.int32)
        if slot < slots - 1:
            slot_down = slot_down + (down >= end).astype(jnp.int32)
            slot_across = slot_across + (across >= end).astype(jnp.int32)
    asked = jnp.zeros((rows, HD), jnp.int32)
    for slot in range(slots):
        asked = jnp.where(
            slot_down[:, :HD] == slot,
            facts[slot : slot + 1, half : half + HD].astype(jnp.int32),
            asked,
        )
    local = ((slot_down == slot_across) & (down < end) & (across < end)) | (down == across)
    mark = (asked == across[:, :HD]).astype(F32).astype(BF16)
    same = lambda other: lax.dot_general(
        mark, other[:, 2 * columns :], NT, preferred_element_type=F32
    ) > 0.5
    masks = [local, same(near) & (across != here + slot_down), same(far)]
    scale = 1.0 / math.sqrt(HD)
    heads = []
    for head in range(columns // HD):
        lanes = slice(head * HD, (head + 1) * HD)
        value_lanes = slice(columns + head * HD, columns + (head + 1) * HD)
        swapped = columns - HD * (1 + head)
        far_lanes = slice(swapped, swapped + HD)
        far_value_lanes = slice(columns + swapped, columns + swapped + HD)
        query = queries[:, lanes]
        scores = [
            jnp.where(
                mask,
                lax.dot_general(query, key, NT, preferred_element_type=F32) * scale,
                NEGATIVE,
            )
            for mask, key in zip(masks, (keys[:, lanes], near[:, lanes], far[:, far_lanes]))
        ]
        peak = jnp.maximum(jnp.maximum(scores[0], scores[1]), scores[2])
        peak = jnp.max(peak, axis=1, keepdims=True)
        raised = [jnp.exp(score - peak) for score in scores]
        bottom = jnp.sum(raised[0] + raised[1] + raised[2], axis=1, keepdims=True)
        top = jnp.zeros((rows, HD), F32)
        for part, value in zip(
            raised, (values[:, lanes], near[:, value_lanes], far[:, far_value_lanes])
        ):
            top = top + jnp.dot(part.astype(BF16), value, preferred_element_type=F32)
        heads.append(jnp.where(down[:, :HD] < end[:, :HD], top / bottom, 0.0).astype(BF16))
    attended = jnp.concatenate(heads, axis=1)
    along_z, along_x, cores, depth, _ = own_weights.shape
    width = cores * depth
    for x in range(along_x):
        for z in range(0, along_z, 2):
            block = jnp.concatenate(
                [
                    source[z : z + 2, x].reshape(2 * width, HD)
                    for source in (own_weights, sibling_weights)
                ],
                axis=1,
            )
            at = (x * along_z + z) * width
            out[:, at : at + 2 * width] = lax.dot_general(
                attended, block, NT, preferred_element_type=F32
            ).astype(BF16)


def attend(queries, keys, values, near, far, facts, own_weights, sibling_weights):
    rows = queries.shape[0]
    along_z, along_x, cores, depth, _ = own_weights.shape
    depth = depth // 4
    whole = lambda array: pl.BlockSpec(array.shape, lambda i: (0, 0))
    weight = pl.BlockSpec((along_z, along_x, cores, depth, HD), lambda i: (0, 0, 0, 3, 0))
    small = (queries, keys, values, near, far, facts)
    width = along_z * along_x * cores * depth
    return pl.pallas_call(
        attend_kernel,
        out_shape=jax.ShapeDtypeStruct((rows, width), BF16),
        grid=(1,),
        in_specs=[whole(array) for array in small] + [weight, weight],
        out_specs=pl.BlockSpec((rows, width), lambda i: (0, 0)),
        compiler_params=pltpu.CompilerParams(vmem_limit_bytes=VMEM_LIMIT),
    )(*small, own_weights, sibling_weights)


def shards(passages, norm_gain, w_qkv, w_out, counts, owners, query_of):
    devices = lax.axis_size("cand")
    parts = lax.axis_size("mp")
    me = lax.axis_index("mp")
    core = lax.rem(lax.axis_index("cand"), 2)
    along_x = devices // (2 * ALONG_Z)
    with jax.named_scope("weights_gathered"):
        copies = copies_by_head(w_qkv, w_out.T, 2 * along_x)
        from_x = lax.all_to_all(
            copies.reshape(-1, HD), "cand", 0, 0, tiled=True, axis_index_groups=x_groups()
        ).reshape(along_x, 2, -1, HD)
        weights = lax.all_gather(from_x, "cand", axis_index_groups=z_groups())
    with jax.named_scope("passages_handed_over"):
        inner, outer, kept = pick(jnp.stack([owners, counts, query_of]), passages)
        from_x, inner, outer = lax.optimization_barrier((from_x, inner, outer))
        inner, outer = to_sibling(inner), to_outer(outer)
    with jax.named_scope("passages_packed"):
        packed, facts = pack(inner, kept, outer)
    with jax.named_scope("features_gathered"):
        half = packed.shape[0] // 2
        third, fourth = opposed(packed, 2), opposed(packed, -2)
        first, second = opposed(packed, 1), opposed(packed, -1)
        first, second, third, fourth = lax.optimization_barrier((first, second, third, fourth))
        fifth, sixth = opposed(third, 1), opposed(fourth, -1)
        last = (opposed(third[:half], 2), opposed(fourth[half:], -2))
        pieces = [packed, first, second, third, fourth, fifth, sixth, *last]
    away = jnp.array([0, -1, 1, -2, 2, -3, 3, 4, 0], jnp.int32)
    place = lax.rem(me + parts + away * (1 - 2 * core), parts).astype(jnp.int32)
    normed, residual = norm(place, pieces, norm_gain.reshape(parts, 1, -1))
    with jax.named_scope("weights_swapped"):
        weights, *_ = lax.optimization_barrier((weights, fifth, sixth, *last))
        sibling_weights = to_sibling(weights)
    queries, keys, values, sent = project(normed, weights, sibling_weights, facts, devices // 2)
    with jax.named_scope("interaction_gathered"):
        near = lax.all_to_all(
            sent, "cand", 0, 0, tiled=True, axis_index_groups=same_core_groups()
        )
        far = to_sibling(near)
    partial = attend(queries, keys, values, near, far, facts, weights, sibling_weights)
    with jax.named_scope("heads_summed"):
        summed = lax.psum_scatter(partial, "mp", scatter_dimension=0, tiled=True)
    return (residual.astype(F32) + summed.astype(F32)).astype(BF16)


def solution(mesh):
    in_specs = (
        P("cand", None, "mp"),
        P(),
        P(None, "cand", "mp"),
        P("mp", "cand"),
        P("cand"),
        P("cand"),
        P("cand"),
    )
    out_specs = P(("cand", "mp"), None)
    return jax.shard_map(shards, mesh=mesh, in_specs=in_specs, out_specs=out_specs, check_vma=False)
```

```python
import math

import jax
import jax.numpy as jnp
from jax import lax
from jax.experimental import pallas as pl
from jax.experimental.pallas import tpu as pltpu
from jax.sharding import PartitionSpec as P

HD = 128
EPS = 1e-05
NEGATIVE = -1e30
VMEM_LIMIT = 48 * 1024 * 1024
F32 = jnp.float32
BF16 = jnp.bfloat16
NT = (((1,), (1,)), ((), ()))


def along(shard, axis, by):
    length = lax.axis_size(axis)
    return lax.ppermute(shard, axis, [(i, (i + by) % length) for i in range(length)])


def to_sibling(shard):
    length = lax.axis_size("cand")
    return lax.ppermute(shard, "cand", [(i, i ^ 1) for i in range(length)])


def same_core_groups():
    length = lax.axis_size("cand")
    return [list(range(core, length, 2)) for core in range(2)]


ALONG_Z = 8


def x_groups():
    length = lax.axis_size("cand")
    step = 2 * ALONG_Z
    return [
        [x + 2 * z + core for x in range(0, length, step) for core in range(2)]
        for z in range(ALONG_Z)
    ]


def z_groups():
    length = lax.axis_size("cand")
    step = 2 * ALONG_Z
    return [
        [x + 2 * z + core for z in range(ALONG_Z)]
        for x in range(0, length, step)
        for core in range(2)
    ]


def to_outer(shard):
    length = lax.axis_size("cand")
    pairs = [(i, (i + (1 if i % 2 else length - 1)) % length) for i in range(length)]
    return lax.ppermute(shard, "cand", pairs)


def quarter_groups():
    devices, parts = lax.axis_size("cand"), lax.axis_size("mp")
    return [
        [(chip + core) * parts + part for part in range(parity, parts, 2) for core in range(2)]
        for chip in range(0, devices, 2)
        for parity in range(2)
    ]


def opposed(shard, by):
    chips, parts = lax.axis_size("cand"), lax.axis_size("mp")
    pairs = []
    for device in range(chips):
        signed = by if device % 2 == 0 else -by
        for part in range(parts):
            pairs.append((device * parts + part, device * parts + (part + signed) % parts))
    return lax.ppermute(shard, ("cand", "mp"), pairs)


def pick_kernel(table, passages, inner, outer, kept):
    me = lax.axis_index("cand")
    devices = lax.axis_size("cand")
    slots, length, width = passages.shape
    row = lax.broadcasted_iota(jnp.int32, (16, width), 0)
    lane = lax.broadcasted_iota(jnp.int32, (16, width), 1)
    number = [jnp.int32(0)] * 3
    core = lax.rem(me, 2)
    inward = jnp.where(core == 0, 1, devices - 1)
    outward = jnp.where(core == 0, devices - 1, 1)
    for slot in range(slots):
        ahead = lax.rem(table[0, slot] - me + devices, devices)
        facts = jnp.where(lane < width // 2, table[1, slot], table[2, slot]).astype(F32)
        tail = passages[slot, length - 16 :, :].astype(F32)
        tail = jnp.where(row == 15, facts, tail).astype(BF16)
        for which, (wanted, target) in enumerate(((inward, inner), (outward, outer), (0, kept))):
            hit = ahead == wanted
            place = jnp.minimum(number[which], target.shape[0] - 1)

            @pl.when(hit)
            def _():
                target[place, : length - 16, :] = passages[slot, : length - 16, :]
                target[place, length - 16 :, :] = tail

            number[which] = number[which] + hit.astype(jnp.int32)


def pick(table, passages):
    slots, length, width = passages.shape
    smem = pl.BlockSpec(memory_space=pltpu.SMEM)
    vmem = pl.BlockSpec(memory_space=pltpu.VMEM)
    shape = lambda n: jax.ShapeDtypeStruct((n, length, width), BF16)
    return pl.pallas_call(
        pick_kernel,
        out_shape=(shape(2), shape(2), shape(slots - 4)),
        in_specs=[smem, vmem],
        out_specs=(vmem, vmem, vmem),
        compiler_params=pltpu.CompilerParams(vmem_limit_bytes=VMEM_LIMIT),
    )(table, passages)


def copy_kernel(w_qkv, w_out, copies):
    depth = w_qkv.shape[1]
    for copy in range(copies.shape[0]):
        lanes = slice(copy % 2 * HD, (copy % 2 + 1) * HD)
        for part in range(3):
            copies[copy, part * depth : (part + 1) * depth, :] = w_qkv[part, :, lanes]
        copies[copy, 3 * depth :, :] = w_out[:, lanes]


def copies_by_head(w_qkv, w_out, number):
    vmem = pl.BlockSpec(memory_space=pltpu.VMEM)
    depth = 3 * w_qkv.shape[1] + w_out.shape[0]
    return pl.pallas_call(
        copy_kernel,
        out_shape=jax.ShapeDtypeStruct((number, depth, HD), BF16),
        in_specs=[vmem, vmem],
        out_specs=vmem,
        compiler_params=pltpu.CompilerParams(vmem_limit_bytes=VMEM_LIMIT),
    )(w_qkv, w_out)


def pack_kernel(inner, kept, outer, packed, facts):
    rows = packed.shape[0]
    length = kept.shape[1]
    first = lax.rem(lax.axis_index("cand"), 2) == 0
    blocks = (
        [jnp.where(first, outer[i], inner[i]) for i in range(outer.shape[0])]
        + [kept[i] for i in range(kept.shape[0])]
        + [jnp.where(first, inner[i], outer[i]) for i in range(inner.shape[0])]
    )
    position = lax.broadcasted_iota(jnp.int32, (rows, length), 0)
    offset = lax.broadcasted_iota(jnp.int32, (rows, length), 1)
    start = jnp.zeros((1, length), jnp.int32)
    total = jnp.zeros(packed.shape, F32)
    for slot, block in enumerate(blocks):
        fact = block[length - 16 :, :].astype(F32)[15:16, :]
        facts[slot : slot + 1, :] = fact
        count = fact[:, :length].astype(jnp.int32)
        chosen = (position == start + offset) & (offset < count)
        total = total + jnp.dot(
            chosen.astype(F32).astype(BF16), block, preferred_element_type=F32
        )
        start = start + count
    packed[...] = total.astype(BF16)


def pack(inner, kept, outer):
    slots = inner.shape[0] + kept.shape[0] + outer.shape[0]
    length, width = kept.shape[1:]
    vmem = pl.BlockSpec(memory_space=pltpu.VMEM)
    return pl.pallas_call(
        pack_kernel,
        out_shape=(
            jax.ShapeDtypeStruct((slots * length // 2, width), BF16),
            jax.ShapeDtypeStruct((slots, width), F32),
        ),
        in_specs=[vmem] * 3,
        out_specs=(vmem, vmem),
        compiler_params=pltpu.CompilerParams(vmem_limit_bytes=VMEM_LIMIT),
    )(inner, kept, outer)


def norm_kernel(place, *refs):
    pieces, (gain, normed, residual, rows_in) = refs[:9], refs[9:]
    rows, width = pieces[0].shape
    parts = rows_in.shape[0]
    half = rows // 2
    share = residual.shape[0]
    row = pl.multiple_of(place[8] * share, share)
    square = jnp.zeros((rows, HD), F32)
    for number in range(8):
        if number < 7:
            block = pieces[number][...]
        else:
            block = jnp.concatenate([pieces[7][...], pieces[8][...]], axis=0)
        rows_in[place[number]] = block
        x = block.astype(F32)
        x = x * x
        for lane in range(0, width, HD):
            square = square + x[:, lane : lane + HD]
    inverse = lax.rsqrt(jnp.sum(square, axis=1, keepdims=True) / (parts * width) + EPS)
    for part in range(parts):
        lanes = slice(part * width, (part + 1) * width)
        x = rows_in[part].astype(F32)
        normed[:, lanes] = (x * inverse * gain[part]).astype(BF16)
        residual[:, lanes] = rows_in[part, pl.ds(row, share), :]


def norm(place, pieces, gain):
    rows, width = pieces[0].shape
    smem = pl.BlockSpec(memory_space=pltpu.SMEM)
    vmem = pl.BlockSpec(memory_space=pltpu.VMEM)
    return pl.pallas_call(
        norm_kernel,
        out_shape=(
            jax.ShapeDtypeStruct((rows, 8 * width), BF16),
            jax.ShapeDtypeStruct((rows // 8, 8 * width), BF16),
        ),
        in_specs=[smem] + [vmem] * 10,
        out_specs=(vmem, vmem),
        scratch_shapes=[pltpu.VMEM((8, rows, width), BF16)],
        compiler_params=pltpu.CompilerParams(vmem_limit_bytes=VMEM_LIMIT),
    )(place, *pieces, gain)


def project_kernel(x, own_weights, sibling_weights, facts, queries, keys, values, sent, total):
    step = pl.program_id(0)
    rows = x.shape[0]
    columns = 2 * HD
    depth = own_weights.shape[3] // 3
    block = jnp.concatenate(
        [
            source[:, 0, :, part * depth : (part + 1) * depth, :].reshape(-1, HD)
            for part in range(3)
            for source in (own_weights, sibling_weights)
        ],
        axis=1,
    )
    product = jnp.dot(x[...], block, preferred_element_type=F32)

    @pl.when(step == 0)
    def _():
        total[...] = product

    @pl.when(step > 0)
    def _():
        total[...] += product

    @pl.when(step == pl.num_programs(0) - 1)
    def _():
        done = [
            total[:, part * columns : (part + 1) * columns].astype(BF16) for part in range(3)
        ]
        queries[...], keys[...], values[...] = done
        slots = facts.shape[0]
        half = facts.shape[1] // 2
        slot_of = lax.broadcasted_iota(jnp.int32, (2 * slots, rows), 0) % slots
        position = lax.broadcasted_iota(jnp.int32, (2 * slots, rows), 1)
        start = jnp.zeros((1, rows), jnp.int32)
        first = jnp.zeros((2 * slots, rows), jnp.int32)
        asked = jnp.zeros((2 * slots, HD), jnp.int32)
        for slot in range(slots):
            here = slot_of == slot
            first = jnp.where(here, start, first)
            asked = jnp.where(
                here[:, :HD], facts[slot : slot + 1, half : half + HD].astype(jnp.int32), asked
            )
            start = start + facts[slot : slot + 1, :rows].astype(jnp.int32)
        chosen = (first == position).astype(F32).astype(BF16)
        mark = (asked == position[:, :HD]).astype(F32).astype(BF16)
        key_rows = jnp.dot(chosen, done[1], preferred_element_type=F32).astype(BF16)
        value_rows = jnp.dot(chosen, done[2], preferred_element_type=F32).astype(BF16)
        for copy in range(sent.shape[0] // (2 * slots)):
            there = slice(copy * 2 * slots, (copy + 1) * 2 * slots)
            sent[there, :columns] = key_rows
            sent[there, columns : 2 * columns] = value_rows
            sent[there, 2 * columns :] = mark


def project(normed, own_weights, sibling_weights, facts, copies):
    rows, features = normed.shape
    along_z, along_x, cores = own_weights.shape[:3]
    columns = 2 * HD
    out = lambda *shape: (
        jax.ShapeDtypeStruct(shape, BF16),
        pl.BlockSpec(shape, lambda i: (0, 0)),
    )
    outs = [out(rows, columns)] * 3 + [out(copies * facts.shape[0], 2 * columns + HD)]
    weight = pl.BlockSpec((along_z, 1, cores, 192, HD), lambda i: (0, i, 0, 0, 0))
    return pl.pallas_call(
        project_kernel,
        out_shape=tuple(o[0] for o in outs),
        grid=(along_x,),
        in_specs=[
            pl.BlockSpec((rows, features // along_x), lambda i: (0, i)),
            weight,
            weight,
            pl.BlockSpec(facts.shape, lambda i: (0, 0)),
        ],
        out_specs=tuple(o[1] for o in outs),
        scratch_shapes=[pltpu.VMEM((rows, 3 * columns), F32)],
        compiler_params=pltpu.CompilerParams(vmem_limit_bytes=VMEM_LIMIT),
    )(normed, own_weights, sibling_weights, facts)


def attend_kernel(queries, keys, values, near, far, facts, out):
    rows, columns = queries.shape
    slots = facts.shape[0]
    half = facts.shape[1] // 2
    here = lax.axis_index("cand") // 2 * slots
    down = lax.broadcasted_iota(jnp.int32, (rows, rows), 0)
    across = lax.broadcasted_iota(jnp.int32, (rows, rows), 1)
    slot_down = jnp.zeros((rows, rows), jnp.int32)
    slot_across = jnp.zeros((rows, rows), jnp.int32)
    end = jnp.zeros((1, rows), jnp.int32)
    for slot in range(slots):
        end = end + facts[slot : slot + 1, :rows].astype(jnp.int32)
        if slot < slots - 1:
            slot_down = slot_down + (down >= end).astype(jnp.int32)
            slot_across = slot_across + (across >= end).astype(jnp.int32)
    asked = jnp.zeros((rows, HD), jnp.int32)
    for slot in range(slots):
        asked = jnp.where(
            slot_down[:, :HD] == slot,
            facts[slot : slot + 1, half : half + HD].astype(jnp.int32),
            asked,
        )
    local = ((slot_down == slot_across) & (down < end) & (across < end)) | (down == across)
    mark = (asked == across[:, :HD]).astype(F32).astype(BF16)
    same = lambda other: lax.dot_general(
        mark, other[:, 2 * columns :], NT, preferred_element_type=F32
    ) > 0.5
    masks = [local, same(near) & (across != here + slot_down), same(far)]
    scale = 1.0 / math.sqrt(HD)
    heads = []
    for head in range(columns // HD):
        lanes = slice(head * HD, (head + 1) * HD)
        value_lanes = slice(columns + head * HD, columns + (head + 1) * HD)
        swapped = columns - HD * (1 + head)
        far_lanes = slice(swapped, swapped + HD)
        far_value_lanes = slice(columns + swapped, columns + swapped + HD)
        query = queries[:, lanes]
        scores = [
            jnp.where(
                mask,
                lax.dot_general(query, key, NT, preferred_element_type=F32) * scale,
                NEGATIVE,
            )
            for mask, key in zip(masks, (keys[:, lanes], near[:, lanes], far[:, far_lanes]))
        ]
        peak = jnp.maximum(jnp.maximum(scores[0], scores[1]), scores[2])
        peak = jnp.max(peak, axis=1, keepdims=True)
        raised = [jnp.exp(score - peak) for score in scores]
        bottom = jnp.sum(raised[0] + raised[1] + raised[2], axis=1, keepdims=True)
        top = jnp.zeros((rows, HD), F32)
        for part, value in zip(
            raised, (values[:, lanes], near[:, value_lanes], far[:, far_value_lanes])
        ):
            top = top + jnp.dot(part.astype(BF16), value, preferred_element_type=F32)
        heads.append(jnp.where(down[:, :HD] < end[:, :HD], top / bottom, 0.0).astype(BF16))
    first = lax.rem(lax.axis_index("cand"), 2) == 0
    by_core = [jnp.where(first, heads[core], heads[1 - core]) for core in range(2)]
    share = out.shape[1]
    for place in range(out.shape[0] // 2):
        for core in range(2):
            out[2 * place + core] = by_core[core][place * share : (place + 1) * share]


def attend(queries, keys, values, near, far, facts):
    vmem = pl.BlockSpec(memory_space=pltpu.VMEM)
    return pl.pallas_call(
        attend_kernel,
        out_shape=jax.ShapeDtypeStruct((8, queries.shape[0] // 4, HD), BF16),
        in_specs=[vmem] * 6,
        out_specs=vmem,
        compiler_params=pltpu.CompilerParams(vmem_limit_bytes=VMEM_LIMIT),
    )(queries, keys, values, near, far, facts)


def mix_kernel(place, attended, weights, mine, other):
    along_z, group, _, cores, depth, _ = weights.shape
    share = attended.shape[1]
    core = lax.rem(lax.axis_index("cand"), 2)
    rows = jnp.concatenate(
        [
            jnp.concatenate([attended[2 * member + owner] for member in range(group)], axis=1)
            for owner in (core, 1 - core)
        ],
        axis=0,
    )
    width = cores * depth
    for z in range(0, along_z, 2):
        block = jnp.concatenate(
            [
                jnp.concatenate(
                    [weights[z + i, place[member], 0].reshape(width, HD) for i in range(2)], axis=0
                )
                for member in range(group)
            ],
            axis=1,
        )
        done = lax.dot_general(rows, block, NT, preferred_element_type=F32).astype(BF16)
        lanes = slice(z * width, (z + 2) * width)
        mine[:, lanes] = done[:share]
        other[:, lanes] = done[share:]


def mix(place, attended, weights):
    along_z, group, along_x, cores, depth, _ = weights.shape
    share, width = attended.shape[1], along_z * cores * depth
    shape = jax.ShapeDtypeStruct((share, along_x * width), BF16)
    out = pl.BlockSpec((share, width), lambda i, place: (0, i))
    return pl.pallas_call(
        mix_kernel,
        out_shape=(shape, shape),
        grid_spec=pltpu.PrefetchScalarGridSpec(
            num_scalar_prefetch=1,
            grid=(along_x,),
            in_specs=[
                pl.BlockSpec(attended.shape, lambda i, place: (0, 0, 0)),
                pl.BlockSpec(
                    (along_z, group, 1, cores, depth, HD), lambda i, place: (0, 0, i, 0, 0, 0)
                ),
            ],
            out_specs=(out, out),
        ),
        compiler_params=pltpu.CompilerParams(vmem_limit_bytes=VMEM_LIMIT),
    )(place, attended, weights)


def fold_kernel(mine, theirs, residual, kept, sent):
    half = kept.shape[0]
    odd = lax.rem(lax.axis_index("mp"), 2)
    own = pl.ds(pl.multiple_of(odd * half, half), half)
    away = pl.ds(pl.multiple_of((1 - odd) * half, half), half)
    kept[...] = residual[...].astype(F32) + mine[own, :].astype(F32) + theirs[own, :].astype(F32)
    sent[...] = (mine[away, :].astype(F32) + theirs[away, :].astype(F32)).astype(BF16)


def fold(mine, theirs, residual):
    vmem = pl.BlockSpec(memory_space=pltpu.VMEM)
    return pl.pallas_call(
        fold_kernel,
        out_shape=(
            jax.ShapeDtypeStruct(residual.shape, F32),
            jax.ShapeDtypeStruct(residual.shape, BF16),
        ),
        in_specs=[vmem] * 3,
        out_specs=(vmem, vmem),
        compiler_params=pltpu.CompilerParams(vmem_limit_bytes=VMEM_LIMIT),
    )(mine, theirs, residual)


def shards(passages, norm_gain, w_qkv, w_out, counts, owners, query_of):
    devices = lax.axis_size("cand")
    parts = lax.axis_size("mp")
    me = lax.axis_index("mp")
    core = lax.rem(lax.axis_index("cand"), 2)
    along_x = devices // (2 * ALONG_Z)
    with jax.named_scope("weights_gathered"):
        copies = copies_by_head(w_qkv, w_out.T, 2 * along_x)
        from_x = lax.all_to_all(
            copies.reshape(-1, HD), "cand", 0, 0, tiled=True, axis_index_groups=x_groups()
        ).reshape(along_x, 2, -1, HD)
        split = w_qkv.shape[0] * w_qkv.shape[1]
        along_z = lambda shard: lax.all_gather(shard, "cand", axis_index_groups=z_groups())
        weights = along_z(from_x[:, :, :split])
        shared = [from_x[:, :, split:]]
    with jax.named_scope("passages_handed_over"):
        inner, outer, kept = pick(jnp.stack([owners, counts, query_of]), passages)
        from_x, inner, outer = lax.optimization_barrier((from_x, inner, outer))
        inner, outer = to_sibling(inner), to_outer(outer)
    with jax.named_scope("weights_shared"):
        shared += [opposed(shared[0], 2), opposed(shared[0], -2), opposed(shared[0], 4)]
        inner, outer, *shared = lax.optimization_barrier((inner, outer, *shared))
        mix_weights = along_z(jnp.stack(shared))
    with jax.named_scope("passages_packed"):
        packed, facts = pack(inner, kept, outer)
    with jax.named_scope("features_gathered"):
        half = packed.shape[0] // 2
        third, fourth = opposed(packed, 2), opposed(packed, -2)
        first, second = opposed(packed, 1), opposed(packed, -1)
        first, second, third, fourth = lax.optimization_barrier((first, second, third, fourth))
        fifth, sixth = opposed(third, 1), opposed(fourth, -1)
        last = (opposed(third[:half], 2), opposed(fourth[half:], -2))
        pieces = [packed, first, second, third, fourth, fifth, sixth, *last]
    away = jnp.array([0, -1, 1, -2, 2, -3, 3, 4, 0], jnp.int32)
    place = lax.rem(me + parts + away * (1 - 2 * core), parts).astype(jnp.int32)
    normed, residual = norm(place, pieces, norm_gain.reshape(parts, 1, -1))
    with jax.named_scope("weights_swapped"):
        weights, _ = lax.optimization_barrier((weights, third))
        sibling_weights = to_sibling(weights)
    queries, keys, values, sent = project(normed, weights, sibling_weights, facts, devices // 2)
    with jax.named_scope("interaction_gathered"):
        near = lax.all_to_all(
            sent, "cand", 0, 0, tiled=True, axis_index_groups=same_core_groups()
        )
        far = to_sibling(near)
    attended = attend(queries, keys, values, near, far, facts)
    with jax.named_scope("heads_exchanged"):
        attended = lax.all_to_all(
            attended, ("cand", "mp"), 0, 0, tiled=True, axis_index_groups=quarter_groups()
        )
    apart = lax.rem((2 * jnp.arange(parts // 2) + lax.rem(me, 2) - me) * (1 - 2 * core) + parts, parts)
    where_shared = jnp.where(apart == 0, 0, jnp.where(apart == 6, 1, 1 + apart // 2))
    mine, other = mix(where_shared.astype(jnp.int32), attended, mix_weights)
    with jax.named_scope("heads_summed"):
        total, leaving = fold(mine, to_sibling(other), residual)
        pairs = [(part, part ^ 1) for part in range(parts)]
        return (total + lax.ppermute(leaving, "mp", pairs).astype(F32)).astype(BF16)


def solution(mesh):
    in_specs = (
        P("cand", None, "mp"),
        P(),
        P(None, "cand", "mp"),
        P("mp", "cand"),
        P("cand"),
        P("cand"),
        P("cand"),
    )
    out_specs = P(("cand", "mp"), None)
    return jax.shard_map(shards, mesh=mesh, in_specs=in_specs, out_specs=out_specs, check_vma=False)
```

```python
import math

import jax
import jax.numpy as jnp
from jax import lax
from jax.experimental import pallas as pl
from jax.experimental.pallas import tpu as pltpu
from jax.sharding import PartitionSpec as P

HD = 128
EPS = 1e-05
NEGATIVE = -1e30
VMEM_LIMIT = 48 * 1024 * 1024
F32 = jnp.float32
BF16 = jnp.bfloat16
NT = (((1,), (1,)), ((), ()))


def along(shard, axis, by):
    length = lax.axis_size(axis)
    return lax.ppermute(shard, axis, [(i, (i + by) % length) for i in range(length)])


def to_sibling(shard):
    length = lax.axis_size("cand")
    return lax.ppermute(shard, "cand", [(i, i ^ 1) for i in range(length)])


def same_core_groups():
    length = lax.axis_size("cand")
    return [list(range(core, length, 2)) for core in range(2)]


ALONG_Z = 8


def x_groups():
    length = lax.axis_size("cand")
    step = 2 * ALONG_Z
    return [
        [x + 2 * z + core for x in range(0, length, step) for core in range(2)]
        for z in range(ALONG_Z)
    ]


def z_groups():
    length = lax.axis_size("cand")
    step = 2 * ALONG_Z
    return [
        [x + 2 * z + core for z in range(ALONG_Z)]
        for x in range(0, length, step)
        for core in range(2)
    ]


def to_outer(shard):
    length = lax.axis_size("cand")
    pairs = [(i, (i + (1 if i % 2 else length - 1)) % length) for i in range(length)]
    return lax.ppermute(shard, "cand", pairs)


def opposed(shard, by):
    chips, parts = lax.axis_size("cand"), lax.axis_size("mp")
    pairs = []
    for device in range(chips):
        signed = by if device % 2 == 0 else -by
        for part in range(parts):
            pairs.append((device * parts + part, device * parts + (part + signed) % parts))
    return lax.ppermute(shard, ("cand", "mp"), pairs)


def pick_kernel(table, passages, inner, outer, kept):
    me = lax.axis_index("cand")
    devices = lax.axis_size("cand")
    slots, length, width = passages.shape
    row = lax.broadcasted_iota(jnp.int32, (16, width), 0)
    lane = lax.broadcasted_iota(jnp.int32, (16, width), 1)
    number = [jnp.int32(0)] * 3
    core = lax.rem(me, 2)
    inward = jnp.where(core == 0, 1, devices - 1)
    outward = jnp.where(core == 0, devices - 1, 1)
    for slot in range(slots):
        ahead = lax.rem(table[0, slot] - me + devices, devices)
        facts = jnp.where(lane < width // 2, table[1, slot], table[2, slot]).astype(F32)
        tail = passages[slot, length - 16 :, :].astype(F32)
        tail = jnp.where(row == 15, facts, tail).astype(BF16)
        for which, (wanted, target) in enumerate(((inward, inner), (outward, outer), (0, kept))):
            hit = ahead == wanted
            place = jnp.minimum(number[which], target.shape[0] - 1)

            @pl.when(hit)
            def _():
                target[place, : length - 16, :] = passages[slot, : length - 16, :]
                target[place, length - 16 :, :] = tail

            number[which] = number[which] + hit.astype(jnp.int32)


def pick(table, passages):
    slots, length, width = passages.shape
    smem = pl.BlockSpec(memory_space=pltpu.SMEM)
    vmem = pl.BlockSpec(memory_space=pltpu.VMEM)
    shape = lambda n: jax.ShapeDtypeStruct((n, length, width), BF16)
    return pl.pallas_call(
        pick_kernel,
        out_shape=(shape(2), shape(2), shape(slots - 4)),
        in_specs=[smem, vmem],
        out_specs=(vmem, vmem, vmem),
        compiler_params=pltpu.CompilerParams(vmem_limit_bytes=VMEM_LIMIT),
    )(table, passages)


def copy_kernel(w_qkv, w_out, copies):
    depth = w_qkv.shape[1]
    for copy in range(copies.shape[0]):
        lanes = slice(copy % 2 * HD, (copy % 2 + 1) * HD)
        for part in range(3):
            copies[copy, part * depth : (part + 1) * depth, :] = w_qkv[part, :, lanes]
        for head in range(2):
            there = slice((3 + head) * depth, (4 + head) * depth)
            copies[copy, there, :] = w_out[:, head * HD : (head + 1) * HD]


def copies_by_head(w_qkv, w_out, number):
    vmem = pl.BlockSpec(memory_space=pltpu.VMEM)
    depth = 3 * w_qkv.shape[1] + 2 * w_out.shape[0]
    return pl.pallas_call(
        copy_kernel,
        out_shape=jax.ShapeDtypeStruct((number, depth, HD), BF16),
        in_specs=[vmem, vmem],
        out_specs=vmem,
        compiler_params=pltpu.CompilerParams(vmem_limit_bytes=VMEM_LIMIT),
    )(w_qkv, w_out)


def pack_kernel(inner, kept, outer, packed, facts):
    rows = packed.shape[0]
    length = kept.shape[1]
    first = lax.rem(lax.axis_index("cand"), 2) == 0
    blocks = (
        [jnp.where(first, outer[i], inner[i]) for i in range(outer.shape[0])]
        + [kept[i] for i in range(kept.shape[0])]
        + [jnp.where(first, inner[i], outer[i]) for i in range(inner.shape[0])]
    )
    position = lax.broadcasted_iota(jnp.int32, (rows, length), 0)
    offset = lax.broadcasted_iota(jnp.int32, (rows, length), 1)
    start = jnp.zeros((1, length), jnp.int32)
    total = jnp.zeros(packed.shape, F32)
    for slot, block in enumerate(blocks):
        fact = block[length - 16 :, :].astype(F32)[15:16, :]
        facts[slot : slot + 1, :] = fact
        count = fact[:, :length].astype(jnp.int32)
        chosen = (position == start + offset) & (offset < count)
        total = total + jnp.dot(
            chosen.astype(F32).astype(BF16), block, preferred_element_type=F32
        )
        start = start + count
    packed[...] = total.astype(BF16)


def pack(inner, kept, outer):
    slots = inner.shape[0] + kept.shape[0] + outer.shape[0]
    length, width = kept.shape[1:]
    vmem = pl.BlockSpec(memory_space=pltpu.VMEM)
    return pl.pallas_call(
        pack_kernel,
        out_shape=(
            jax.ShapeDtypeStruct((slots * length // 2, width), BF16),
            jax.ShapeDtypeStruct((slots, width), F32),
        ),
        in_specs=[vmem] * 3,
        out_specs=(vmem, vmem),
        compiler_params=pltpu.CompilerParams(vmem_limit_bytes=VMEM_LIMIT),
    )(inner, kept, outer)


def norm_kernel(place, *refs):
    pieces, (gain, normed, residual, rows_in) = refs[:9], refs[9:]
    rows, width = pieces[0].shape
    parts = rows_in.shape[0]
    half = rows // 2
    share = residual.shape[0]
    row = pl.multiple_of(place[8] * share, share)
    square = jnp.zeros((rows, HD), F32)
    for number in range(8):
        if number < 7:
            block = pieces[number][...]
        else:
            block = jnp.concatenate([pieces[7][...], pieces[8][...]], axis=0)
        rows_in[place[number]] = block
        x = block.astype(F32)
        x = x * x
        for lane in range(0, width, HD):
            square = square + x[:, lane : lane + HD]
    inverse = lax.rsqrt(jnp.sum(square, axis=1, keepdims=True) / (parts * width) + EPS)
    for part in range(parts):
        lanes = slice(part * width, (part + 1) * width)
        x = rows_in[part].astype(F32)
        normed[:, lanes] = (x * inverse * gain[part]).astype(BF16)
        residual[:, lanes] = rows_in[part, pl.ds(row, share), :]


def norm(place, pieces, gain):
    rows, width = pieces[0].shape
    smem = pl.BlockSpec(memory_space=pltpu.SMEM)
    vmem = pl.BlockSpec(memory_space=pltpu.VMEM)
    return pl.pallas_call(
        norm_kernel,
        out_shape=(
            jax.ShapeDtypeStruct((rows, 8 * width), BF16),
            jax.ShapeDtypeStruct((rows // 8, 8 * width), BF16),
        ),
        in_specs=[smem] + [vmem] * 10,
        out_specs=(vmem, vmem),
        scratch_shapes=[pltpu.VMEM((8, rows, width), BF16)],
        compiler_params=pltpu.CompilerParams(vmem_limit_bytes=VMEM_LIMIT),
    )(place, *pieces, gain)


def project_kernel(x, own_weights, sibling_weights, facts, queries, keys, values, sent, total):
    step = pl.program_id(0)
    rows = x.shape[0]
    columns = 2 * HD
    depth = own_weights.shape[3] // 3
    block = jnp.concatenate(
        [
            source[:, 0, :, part * depth : (part + 1) * depth, :].reshape(-1, HD)
            for part in range(3)
            for source in (own_weights, sibling_weights)
        ],
        axis=1,
    )
    product = jnp.dot(x[...], block, preferred_element_type=F32)

    @pl.when(step == 0)
    def _():
        total[...] = product

    @pl.when(step > 0)
    def _():
        total[...] += product

    @pl.when(step == pl.num_programs(0) - 1)
    def _():
        done = [
            total[:, part * columns : (part + 1) * columns].astype(BF16) for part in range(3)
        ]
        queries[...], keys[...], values[...] = done
        slots = facts.shape[0]
        half = facts.shape[1] // 2
        slot_of = lax.broadcasted_iota(jnp.int32, (2 * slots, rows), 0) % slots
        position = lax.broadcasted_iota(jnp.int32, (2 * slots, rows), 1)
        start = jnp.zeros((1, rows), jnp.int32)
        first = jnp.zeros((2 * slots, rows), jnp.int32)
        asked = jnp.zeros((2 * slots, HD), jnp.int32)
        for slot in range(slots):
            here = slot_of == slot
            first = jnp.where(here, start, first)
            asked = jnp.where(
                here[:, :HD], facts[slot : slot + 1, half : half + HD].astype(jnp.int32), asked
            )
            start = start + facts[slot : slot + 1, :rows].astype(jnp.int32)
        chosen = (first == position).astype(F32).astype(BF16)
        mark = (asked == position[:, :HD]).astype(F32).astype(BF16)
        key_rows = jnp.dot(chosen, done[1], preferred_element_type=F32).astype(BF16)
        value_rows = jnp.dot(chosen, done[2], preferred_element_type=F32).astype(BF16)
        for copy in range(sent.shape[0] // (2 * slots)):
            there = slice(copy * 2 * slots, (copy + 1) * 2 * slots)
            sent[there, :columns] = key_rows
            sent[there, columns : 2 * columns] = value_rows
            sent[there, 2 * columns :] = mark


def project(normed, own_weights, sibling_weights, facts, copies):
    rows, features = normed.shape
    along_z, along_x, cores = own_weights.shape[:3]
    columns = 2 * HD
    out = lambda *shape: (
        jax.ShapeDtypeStruct(shape, BF16),
        pl.BlockSpec(shape, lambda i: (0, 0)),
    )
    outs = [out(rows, columns)] * 3 + [out(copies * facts.shape[0], 2 * columns + HD)]
    weight = pl.BlockSpec((along_z, 1, cores, 192, HD), lambda i: (0, i, 0, 0, 0))
    return pl.pallas_call(
        project_kernel,
        out_shape=tuple(o[0] for o in outs),
        grid=(along_x,),
        in_specs=[
            pl.BlockSpec((rows, features // along_x), lambda i: (0, i)),
            weight,
            weight,
            pl.BlockSpec(facts.shape, lambda i: (0, 0)),
        ],
        out_specs=tuple(o[1] for o in outs),
        scratch_shapes=[pltpu.VMEM((rows, 3 * columns), F32)],
        compiler_params=pltpu.CompilerParams(vmem_limit_bytes=VMEM_LIMIT),
    )(normed, own_weights, sibling_weights, facts)


def attend_kernel(queries, keys, values, near, far, facts, out):
    rows, columns = queries.shape
    slots = facts.shape[0]
    half = facts.shape[1] // 2
    here = lax.axis_index("cand") // 2 * slots
    down = lax.broadcasted_iota(jnp.int32, (rows, rows), 0)
    across = lax.broadcasted_iota(jnp.int32, (rows, rows), 1)
    slot_down = jnp.zeros((rows, rows), jnp.int32)
    slot_across = jnp.zeros((rows, rows), jnp.int32)
    end = jnp.zeros((1, rows), jnp.int32)
    for slot in range(slots):
        end = end + facts[slot : slot + 1, :rows].astype(jnp.int32)
        if slot < slots - 1:
            slot_down = slot_down + (down >= end).astype(jnp.int32)
            slot_across = slot_across + (across >= end).astype(jnp.int32)
    asked = jnp.zeros((rows, HD), jnp.int32)
    for slot in range(slots):
        asked = jnp.where(
            slot_down[:, :HD] == slot,
            facts[slot : slot + 1, half : half + HD].astype(jnp.int32),
            asked,
        )
    local = ((slot_down == slot_across) & (down < end) & (across < end)) | (down == across)
    mark = (asked == across[:, :HD]).astype(F32).astype(BF16)
    same = lambda other: lax.dot_general(
        mark, other[:, 2 * columns :], NT, preferred_element_type=F32
    ) > 0.5
    masks = [local, same(near) & (across != here + slot_down), same(far)]
    scale = 1.0 / math.sqrt(HD)
    heads = []
    for head in range(columns // HD):
        lanes = slice(head * HD, (head + 1) * HD)
        value_lanes = slice(columns + head * HD, columns + (head + 1) * HD)
        swapped = columns - HD * (1 + head)
        far_lanes = slice(swapped, swapped + HD)
        far_value_lanes = slice(columns + swapped, columns + swapped + HD)
        query = queries[:, lanes]
        scores = [
            jnp.where(
                mask,
                lax.dot_general(query, key, NT, preferred_element_type=F32) * scale,
                NEGATIVE,
            )
            for mask, key in zip(masks, (keys[:, lanes], near[:, lanes], far[:, far_lanes]))
        ]
        peak = jnp.maximum(jnp.maximum(scores[0], scores[1]), scores[2])
        peak = jnp.max(peak, axis=1, keepdims=True)
        raised = [jnp.exp(score - peak) for score in scores]
        bottom = jnp.sum(raised[0] + raised[1] + raised[2], axis=1, keepdims=True)
        top = jnp.zeros((rows, HD), F32)
        for part, value in zip(
            raised, (values[:, lanes], near[:, value_lanes], far[:, far_value_lanes])
        ):
            top = top + jnp.dot(part.astype(BF16), value, preferred_element_type=F32)
        heads.append(jnp.where(down[:, :HD] < end[:, :HD], top / bottom, 0.0).astype(BF16))
    first = lax.rem(lax.axis_index("cand"), 2) == 0
    for head in range(2):
        out[:, head * HD : (head + 1) * HD] = jnp.where(first, heads[head], heads[1 - head])


def attend(queries, keys, values, near, far, facts):
    vmem = pl.BlockSpec(memory_space=pltpu.VMEM)
    return pl.pallas_call(
        attend_kernel,
        out_shape=jax.ShapeDtypeStruct(queries.shape, BF16),
        in_specs=[vmem] * 6,
        out_specs=vmem,
        compiler_params=pltpu.CompilerParams(vmem_limit_bytes=VMEM_LIMIT),
    )(queries, keys, values, near, far, facts)


def mix_kernel(attended, weights, out):
    along_z, along_x, cores, depth, _ = weights.shape
    depth = depth // 2
    width = cores * depth
    for x in range(along_x):
        for z in range(0, along_z, 2):
            block = jnp.concatenate(
                [
                    weights[z : z + 2, x, :, head * depth : (head + 1) * depth].reshape(-1, HD)
                    for head in range(2)
                ],
                axis=1,
            )
            at = (x * along_z + z) * width
            out[:, at : at + 2 * width] = lax.dot_general(
                attended[...], block, NT, preferred_element_type=F32
            ).astype(BF16)


def mix(attended, weights):
    along_z, along_x, cores, depth, _ = weights.shape
    whole = lambda array: pl.BlockSpec(array.shape, lambda i: (0,) * array.ndim)
    shape = (attended.shape[0], along_z * along_x * cores * depth // 2)
    return pl.pallas_call(
        mix_kernel,
        out_shape=jax.ShapeDtypeStruct(shape, BF16),
        grid=(1,),
        in_specs=[whole(attended), whole(weights)],
        out_specs=pl.BlockSpec(shape, lambda i: (0, 0)),
        compiler_params=pltpu.CompilerParams(vmem_limit_bytes=VMEM_LIMIT),
    )(attended, weights)


def shards(passages, norm_gain, w_qkv, w_out, counts, owners, query_of):
    devices = lax.axis_size("cand")
    parts = lax.axis_size("mp")
    me = lax.axis_index("mp")
    core = lax.rem(lax.axis_index("cand"), 2)
    along_x = devices // (2 * ALONG_Z)
    with jax.named_scope("passages_handed_over"):
        inner, outer, kept = pick(jnp.stack([owners, counts, query_of]), passages)
        inner, outer = to_sibling(inner), to_outer(outer)
    with jax.named_scope("weights_gathered"):
        copies = copies_by_head(w_qkv, w_out.T, 2 * along_x)
        copies, inner = lax.optimization_barrier((copies, inner))
        from_x = lax.all_to_all(
            copies.reshape(-1, HD), "cand", 0, 0, tiled=True, axis_index_groups=x_groups()
        ).reshape(along_x, 2, -1, HD)
        from_x, outer = lax.optimization_barrier((from_x, outer))
        split = w_qkv.shape[0] * w_qkv.shape[1]
        along_z = lambda shard: lax.all_gather(shard, "cand", axis_index_groups=z_groups())
        weights = along_z(from_x[:, :, :split])
        mix_weights = along_z(from_x[:, :, split:])
    with jax.named_scope("passages_packed"):
        packed, facts = pack(inner, kept, outer)
    with jax.named_scope("features_gathered"):
        half = packed.shape[0] // 2
        third, fourth = opposed(packed, 2), opposed(packed, -2)
        first, second = opposed(packed, 1), opposed(packed, -1)
        first, second, third, fourth = lax.optimization_barrier((first, second, third, fourth))
        fifth, sixth = opposed(third, 1), opposed(fourth, -1)
        last = (opposed(third[:half], 2), opposed(fourth[half:], -2))
        pieces = [packed, first, second, third, fourth, fifth, sixth, *last]
    away = jnp.array([0, -1, 1, -2, 2, -3, 3, 4, 0], jnp.int32)
    place = lax.rem(me + parts + away * (1 - 2 * core), parts).astype(jnp.int32)
    normed, residual = norm(place, pieces, norm_gain.reshape(parts, 1, -1))
    with jax.named_scope("weights_swapped"):
        weights, *_ = lax.optimization_barrier((weights, fifth, sixth, *last))
        sibling_weights = to_sibling(weights)
    queries, keys, values, sent = project(normed, weights, sibling_weights, facts, devices // 2)
    with jax.named_scope("interaction_gathered"):
        near = lax.all_to_all(
            sent, "cand", 0, 0, tiled=True, axis_index_groups=same_core_groups()
        )
        far = to_sibling(near)
    own = attend(queries, keys, values, near, far, facts)
    partial = mix(own, mix_weights)
    with jax.named_scope("heads_summed"):
        summed = lax.psum_scatter(partial, "mp", scatter_dimension=0, tiled=True)
    return (residual.astype(F32) + summed.astype(F32)).astype(BF16)


def solution(mesh):
    in_specs = (
        P("cand", None, "mp"),
        P(),
        P(None, "cand", "mp"),
        P("mp", "cand"),
        P("cand"),
        P("cand"),
        P("cand"),
    )
    out_specs = P(("cand", "mp"), None)
    return jax.shard_map(shards, mesh=mesh, in_specs=in_specs, out_specs=out_specs, check_vma=False)
```

```python
import math

import jax
import jax.numpy as jnp
from jax import lax
from jax.experimental import pallas as pl
from jax.experimental.pallas import tpu as pltpu
from jax.sharding import PartitionSpec as P

HD = 128
EPS = 1e-05
NEGATIVE = -1e30
VMEM_LIMIT = 48 * 1024 * 1024
F32 = jnp.float32
BF16 = jnp.bfloat16
NT = (((1,), (1,)), ((), ()))


def along(shard, axis, by):
    length = lax.axis_size(axis)
    return lax.ppermute(shard, axis, [(i, (i + by) % length) for i in range(length)])


def to_sibling(shard):
    length = lax.axis_size("cand")
    return lax.ppermute(shard, "cand", [(i, i ^ 1) for i in range(length)])


def same_core_groups():
    length = lax.axis_size("cand")
    return [list(range(core, length, 2)) for core in range(2)]


ALONG_Z = 8


def x_groups():
    length = lax.axis_size("cand")
    step = 2 * ALONG_Z
    return [
        [x + 2 * z + core for x in range(0, length, step) for core in range(2)]
        for z in range(ALONG_Z)
    ]


def z_groups():
    length = lax.axis_size("cand")
    step = 2 * ALONG_Z
    return [
        [x + 2 * z + core for z in range(ALONG_Z)]
        for x in range(0, length, step)
        for core in range(2)
    ]


def to_outer(shard):
    length = lax.axis_size("cand")
    pairs = [(i, (i + (1 if i % 2 else length - 1)) % length) for i in range(length)]
    return lax.ppermute(shard, "cand", pairs)


def opposed(shard, by):
    chips, parts = lax.axis_size("cand"), lax.axis_size("mp")
    pairs = []
    for device in range(chips):
        signed = by if device % 2 == 0 else -by
        for part in range(parts):
            pairs.append((device * parts + part, device * parts + (part + signed) % parts))
    return lax.ppermute(shard, ("cand", "mp"), pairs)


def pick_kernel(table, passages, inner, outer, kept):
    me = lax.axis_index("cand")
    devices = lax.axis_size("cand")
    slots, length, width = passages.shape
    row = lax.broadcasted_iota(jnp.int32, (16, width), 0)
    lane = lax.broadcasted_iota(jnp.int32, (16, width), 1)
    number = [jnp.int32(0)] * 3
    core = lax.rem(me, 2)
    inward = jnp.where(core == 0, 1, devices - 1)
    outward = jnp.where(core == 0, devices - 1, 1)
    for slot in range(slots):
        ahead = lax.rem(table[0, slot] - me + devices, devices)
        facts = jnp.where(lane < width // 2, table[1, slot], table[2, slot]).astype(F32)
        tail = passages[slot, length - 16 :, :].astype(F32)
        tail = jnp.where(row == 15, facts, tail).astype(BF16)
        for which, (wanted, target) in enumerate(((inward, inner), (outward, outer), (0, kept))):
            hit = ahead == wanted
            place = jnp.minimum(number[which], target.shape[0] - 1)

            @pl.when(hit)
            def _():
                target[place, : length - 16, :] = passages[slot, : length - 16, :]
                target[place, length - 16 :, :] = tail

            number[which] = number[which] + hit.astype(jnp.int32)


def pick(table, passages):
    slots, length, width = passages.shape
    smem = pl.BlockSpec(memory_space=pltpu.SMEM)
    vmem = pl.BlockSpec(memory_space=pltpu.VMEM)
    shape = lambda n: jax.ShapeDtypeStruct((n, length, width), BF16)
    return pl.pallas_call(
        pick_kernel,
        out_shape=(shape(2), shape(2), shape(slots - 4)),
        in_specs=[smem, vmem],
        out_specs=(vmem, vmem, vmem),
        compiler_params=pltpu.CompilerParams(vmem_limit_bytes=VMEM_LIMIT),
    )(table, passages)


def copy_kernel(w_qkv, w_out, copies):
    depth = w_qkv.shape[1]
    for copy in range(copies.shape[0]):
        lanes = slice(copy % 2 * HD, (copy % 2 + 1) * HD)
        for part in range(3):
            copies[copy, part * depth : (part + 1) * depth, :] = w_qkv[part, :, lanes]
        copies[copy, 3 * depth :, :] = w_out[:, lanes]


def copies_by_head(w_qkv, w_out, number):
    vmem = pl.BlockSpec(memory_space=pltpu.VMEM)
    depth = 3 * w_qkv.shape[1] + w_out.shape[0]
    return pl.pallas_call(
        copy_kernel,
        out_shape=jax.ShapeDtypeStruct((number, depth, HD), BF16),
        in_specs=[vmem, vmem],
        out_specs=vmem,
        compiler_params=pltpu.CompilerParams(vmem_limit_bytes=VMEM_LIMIT),
    )(w_qkv, w_out)


def pack_kernel(inner, kept, outer, packed, facts):
    rows = packed.shape[0]
    length = kept.shape[1]
    first = lax.rem(lax.axis_index("cand"), 2) == 0
    blocks = (
        [jnp.where(first, outer[i], inner[i]) for i in range(outer.shape[0])]
        + [kept[i] for i in range(kept.shape[0])]
        + [jnp.where(first, inner[i], outer[i]) for i in range(inner.shape[0])]
    )
    position = lax.broadcasted_iota(jnp.int32, (rows, length), 0)
    offset = lax.broadcasted_iota(jnp.int32, (rows, length), 1)
    start = jnp.zeros((1, length), jnp.int32)
    total = jnp.zeros(packed.shape, F32)
    for slot, block in enumerate(blocks):
        fact = block[length - 16 :, :].astype(F32)[15:16, :]
        facts[slot : slot + 1, :] = fact
        count = fact[:, :length].astype(jnp.int32)
        chosen = (position == start + offset) & (offset < count)
        total = total + jnp.dot(
            chosen.astype(F32).astype(BF16), block, preferred_element_type=F32
        )
        start = start + count
    packed[...] = total.astype(BF16)


def pack(inner, kept, outer):
    slots = inner.shape[0] + kept.shape[0] + outer.shape[0]
    length, width = kept.shape[1:]
    vmem = pl.BlockSpec(memory_space=pltpu.VMEM)
    return pl.pallas_call(
        pack_kernel,
        out_shape=(
            jax.ShapeDtypeStruct((slots * length // 2, width), BF16),
            jax.ShapeDtypeStruct((slots, width), F32),
        ),
        in_specs=[vmem] * 3,
        out_specs=(vmem, vmem),
        compiler_params=pltpu.CompilerParams(vmem_limit_bytes=VMEM_LIMIT),
    )(inner, kept, outer)


def first_rows(facts, rows):
    slots = facts.shape[0]
    slot_of = lax.broadcasted_iota(jnp.int32, (2 * slots, rows), 0) % slots
    position = lax.broadcasted_iota(jnp.int32, (2 * slots, rows), 1)
    start = jnp.zeros((1, rows), jnp.int32)
    first = jnp.zeros((2 * slots, rows), jnp.int32)
    for slot in range(slots):
        first = jnp.where(slot_of == slot, start, first)
        start = start + facts[slot : slot + 1, :rows].astype(jnp.int32)
    return (first == position).astype(F32).astype(BF16)


def norm_kernel(place, *refs):
    pieces, (gain, facts, normed, residual, firsts, rows_in) = refs[:9], refs[9:]
    rows, width = pieces[0].shape
    parts = rows_in.shape[0]
    half = rows // 2
    share = residual.shape[0]
    row = pl.multiple_of(place[8] * share, share)
    square = jnp.zeros((rows, HD), F32)
    for number in range(8):
        if number < 7:
            block = pieces[number][...]
        else:
            block = jnp.concatenate([pieces[7][...], pieces[8][...]], axis=0)
        rows_in[place[number]] = block
        x = block.astype(F32)
        x = x * x
        for lane in range(0, width, HD):
            square = square + x[:, lane : lane + HD]
    chosen = first_rows(facts, rows)
    inverse = lax.rsqrt(jnp.sum(square, axis=1, keepdims=True) / (parts * width) + EPS)
    for part in range(parts):
        lanes = slice(part * width, (part + 1) * width)
        x = rows_in[part].astype(F32)
        x = (x * inverse * gain[part]).astype(BF16)
        normed[:, lanes] = x
        firsts[:, lanes] = jnp.dot(chosen, x, preferred_element_type=F32).astype(BF16)
        residual[:, lanes] = rows_in[part, pl.ds(row, share), :]


def norm(place, pieces, gain, facts):
    rows, width = pieces[0].shape
    smem = pl.BlockSpec(memory_space=pltpu.SMEM)
    vmem = pl.BlockSpec(memory_space=pltpu.VMEM)
    return pl.pallas_call(
        norm_kernel,
        out_shape=(
            jax.ShapeDtypeStruct((rows, 8 * width), BF16),
            jax.ShapeDtypeStruct((rows // 8, 8 * width), BF16),
            jax.ShapeDtypeStruct((16, 8 * width), BF16),
        ),
        in_specs=[smem] + [vmem] * 11,
        out_specs=(vmem, vmem, vmem),
        scratch_shapes=[pltpu.VMEM((8, rows, width), BF16)],
        compiler_params=pltpu.CompilerParams(vmem_limit_bytes=VMEM_LIMIT),
    )(place, *pieces, gain, facts)


def project_kernel(x, weights, queries, keys, values, total):
    step = pl.program_id(0)
    depth = weights.shape[3] // 3
    block = jnp.concatenate(
        [
            weights[:, 0, :, part * depth : (part + 1) * depth, :].reshape(-1, HD)
            for part in range(3)
        ],
        axis=1,
    )
    product = jnp.dot(x[...], block, preferred_element_type=F32)

    @pl.when(step == 0)
    def _():
        total[...] = product

    @pl.when(step > 0)
    def _():
        total[...] += product

    @pl.when(step == pl.num_programs(0) - 1)
    def _():
        for part, out in enumerate((queries, keys, values)):
            out[...] = total[:, part * HD : (part + 1) * HD].astype(BF16)


def project(normed, weights):
    rows, features = normed.shape
    along_z, along_x, cores = weights.shape[:3]
    out = jax.ShapeDtypeStruct((rows, HD), BF16)
    spec = pl.BlockSpec((rows, HD), lambda i: (0, 0))
    return pl.pallas_call(
        project_kernel,
        out_shape=(out, out, out),
        grid=(along_x,),
        in_specs=[
            pl.BlockSpec((rows, features // along_x), lambda i: (0, i)),
            pl.BlockSpec((along_z, 1, cores, 192, HD), lambda i: (0, i, 0, 0, 0)),
        ],
        out_specs=(spec, spec, spec),
        scratch_shapes=[pltpu.VMEM((rows, 3 * HD), F32)],
        compiler_params=pltpu.CompilerParams(vmem_limit_bytes=VMEM_LIMIT),
    )(normed, weights)


def send_kernel(firsts, key_weights, value_weights, keys, values, facts, sent, total):
    step = pl.program_id(0)
    steps = pl.num_programs(0)
    along_z, along_x, cores, depth, _ = key_weights.shape
    product = jnp.zeros(total.shape, F32)
    width = along_z * cores * depth
    for x in range(along_x):
        block = jnp.concatenate(
            [key_weights[:, x].reshape(width, HD), value_weights[:, x].reshape(width, HD)], axis=1
        )
        product = product + jnp.dot(
            firsts[:, x * width : (x + 1) * width], block, preferred_element_type=F32
        )

    @pl.when(step == 0)
    def _():
        total[...] = product

    @pl.when(step == steps - 1)
    def _():
        rows = keys.shape[0]
        slots = facts.shape[0]
        half = facts.shape[1] // 2
        slot_of = lax.broadcasted_iota(jnp.int32, (2 * slots, HD), 0) % slots
        lane = lax.broadcasted_iota(jnp.int32, (2 * slots, HD), 1)
        asked = jnp.zeros((2 * slots, HD), jnp.int32)
        for slot in range(slots):
            here = facts[slot : slot + 1, half : half + HD].astype(jnp.int32)
            asked = jnp.where(slot_of == slot, here, asked)
        mark = (asked == lane).astype(F32).astype(BF16)
        chosen = first_rows(facts, rows)
        theirs = (total[...] + product).astype(BF16)
        own = [
            jnp.dot(chosen, source[...], preferred_element_type=F32).astype(BF16)
            for source in (keys, values)
        ]
        line = jnp.concatenate([own[0], theirs[:, :HD], own[1], theirs[:, HD:], mark], axis=1)
        for copy in range(sent.shape[0] // (2 * slots)):
            sent[copy * 2 * slots : (copy + 1) * 2 * slots, :] = line


def send(firsts, weights, keys, values, facts, copies):
    along_z, along_x, cores, depth, _ = weights.shape
    depth = depth // 4
    whole = lambda array: pl.BlockSpec(array.shape, lambda i: (0, 0))
    weight = lambda part: pl.BlockSpec(
        (along_z, along_x // 2, cores, depth, HD), lambda i: (0, i, 0, part, 0)
    )
    shape = (copies * facts.shape[0], 5 * HD)
    return pl.pallas_call(
        send_kernel,
        out_shape=jax.ShapeDtypeStruct(shape, BF16),
        grid=(2,),
        in_specs=[
            pl.BlockSpec((firsts.shape[0], firsts.shape[1] // 2), lambda i: (0, i)),
            weight(1),
            weight(2),
            whole(keys),
            whole(values),
            whole(facts),
        ],
        out_specs=pl.BlockSpec(shape, lambda i: (0, 0)),
        scratch_shapes=[pltpu.VMEM((16, 2 * HD), F32)],
        compiler_params=pltpu.CompilerParams(vmem_limit_bytes=VMEM_LIMIT),
    )(firsts, weights, weights, keys, values, facts)


def attend_kernel(*refs):
    queries, keys, values = refs[0:6:3], refs[1:6:3], refs[2:6:3]
    near, far, facts, out = refs[6:]
    rows, columns = out.shape
    slots = facts.shape[0]
    half = facts.shape[1] // 2
    here = lax.axis_index("cand") // 2 * slots
    down = lax.broadcasted_iota(jnp.int32, (rows, rows), 0)
    across = lax.broadcasted_iota(jnp.int32, (rows, rows), 1)
    slot_down = jnp.zeros((rows, rows), jnp.int32)
    slot_across = jnp.zeros((rows, rows), jnp.int32)
    end = jnp.zeros((1, rows), jnp.int32)
    for slot in range(slots):
        end = end + facts[slot : slot + 1, :rows].astype(jnp.int32)
        if slot < slots - 1:
            slot_down = slot_down + (down >= end).astype(jnp.int32)
            slot_across = slot_across + (across >= end).astype(jnp.int32)
    asked = jnp.zeros((rows, HD), jnp.int32)
    for slot in range(slots):
        asked = jnp.where(
            slot_down[:, :HD] == slot,
            facts[slot : slot + 1, half : half + HD].astype(jnp.int32),
            asked,
        )
    local = ((slot_down == slot_across) & (down < end) & (across < end)) | (down == across)
    mark = (asked == across[:, :HD]).astype(F32).astype(BF16)
    same = lambda other: lax.dot_general(
        mark, other[:, 2 * columns :], NT, preferred_element_type=F32
    ) > 0.5
    masks = [local, same(near) & (across != here + slot_down), same(far)]
    scale = 1.0 / math.sqrt(HD)
    heads = []
    for head in range(columns // HD):
        lanes = slice(head * HD, (head + 1) * HD)
        value_lanes = slice(columns + head * HD, columns + (head + 1) * HD)
        swapped = columns - HD * (1 + head)
        far_lanes = slice(swapped, swapped + HD)
        far_value_lanes = slice(columns + swapped, columns + swapped + HD)
        query = queries[head][...]
        scores = [
            jnp.where(
                mask,
                lax.dot_general(query, key, NT, preferred_element_type=F32) * scale,
                NEGATIVE,
            )
            for mask, key in zip(masks, (keys[head][...], near[:, lanes], far[:, far_lanes]))
        ]
        peak = jnp.maximum(jnp.maximum(scores[0], scores[1]), scores[2])
        peak = jnp.max(peak, axis=1, keepdims=True)
        raised = [jnp.exp(score - peak) for score in scores]
        bottom = jnp.sum(raised[0] + raised[1] + raised[2], axis=1, keepdims=True)
        top = jnp.zeros((rows, HD), F32)
        for part, value in zip(
            raised, (values[head][...], near[:, value_lanes], far[:, far_value_lanes])
        ):
            top = top + jnp.dot(part.astype(BF16), value, preferred_element_type=F32)
        heads.append(jnp.where(down[:, :HD] < end[:, :HD], top / bottom, 0.0).astype(BF16))
    out[...] = jnp.concatenate(heads, axis=1)


def attend(own, sibling, near, far, facts):
    vmem = pl.BlockSpec(memory_space=pltpu.VMEM)
    rows = own[0].shape[0]
    return pl.pallas_call(
        attend_kernel,
        out_shape=jax.ShapeDtypeStruct((rows, 2 * HD), BF16),
        in_specs=[vmem] * 9,
        out_specs=vmem,
        compiler_params=pltpu.CompilerParams(vmem_limit_bytes=VMEM_LIMIT),
    )(*own, *sibling, near, far, facts)


def mix_kernel(attended, own_weights, sibling_weights, out):
    along_z, _, cores, depth, _ = own_weights.shape
    width = cores * depth
    for z in range(0, along_z, 2):
        block = jnp.concatenate(
            [
                source[z : z + 2].reshape(2 * width, HD)
                for source in (own_weights, sibling_weights)
            ],
            axis=1,
        )
        out[:, z * width : (z + 2) * width] = lax.dot_general(
            attended[...], block, NT, preferred_element_type=F32
        ).astype(BF16)


def mix(attended, own_weights, sibling_weights):
    along_z, along_x, cores, depth, _ = own_weights.shape
    depth = depth // 4
    rows, width = attended.shape[0], along_z * cores * depth
    weight = pl.BlockSpec((along_z, 1, cores, depth, HD), lambda i: (0, i, 0, 3, 0))
    return pl.pallas_call(
        mix_kernel,
        out_shape=jax.ShapeDtypeStruct((rows, along_x * width), BF16),
        grid=(along_x,),
        in_specs=[pl.BlockSpec(attended.shape, lambda i: (0, 0)), weight, weight],
        out_specs=pl.BlockSpec((rows, width), lambda i: (0, i)),
        compiler_params=pltpu.CompilerParams(vmem_limit_bytes=VMEM_LIMIT),
    )(attended, own_weights, sibling_weights)


def shards(passages, norm_gain, w_qkv, w_out, counts, owners, query_of):
    devices = lax.axis_size("cand")
    parts = lax.axis_size("mp")
    me = lax.axis_index("mp")
    core = lax.rem(lax.axis_index("cand"), 2)
    along_x = devices // (2 * ALONG_Z)
    with jax.named_scope("weights_gathered"):
        copies = copies_by_head(w_qkv, w_out.T, 2 * along_x)
        from_x = lax.all_to_all(
            copies.reshape(-1, HD), "cand", 0, 0, tiled=True, axis_index_groups=x_groups()
        ).reshape(along_x, 2, -1, HD)
        weights = lax.all_gather(from_x, "cand", axis_index_groups=z_groups())
    with jax.named_scope("passages_handed_over"):
        inner, outer, kept = pick(jnp.stack([owners, counts, query_of]), passages)
        from_x, inner, outer = lax.optimization_barrier((from_x, inner, outer))
        inner, outer = to_sibling(inner), to_outer(outer)
    with jax.named_scope("passages_packed"):
        packed, facts = pack(inner, kept, outer)
    with jax.named_scope("features_gathered"):
        half = packed.shape[0] // 2
        third, fourth = opposed(packed, 2), opposed(packed, -2)
        first, second = opposed(packed, 1), opposed(packed, -1)
        first, second, third, fourth = lax.optimization_barrier((first, second, third, fourth))
        fifth, sixth = opposed(third, 1), opposed(fourth, -1)
        last = (opposed(third[:half], 2), opposed(fourth[half:], -2))
        pieces = [packed, first, second, third, fourth, fifth, sixth, *last]
    away = jnp.array([0, -1, 1, -2, 2, -3, 3, 4, 0], jnp.int32)
    place = lax.rem(me + parts + away * (1 - 2 * core), parts).astype(jnp.int32)
    normed, residual, firsts = norm(place, pieces, norm_gain.reshape(parts, 1, -1), facts)
    with jax.named_scope("weights_swapped"):
        weights, *_ = lax.optimization_barrier((weights, fifth, sixth, *last))
        sibling_weights = to_sibling(weights)
    own = project(normed, weights)
    sent = send(firsts, sibling_weights, own[1], own[2], facts, devices // 2)
    sibling = project(normed, sibling_weights)
    with jax.named_scope("interaction_gathered"):
        near = lax.all_to_all(
            sent, "cand", 0, 0, tiled=True, axis_index_groups=same_core_groups()
        )
        far = to_sibling(near)
    attended = attend(own, sibling, near, far, facts)
    partial = mix(attended, weights, sibling_weights)
    with jax.named_scope("heads_summed"):
        summed = lax.psum_scatter(partial, "mp", scatter_dimension=0, tiled=True)
    return (residual.astype(F32) + summed.astype(F32)).astype(BF16)


def solution(mesh):
    in_specs = (
        P("cand", None, "mp"),
        P(),
        P(None, "cand", "mp"),
        P("mp", "cand"),
        P("cand"),
        P("cand"),
        P("cand"),
    )
    out_specs = P(("cand", "mp"), None)
    return jax.shard_map(shards, mesh=mesh, in_specs=in_specs, out_specs=out_specs, check_vma=False)
```

```python
import math

import jax
import jax.numpy as jnp
from jax import lax
from jax.experimental import pallas as pl
from jax.experimental.pallas import tpu as pltpu
from jax.sharding import PartitionSpec as P

HD = 128
EPS = 1e-05
NEGATIVE = -1e30
VMEM_LIMIT = 48 * 1024 * 1024
F32 = jnp.float32
BF16 = jnp.bfloat16
NT = (((1,), (1,)), ((), ()))


def along(shard, axis, by):
    length = lax.axis_size(axis)
    return lax.ppermute(shard, axis, [(i, (i + by) % length) for i in range(length)])


def to_sibling(shard):
    length = lax.axis_size("cand")
    return lax.ppermute(shard, "cand", [(i, i ^ 1) for i in range(length)])


def same_core_groups():
    length = lax.axis_size("cand")
    return [list(range(core, length, 2)) for core in range(2)]


ALONG_Z = 8


def x_groups():
    length = lax.axis_size("cand")
    step = 2 * ALONG_Z
    return [
        [x + 2 * z + core for x in range(0, length, step) for core in range(2)]
        for z in range(ALONG_Z)
    ]


def z_groups():
    length = lax.axis_size("cand")
    step = 2 * ALONG_Z
    return [
        [x + 2 * z + core for z in range(ALONG_Z)]
        for x in range(0, length, step)
        for core in range(2)
    ]


def to_outer(shard):
    length = lax.axis_size("cand")
    pairs = [(i, (i + (1 if i % 2 else length - 1)) % length) for i in range(length)]
    return lax.ppermute(shard, "cand", pairs)


def opposed(shard, by):
    chips, parts = lax.axis_size("cand"), lax.axis_size("mp")
    pairs = []
    for device in range(chips):
        signed = by if device % 2 == 0 else -by
        for part in range(parts):
            pairs.append((device * parts + part, device * parts + (part + signed) % parts))
    return lax.ppermute(shard, ("cand", "mp"), pairs)


def pick_kernel(table, passages, inner, outer, kept):
    me = lax.axis_index("cand")
    devices = lax.axis_size("cand")
    slots, length, width = passages.shape
    row = lax.broadcasted_iota(jnp.int32, (16, width), 0)
    lane = lax.broadcasted_iota(jnp.int32, (16, width), 1)
    number = [jnp.int32(0)] * 3
    core = lax.rem(me, 2)
    inward = jnp.where(core == 0, 1, devices - 1)
    outward = jnp.where(core == 0, devices - 1, 1)
    for slot in range(slots):
        ahead = lax.rem(table[0, slot] - me + devices, devices)
        facts = jnp.where(lane < width // 2, table[1, slot], table[2, slot]).astype(F32)
        tail = passages[slot, length - 16 :, :].astype(F32)
        tail = jnp.where(row == 15, facts, tail).astype(BF16)
        for which, (wanted, target) in enumerate(((inward, inner), (outward, outer), (0, kept))):
            hit = ahead == wanted
            place = jnp.minimum(number[which], target.shape[0] - 1)

            @pl.when(hit)
            def _():
                target[place, : length - 16, :] = passages[slot, : length - 16, :]
                target[place, length - 16 :, :] = tail

            number[which] = number[which] + hit.astype(jnp.int32)


def pick(table, passages):
    slots, length, width = passages.shape
    smem = pl.BlockSpec(memory_space=pltpu.SMEM)
    vmem = pl.BlockSpec(memory_space=pltpu.VMEM)
    shape = lambda n: jax.ShapeDtypeStruct((n, length, width), BF16)
    return pl.pallas_call(
        pick_kernel,
        out_shape=(shape(2), shape(2), shape(slots - 4)),
        in_specs=[smem, vmem],
        out_specs=(vmem, vmem, vmem),
        compiler_params=pltpu.CompilerParams(vmem_limit_bytes=VMEM_LIMIT),
    )(table, passages)


def copy_kernel(w_qkv, w_out, copies):
    depth = w_qkv.shape[1]
    for copy in range(copies.shape[0]):
        lanes = slice(copy % 2 * HD, (copy % 2 + 1) * HD)
        for part in range(3):
            copies[copy, part * depth : (part + 1) * depth, :] = w_qkv[part, :, lanes]
        copies[copy, 3 * depth :, :] = w_out[:, lanes]


def copies_by_head(w_qkv, w_out, number):
    vmem = pl.BlockSpec(memory_space=pltpu.VMEM)
    depth = 3 * w_qkv.shape[1] + w_out.shape[0]
    return pl.pallas_call(
        copy_kernel,
        out_shape=jax.ShapeDtypeStruct((number, depth, HD), BF16),
        in_specs=[vmem, vmem],
        out_specs=vmem,
        compiler_params=pltpu.CompilerParams(vmem_limit_bytes=VMEM_LIMIT),
    )(w_qkv, w_out)


def pack_kernel(inner, kept, outer, packed, facts):
    rows = packed.shape[0]
    length = kept.shape[1]
    first = lax.rem(lax.axis_index("cand"), 2) == 0
    blocks = (
        [jnp.where(first, outer[i], inner[i]) for i in range(outer.shape[0])]
        + [kept[i] for i in range(kept.shape[0])]
        + [jnp.where(first, inner[i], outer[i]) for i in range(inner.shape[0])]
    )
    position = lax.broadcasted_iota(jnp.int32, (rows, length), 0)
    offset = lax.broadcasted_iota(jnp.int32, (rows, length), 1)
    start = jnp.zeros((1, length), jnp.int32)
    total = jnp.zeros(packed.shape, F32)
    for slot, block in enumerate(blocks):
        fact = block[length - 16 :, :].astype(F32)[15:16, :]
        facts[slot : slot + 1, :] = fact
        count = fact[:, :length].astype(jnp.int32)
        chosen = (position == start + offset) & (offset < count)
        total = total + jnp.dot(
            chosen.astype(F32).astype(BF16), block, preferred_element_type=F32
        )
        start = start + count
    packed[...] = total.astype(BF16)


def pack(inner, kept, outer):
    slots = inner.shape[0] + kept.shape[0] + outer.shape[0]
    length, width = kept.shape[1:]
    vmem = pl.BlockSpec(memory_space=pltpu.VMEM)
    return pl.pallas_call(
        pack_kernel,
        out_shape=(
            jax.ShapeDtypeStruct((slots * length // 2, width), BF16),
            jax.ShapeDtypeStruct((slots, width), F32),
        ),
        in_specs=[vmem] * 3,
        out_specs=(vmem, vmem),
        compiler_params=pltpu.CompilerParams(vmem_limit_bytes=VMEM_LIMIT),
    )(inner, kept, outer)


def first_rows(facts, rows):
    slots = facts.shape[0]
    slot_of = lax.broadcasted_iota(jnp.int32, (2 * slots, rows), 0) % slots
    position = lax.broadcasted_iota(jnp.int32, (2 * slots, rows), 1)
    start = jnp.zeros((1, rows), jnp.int32)
    first = jnp.zeros((2 * slots, rows), jnp.int32)
    for slot in range(slots):
        first = jnp.where(slot_of == slot, start, first)
        start = start + facts[slot : slot + 1, :rows].astype(jnp.int32)
    return (first == position).astype(F32).astype(BF16)


def norm_kernel(place, *refs):
    pieces, (gain, facts, normed, residual, firsts, rows_in) = refs[:9], refs[9:]
    rows, width = pieces[0].shape
    parts = rows_in.shape[0]
    half = rows // 2
    share = residual.shape[0]
    row = pl.multiple_of(place[8] * share, share)
    square = jnp.zeros((rows, HD), F32)
    for number in range(8):
        if number < 7:
            block = pieces[number][...]
        else:
            block = jnp.concatenate([pieces[7][...], pieces[8][...]], axis=0)
        rows_in[place[number]] = block
        x = block.astype(F32)
        x = x * x
        for lane in range(0, width, HD):
            square = square + x[:, lane : lane + HD]
    chosen = first_rows(facts, rows)
    inverse = lax.rsqrt(jnp.sum(square, axis=1, keepdims=True) / (parts * width) + EPS)
    for part in range(parts):
        lanes = slice(part * width, (part + 1) * width)
        x = rows_in[part].astype(F32)
        x = (x * inverse * gain[part]).astype(BF16)
        normed[:, lanes] = x
        firsts[:, lanes] = jnp.dot(chosen, x, preferred_element_type=F32).astype(BF16)
        residual[:, lanes] = rows_in[part, pl.ds(row, share), :]


def norm(place, pieces, gain, facts):
    rows, width = pieces[0].shape
    smem = pl.BlockSpec(memory_space=pltpu.SMEM)
    vmem = pl.BlockSpec(memory_space=pltpu.VMEM)
    return pl.pallas_call(
        norm_kernel,
        out_shape=(
            jax.ShapeDtypeStruct((rows, 8 * width), BF16),
            jax.ShapeDtypeStruct((rows // 8, 8 * width), BF16),
            jax.ShapeDtypeStruct((16, 8 * width), BF16),
        ),
        in_specs=[smem] + [vmem] * 11,
        out_specs=(vmem, vmem, vmem),
        scratch_shapes=[pltpu.VMEM((8, rows, width), BF16)],
        compiler_params=pltpu.CompilerParams(vmem_limit_bytes=VMEM_LIMIT),
    )(place, *pieces, gain, facts)


def project_kernel(x, weights, queries, keys, values, total):
    step = pl.program_id(0)
    along_z, along_x, cores, depth, _ = weights.shape
    depth = depth // 3
    width = along_z * cores * depth
    product = jnp.zeros(total.shape, F32)
    for place in range(along_x):
        block = jnp.concatenate(
            [
                weights[:, place, :, part * depth : (part + 1) * depth, :].reshape(-1, HD)
                for part in range(3)
            ],
            axis=1,
        )
        product = product + jnp.dot(
            x[:, place * width : (place + 1) * width], block, preferred_element_type=F32
        )

    @pl.when(step == 0)
    def _():
        total[...] = product

    @pl.when(step > 0)
    def _():
        total[...] += product

    @pl.when(step == pl.num_programs(0) - 1)
    def _():
        for part, out in enumerate((queries, keys, values)):
            out[...] = total[:, part * HD : (part + 1) * HD].astype(BF16)


def project(normed, weights):
    rows, features = normed.shape
    along_z, along_x, cores = weights.shape[:3]
    out = jax.ShapeDtypeStruct((rows, HD), BF16)
    spec = pl.BlockSpec((rows, HD), lambda i: (0, 0))
    return pl.pallas_call(
        project_kernel,
        out_shape=(out, out, out),
        grid=(2,),
        in_specs=[
            pl.BlockSpec((rows, features // 2), lambda i: (0, i)),
            pl.BlockSpec((along_z, along_x // 2, cores, 192, HD), lambda i: (0, i, 0, 0, 0)),
        ],
        out_specs=(spec, spec, spec),
        scratch_shapes=[pltpu.VMEM((rows, 3 * HD), F32)],
        compiler_params=pltpu.CompilerParams(vmem_limit_bytes=VMEM_LIMIT),
    )(normed, weights)


def send_kernel(firsts, key_weights, value_weights, keys, values, facts, sent, total):
    step = pl.program_id(0)
    steps = pl.num_programs(0)
    along_z, along_x, cores, depth, _ = key_weights.shape
    product = jnp.zeros(total.shape, F32)
    width = along_z * cores * depth
    for x in range(along_x):
        block = jnp.concatenate(
            [key_weights[:, x].reshape(width, HD), value_weights[:, x].reshape(width, HD)], axis=1
        )
        product = product + jnp.dot(
            firsts[:, x * width : (x + 1) * width], block, preferred_element_type=F32
        )

    @pl.when(step == 0)
    def _():
        total[...] = product

    @pl.when(step == steps - 1)
    def _():
        rows = keys.shape[0]
        slots = facts.shape[0]
        half = facts.shape[1] // 2
        slot_of = lax.broadcasted_iota(jnp.int32, (2 * slots, HD), 0) % slots
        lane = lax.broadcasted_iota(jnp.int32, (2 * slots, HD), 1)
        asked = jnp.zeros((2 * slots, HD), jnp.int32)
        for slot in range(slots):
            here = facts[slot : slot + 1, half : half + HD].astype(jnp.int32)
            asked = jnp.where(slot_of == slot, here, asked)
        mark = (asked == lane).astype(F32).astype(BF16)
        chosen = first_rows(facts, rows)
        theirs = (total[...] + product).astype(BF16)
        own = [
            jnp.dot(chosen, source[...], preferred_element_type=F32).astype(BF16)
            for source in (keys, values)
        ]
        line = jnp.concatenate([own[0], theirs[:, :HD], own[1], theirs[:, HD:], mark], axis=1)
        for copy in range(sent.shape[0] // (2 * slots)):
            sent[copy * 2 * slots : (copy + 1) * 2 * slots, :] = line


def send(firsts, weights, keys, values, facts, copies):
    along_z, along_x, cores, depth, _ = weights.shape
    depth = depth // 4
    whole = lambda array: pl.BlockSpec(array.shape, lambda i: (0, 0))
    weight = lambda part: pl.BlockSpec(
        (along_z, along_x // 2, cores, depth, HD), lambda i: (0, i, 0, part, 0)
    )
    shape = (copies * facts.shape[0], 5 * HD)
    return pl.pallas_call(
        send_kernel,
        out_shape=jax.ShapeDtypeStruct(shape, BF16),
        grid=(2,),
        in_specs=[
            pl.BlockSpec((firsts.shape[0], firsts.shape[1] // 2), lambda i: (0, i)),
            weight(1),
            weight(2),
            whole(keys),
            whole(values),
            whole(facts),
        ],
        out_specs=pl.BlockSpec(shape, lambda i: (0, 0)),
        scratch_shapes=[pltpu.VMEM((16, 2 * HD), F32)],
        compiler_params=pltpu.CompilerParams(vmem_limit_bytes=VMEM_LIMIT),
    )(firsts, weights, weights, keys, values, facts)


def attend_kernel(*refs):
    queries, keys, values = refs[0:6:3], refs[1:6:3], refs[2:6:3]
    near, far, facts, own_weights, sibling_weights, out, held, done, arrived, left = refs[6:]
    rows, columns = near.shape[0], 2 * HD
    _, along_z, along_x, cores, depth, _ = held.shape
    width = along_z * cores * depth
    fetches = [
        [
            pltpu.make_async_copy(
                source.at[:, x, :, pl.ds(3 * depth, depth), :],
                held.at[which, :, x],
                arrived.at[which, x],
            )
            for which, source in enumerate((own_weights, sibling_weights))
        ]
        for x in range(along_x)
    ]
    for pair in fetches:
        for fetch in pair:
            fetch.start()
    slots = facts.shape[0]
    half = facts.shape[1] // 2
    here = lax.axis_index("cand") // 2 * slots
    down = lax.broadcasted_iota(jnp.int32, (rows, rows), 0)
    across = lax.broadcasted_iota(jnp.int32, (rows, rows), 1)
    slot_down = jnp.zeros((rows, rows), jnp.int32)
    slot_across = jnp.zeros((rows, rows), jnp.int32)
    end = jnp.zeros((1, rows), jnp.int32)
    for slot in range(slots):
        end = end + facts[slot : slot + 1, :rows].astype(jnp.int32)
        if slot < slots - 1:
            slot_down = slot_down + (down >= end).astype(jnp.int32)
            slot_across = slot_across + (across >= end).astype(jnp.int32)
    asked = jnp.zeros((rows, HD), jnp.int32)
    for slot in range(slots):
        asked = jnp.where(
            slot_down[:, :HD] == slot,
            facts[slot : slot + 1, half : half + HD].astype(jnp.int32),
            asked,
        )
    local = ((slot_down == slot_across) & (down < end) & (across < end)) | (down == across)
    mark = (asked == across[:, :HD]).astype(F32).astype(BF16)
    same = lambda other: lax.dot_general(
        mark, other[:, 2 * columns :], NT, preferred_element_type=F32
    ) > 0.5
    masks = [local, same(near) & (across != here + slot_down), same(far)]
    scale = 1.0 / math.sqrt(HD)
    heads = []
    for head in range(columns // HD):
        lanes = slice(head * HD, (head + 1) * HD)
        value_lanes = slice(columns + head * HD, columns + (head + 1) * HD)
        swapped = columns - HD * (1 + head)
        far_lanes = slice(swapped, swapped + HD)
        far_value_lanes = slice(columns + swapped, columns + swapped + HD)
        query = queries[head][...]
        scores = [
            jnp.where(
                mask,
                lax.dot_general(query, key, NT, preferred_element_type=F32) * scale,
                NEGATIVE,
            )
            for mask, key in zip(masks, (keys[head][...], near[:, lanes], far[:, far_lanes]))
        ]
        peak = jnp.maximum(jnp.maximum(scores[0], scores[1]), scores[2])
        peak = jnp.max(peak, axis=1, keepdims=True)
        raised = [jnp.exp(score - peak) for score in scores]
        bottom = jnp.sum(raised[0] + raised[1] + raised[2], axis=1, keepdims=True)
        top = jnp.zeros((rows, HD), F32)
        for part, value in zip(
            raised, (values[head][...], near[:, value_lanes], far[:, far_value_lanes])
        ):
            top = top + jnp.dot(part.astype(BF16), value, preferred_element_type=F32)
        heads.append(jnp.where(down[:, :HD] < end[:, :HD], top / bottom, 0.0).astype(BF16))
    attended = jnp.concatenate(heads, axis=1)
    leaving = []
    for x in range(along_x):
        for fetch in fetches[x]:
            fetch.wait()
        for z in range(0, along_z, 2):
            block = jnp.concatenate(
                [held[which, z : z + 2, x].reshape(-1, HD) for which in range(2)], axis=1
            )
            at = x * width + z * cores * depth
            done[:, at : at + 2 * cores * depth] = lax.dot_general(
                attended, block, NT, preferred_element_type=F32
            ).astype(BF16)
        lanes = pl.ds(x * width, width)
        leaving.append(pltpu.make_async_copy(done.at[:, lanes], out.at[:, lanes], left.at[x]))
        leaving[x].start()
    for copy in leaving:
        copy.wait()


def attend(own, sibling, near, far, facts, own_weights, sibling_weights):
    along_z, along_x, cores, depth, _ = own_weights.shape
    depth = depth // 4
    rows = own[0].shape[0]
    columns = along_z * along_x * cores * depth
    vmem = pl.BlockSpec(memory_space=pltpu.VMEM)
    anywhere = pl.BlockSpec(memory_space=pl.ANY)
    return pl.pallas_call(
        attend_kernel,
        out_shape=jax.ShapeDtypeStruct((rows, columns), BF16),
        in_specs=[vmem] * 9 + [anywhere] * 2,
        out_specs=anywhere,
        scratch_shapes=[
            pltpu.VMEM((2, along_z, along_x, cores, depth, HD), BF16),
            pltpu.VMEM((rows, columns), BF16),
            pltpu.SemaphoreType.DMA((2, along_x)),
            pltpu.SemaphoreType.DMA((along_x,)),
        ],
        compiler_params=pltpu.CompilerParams(vmem_limit_bytes=VMEM_LIMIT),
    )(*own, *sibling, near, far, facts, own_weights, sibling_weights)


def add_kernel(residual, summed, out):
    out[...] = (residual[...].astype(F32) + summed[...].astype(F32)).astype(BF16)


def add(residual, summed):
    rows, width = residual.shape
    half = pl.BlockSpec((rows, width // 2), lambda i: (0, i))
    return pl.pallas_call(
        add_kernel,
        out_shape=jax.ShapeDtypeStruct(residual.shape, BF16),
        grid=(2,),
        in_specs=[half, half],
        out_specs=half,
        compiler_params=pltpu.CompilerParams(vmem_limit_bytes=VMEM_LIMIT),
    )(residual, summed)


def shards(passages, norm_gain, w_qkv, w_out, counts, owners, query_of):
    devices = lax.axis_size("cand")
    parts = lax.axis_size("mp")
    me = lax.axis_index("mp")
    core = lax.rem(lax.axis_index("cand"), 2)
    along_x = devices // (2 * ALONG_Z)
    with jax.named_scope("weights_gathered"):
        copies = copies_by_head(w_qkv, w_out.T, 2 * along_x)
        from_x = lax.all_to_all(
            copies.reshape(-1, HD), "cand", 0, 0, tiled=True, axis_index_groups=x_groups()
        ).reshape(along_x, 2, -1, HD)
        weights = lax.all_gather(from_x, "cand", axis_index_groups=z_groups())
    with jax.named_scope("passages_handed_over"):
        inner, outer, kept = pick(jnp.stack([owners, counts, query_of]), passages)
        from_x, inner, outer = lax.optimization_barrier((from_x, inner, outer))
        inner, outer = to_sibling(inner), to_outer(outer)
    with jax.named_scope("passages_packed"):
        packed, facts = pack(inner, kept, outer)
    with jax.named_scope("features_gathered"):
        half = packed.shape[0] // 2
        third, fourth = opposed(packed, 2), opposed(packed, -2)
        first, second = opposed(packed, 1), opposed(packed, -1)
        first, second, third, fourth = lax.optimization_barrier((first, second, third, fourth))
        fifth, sixth = opposed(third, 1), opposed(fourth, -1)
        last = (opposed(third[:half], 2), opposed(fourth[half:], -2))
        pieces = [packed, first, second, third, fourth, fifth, sixth, *last]
    away = jnp.array([0, -1, 1, -2, 2, -3, 3, 4, 0], jnp.int32)
    place = lax.rem(me + parts + away * (1 - 2 * core), parts).astype(jnp.int32)
    normed, residual, firsts = norm(place, pieces, norm_gain.reshape(parts, 1, -1), facts)
    with jax.named_scope("weights_swapped"):
        weights, *_ = lax.optimization_barrier((weights, fifth, sixth, *last))
        sibling_weights = to_sibling(weights)
    own = project(normed, weights)
    sent = send(firsts, sibling_weights, own[1], own[2], facts, devices // 2)
    sibling = project(normed, sibling_weights)
    with jax.named_scope("interaction_gathered"):
        near = lax.all_to_all(
            sent, "cand", 0, 0, tiled=True, axis_index_groups=same_core_groups()
        )
        far = to_sibling(near)
    partial = attend(own, sibling, near, far, facts, weights, sibling_weights)
    with jax.named_scope("heads_summed"):
        summed = lax.psum_scatter(partial, "mp", scatter_dimension=0, tiled=True)
    return add(residual, summed)


def solution(mesh):
    in_specs = (
        P("cand", None, "mp"),
        P(),
        P(None, "cand", "mp"),
        P("mp", "cand"),
        P("cand"),
        P("cand"),
        P("cand"),
    )
    out_specs = P(("cand", "mp"), None)
    return jax.shard_map(shards, mesh=mesh, in_specs=in_specs, out_specs=out_specs, check_vma=False)
```

```python
import math

import jax
import jax.numpy as jnp
from jax import lax
from jax.experimental import pallas as pl
from jax.experimental.pallas import tpu as pltpu
from jax.sharding import PartitionSpec as P

HD = 128
EPS = 1e-05
NEGATIVE = -1e30
VMEM_LIMIT = 48 * 1024 * 1024
F32 = jnp.float32
BF16 = jnp.bfloat16
NT = (((1,), (1,)), ((), ()))


def along(shard, axis, by):
    length = lax.axis_size(axis)
    return lax.ppermute(shard, axis, [(i, (i + by) % length) for i in range(length)])


def to_sibling(shard):
    length = lax.axis_size("cand")
    return lax.ppermute(shard, "cand", [(i, i ^ 1) for i in range(length)])


def same_core_groups():
    length = lax.axis_size("cand")
    return [list(range(core, length, 2)) for core in range(2)]


ALONG_Z = 8


def x_groups():
    length = lax.axis_size("cand")
    step = 2 * ALONG_Z
    return [
        [x + 2 * z + core for x in range(0, length, step) for core in range(2)]
        for z in range(ALONG_Z)
    ]


def z_groups():
    length = lax.axis_size("cand")
    step = 2 * ALONG_Z
    return [list(range(x, x + step)) for x in range(0, length, step)]


def to_outer(shard):
    length = lax.axis_size("cand")
    pairs = [(i, (i + (1 if i % 2 else length - 1)) % length) for i in range(length)]
    return lax.ppermute(shard, "cand", pairs)


def opposed(shard, by):
    chips, parts = lax.axis_size("cand"), lax.axis_size("mp")
    pairs = []
    for device in range(chips):
        signed = by if device % 2 == 0 else -by
        for part in range(parts):
            pairs.append((device * parts + part, device * parts + (part + signed) % parts))
    return lax.ppermute(shard, ("cand", "mp"), pairs)


def pick_kernel(table, passages, inner, outer, kept):
    me = lax.axis_index("cand")
    devices = lax.axis_size("cand")
    slots, length, width = passages.shape
    row = lax.broadcasted_iota(jnp.int32, (16, width), 0)
    lane = lax.broadcasted_iota(jnp.int32, (16, width), 1)
    number = [jnp.int32(0)] * 3
    core = lax.rem(me, 2)
    inward = jnp.where(core == 0, 1, devices - 1)
    outward = jnp.where(core == 0, devices - 1, 1)
    for slot in range(slots):
        ahead = lax.rem(table[0, slot] - me + devices, devices)
        facts = jnp.where(lane < width // 2, table[1, slot], table[2, slot]).astype(F32)
        tail = passages[slot, length - 16 :, :].astype(F32)
        tail = jnp.where(row == 15, facts, tail).astype(BF16)
        for which, (wanted, target) in enumerate(((inward, inner), (outward, outer), (0, kept))):
            hit = ahead == wanted
            place = jnp.minimum(number[which], target.shape[0] - 1)

            @pl.when(hit)
            def _():
                target[place, : length - 16, :] = passages[slot, : length - 16, :]
                target[place, length - 16 :, :] = tail

            number[which] = number[which] + hit.astype(jnp.int32)


def pick(table, passages):
    slots, length, width = passages.shape
    smem = pl.BlockSpec(memory_space=pltpu.SMEM)
    vmem = pl.BlockSpec(memory_space=pltpu.VMEM)
    shape = lambda n: jax.ShapeDtypeStruct((n, length, width), BF16)
    return pl.pallas_call(
        pick_kernel,
        out_shape=(shape(2), shape(2), shape(slots - 4)),
        in_specs=[smem, vmem],
        out_specs=(vmem, vmem, vmem),
        compiler_params=pltpu.CompilerParams(vmem_limit_bytes=VMEM_LIMIT),
    )(table, passages)


def copy_kernel(w_qkv, w_out, copies):
    depth = w_qkv.shape[1]
    for copy in range(copies.shape[0]):
        lanes = slice(copy % 2 * HD, (copy % 2 + 1) * HD)
        for part in range(3):
            copies[copy, part * depth : (part + 1) * depth, :] = w_qkv[part, :, lanes]
        copies[copy, 3 * depth :, :] = w_out[:, lanes]


def copies_by_head(w_qkv, w_out, number):
    vmem = pl.BlockSpec(memory_space=pltpu.VMEM)
    depth = 3 * w_qkv.shape[1] + w_out.shape[0]
    return pl.pallas_call(
        copy_kernel,
        out_shape=jax.ShapeDtypeStruct((number, depth, HD), BF16),
        in_specs=[vmem, vmem],
        out_specs=vmem,
        compiler_params=pltpu.CompilerParams(vmem_limit_bytes=VMEM_LIMIT),
    )(w_qkv, w_out)


def pack_kernel(inner, kept, outer, packed, facts):
    rows = packed.shape[0]
    length = kept.shape[1]
    first = lax.rem(lax.axis_index("cand"), 2) == 0
    blocks = (
        [jnp.where(first, outer[i], inner[i]) for i in range(outer.shape[0])]
        + [kept[i] for i in range(kept.shape[0])]
        + [jnp.where(first, inner[i], outer[i]) for i in range(inner.shape[0])]
    )
    position = lax.broadcasted_iota(jnp.int32, (rows, length), 0)
    offset = lax.broadcasted_iota(jnp.int32, (rows, length), 1)
    start = jnp.zeros((1, length), jnp.int32)
    total = jnp.zeros(packed.shape, F32)
    for slot, block in enumerate(blocks):
        fact = block[length - 16 :, :].astype(F32)[15:16, :]
        facts[slot : slot + 1, :] = fact
        count = fact[:, :length].astype(jnp.int32)
        chosen = (position == start + offset) & (offset < count)
        total = total + jnp.dot(
            chosen.astype(F32).astype(BF16), block, preferred_element_type=F32
        )
        start = start + count
    packed[...] = total.astype(BF16)


def pack(inner, kept, outer):
    slots = inner.shape[0] + kept.shape[0] + outer.shape[0]
    length, width = kept.shape[1:]
    vmem = pl.BlockSpec(memory_space=pltpu.VMEM)
    return pl.pallas_call(
        pack_kernel,
        out_shape=(
            jax.ShapeDtypeStruct((slots * length // 2, width), BF16),
            jax.ShapeDtypeStruct((slots, width), F32),
        ),
        in_specs=[vmem] * 3,
        out_specs=(vmem, vmem),
        compiler_params=pltpu.CompilerParams(vmem_limit_bytes=VMEM_LIMIT),
    )(inner, kept, outer)


def project_kernel(place, *refs):
    pieces, gain, weights, facts = refs[:9], *refs[9:12]
    queries, keys, values, residual, sent, rows_in, total, squares = refs[12:]
    step = pl.program_id(0)
    rows = rows_in.shape[0]
    width = rows_in.shape[1] // 2
    half = rows // 2
    for side in range(2):
        lanes = slice(side * width, (side + 1) * width)
        wanted = place[2 * step + side]
        for number in range(7):

            @pl.when(wanted == number)
            def _():
                rows_in[:, lanes] = pieces[number][...]

        @pl.when(wanted == 7)
        def _():
            rows_in[:half, lanes] = pieces[7][...]
            rows_in[half:, lanes] = pieces[8][...]

    share = residual.shape[0]
    residual[...] = rows_in[pl.ds(pl.multiple_of(place[8] * share, share), share), :]
    x = rows_in[...].astype(F32)
    square = jnp.sum(x * x, axis=1, keepdims=True)
    scaled = (x * gain[0]).astype(BF16)
    depth = weights.shape[4] // 3
    block = jnp.concatenate(
        [
            weights[:, head, 0, :, part * depth : (part + 1) * depth, :].reshape(-1, HD)
            for part in range(3)
            for head in range(2)
        ],
        axis=1,
    )
    product = jnp.dot(scaled, block, preferred_element_type=F32)

    @pl.when(step == 0)
    def _():
        total[...] = product
        squares[...] = square

    @pl.when(step > 0)
    def _():
        total[...] += product
        squares[...] += square

    @pl.when(step == 3)
    def _():
        inverse = lax.rsqrt(squares[...] / (8 * width) + EPS)
        columns = 2 * HD
        done = [
            (total[:, part * columns : (part + 1) * columns] * inverse).astype(BF16)
            for part in range(3)
        ]
        queries[...], keys[...], values[...] = done
        slots = facts.shape[0]
        slot_of = lax.broadcasted_iota(jnp.int32, (2 * slots, rows), 0) % slots
        position = lax.broadcasted_iota(jnp.int32, (2 * slots, rows), 1)
        start = jnp.zeros((1, rows), jnp.int32)
        first = jnp.zeros((2 * slots, rows), jnp.int32)
        asked = jnp.zeros((2 * slots, HD), jnp.int32)
        for slot in range(slots):
            here = slot_of == slot
            first = jnp.where(here, start, first)
            asked = jnp.where(
                here[:, :HD],
                facts[slot : slot + 1, width // 2 : width // 2 + HD].astype(jnp.int32),
                asked,
            )
            start = start + facts[slot : slot + 1, :rows].astype(jnp.int32)
        chosen = (first == position).astype(F32).astype(BF16)
        mark = (asked == position[:, :HD]).astype(F32).astype(BF16)
        key_rows = jnp.dot(chosen, done[1], preferred_element_type=F32).astype(BF16)
        value_rows = jnp.dot(chosen, done[2], preferred_element_type=F32).astype(BF16)
        for copy in range(sent.shape[0] // (2 * slots)):
            there = slice(copy * 2 * slots, (copy + 1) * 2 * slots)
            sent[there, :columns] = key_rows
            sent[there, columns : 2 * columns] = value_rows
            sent[there, 2 * columns :] = mark


def project(place, pieces, gain, weights, facts, copies):
    rows, width = pieces[0].shape
    along_z, heads, along_x, cores = weights.shape[:4]
    columns = 2 * HD
    whole = lambda array: pl.BlockSpec(array.shape, lambda r, place: (0,) * array.ndim)
    out = lambda *shape: (
        jax.ShapeDtypeStruct(shape, BF16),
        pl.BlockSpec(shape, lambda r, place: (0, 0)),
    )
    outs = [out(rows, columns)] * 3
    outs.append(
        (
            jax.ShapeDtypeStruct((rows // 8, 8 * width), BF16),
            pl.BlockSpec((rows // 8, 2 * width), lambda r, place: (0, r)),
        )
    )
    outs.append(out(copies * facts.shape[0], 2 * columns + HD))
    weight = pl.BlockSpec(
        (along_z, heads, 1, cores, 192, HD), lambda r, place: (0, 0, r, 0, 0, 0)
    )
    return pl.pallas_call(
        project_kernel,
        out_shape=tuple(o[0] for o in outs),
        grid_spec=pltpu.PrefetchScalarGridSpec(
            num_scalar_prefetch=1,
            grid=(along_x,),
            in_specs=[whole(piece) for piece in pieces]
            + [
                pl.BlockSpec((1, 1, 2 * width), lambda r, place: (r, 0, 0)),
                weight,
                whole(facts),
            ],
            out_specs=tuple(o[1] for o in outs),
            scratch_shapes=[
                pltpu.VMEM((rows, 2 * width), BF16),
                pltpu.VMEM((rows, 3 * columns), F32),
                pltpu.VMEM((rows, 1), F32),
            ],
        ),
        compiler_params=pltpu.CompilerParams(vmem_limit_bytes=VMEM_LIMIT),
    )(place, *pieces, gain, weights, facts)


def attend_kernel(*refs):
    queries, keys, values, near, far, facts, weights, out, held, done, arrived, left = refs
    rows, columns = near.shape[0], 2 * HD
    _, along_z, along_x, cores, depth, _ = held.shape
    width = along_z * cores * depth
    fetches = [
        [
            pltpu.make_async_copy(
                weights.at[:, which, x, :, pl.ds(3 * depth, depth), :],
                held.at[which, :, x],
                arrived.at[which, x],
            )
            for which in range(2)
        ]
        for x in range(along_x)
    ]
    for pair in fetches:
        for fetch in pair:
            fetch.start()
    slots = facts.shape[0]
    half = facts.shape[1] // 2
    here = lax.axis_index("cand") // 2 * slots
    down = lax.broadcasted_iota(jnp.int32, (rows, rows), 0)
    across = lax.broadcasted_iota(jnp.int32, (rows, rows), 1)
    slot_down = jnp.zeros((rows, rows), jnp.int32)
    slot_across = jnp.zeros((rows, rows), jnp.int32)
    end = jnp.zeros((1, rows), jnp.int32)
    for slot in range(slots):
        end = end + facts[slot : slot + 1, :rows].astype(jnp.int32)
        if slot < slots - 1:
            slot_down = slot_down + (down >= end).astype(jnp.int32)
            slot_across = slot_across + (across >= end).astype(jnp.int32)
    asked = jnp.zeros((rows, HD), jnp.int32)
    for slot in range(slots):
        asked = jnp.where(
            slot_down[:, :HD] == slot,
            facts[slot : slot + 1, half : half + HD].astype(jnp.int32),
            asked,
        )
    local = ((slot_down == slot_across) & (down < end) & (across < end)) | (down == across)
    mark = (asked == across[:, :HD]).astype(F32).astype(BF16)
    same = lambda other: lax.dot_general(
        mark, other[:, 2 * columns :], NT, preferred_element_type=F32
    ) > 0.5
    masks = [local, same(near) & (across != here + slot_down), same(far)]
    scale = 1.0 / math.sqrt(HD)
    heads = []
    for head in range(columns // HD):
        lanes = slice(head * HD, (head + 1) * HD)
        value_lanes = slice(columns + head * HD, columns + (head + 1) * HD)
        query = queries[:, lanes]
        scores = [
            jnp.where(
                mask,
                lax.dot_general(query, key, NT, preferred_element_type=F32) * scale,
                NEGATIVE,
            )
            for mask, key in zip(masks, (keys[:, lanes], near[:, lanes], far[:, lanes]))
        ]
        peak = jnp.maximum(jnp.maximum(scores[0], scores[1]), scores[2])
        peak = jnp.max(peak, axis=1, keepdims=True)
        raised = [jnp.exp(score - peak) for score in scores]
        bottom = jnp.sum(raised[0] + raised[1] + raised[2], axis=1, keepdims=True)
        top = jnp.zeros((rows, HD), F32)
        for part, value in zip(
            raised, (values[:, lanes], near[:, value_lanes], far[:, value_lanes])
        ):
            top = top + jnp.dot(part.astype(BF16), value, preferred_element_type=F32)
        heads.append(jnp.where(down[:, :HD] < end[:, :HD], top / bottom, 0.0).astype(BF16))
    attended = jnp.concatenate(heads, axis=1)
    leaving = []
    for x in range(along_x):
        for fetch in fetches[x]:
            fetch.wait()
        for z in range(0, along_z, 2):
            block = jnp.concatenate(
                [held[which, z : z + 2, x].reshape(-1, HD) for which in range(2)], axis=1
            )
            at = x * width + z * cores * depth
            done[:, at : at + 2 * cores * depth] = lax.dot_general(
                attended, block, NT, preferred_element_type=F32
            ).astype(BF16)
        lanes = pl.ds(x * width, width)
        leaving.append(pltpu.make_async_copy(done.at[:, lanes], out.at[:, lanes], left.at[x]))
        leaving[x].start()
    for copy in leaving:
        copy.wait()


def attend(queries, keys, values, near, far, facts, weights):
    along_z, _, along_x, cores, depth, _ = weights.shape
    depth = depth // 4
    rows = queries.shape[0]
    columns = along_z * along_x * cores * depth
    vmem = pl.BlockSpec(memory_space=pltpu.VMEM)
    anywhere = pl.BlockSpec(memory_space=pl.ANY)
    return pl.pallas_call(
        attend_kernel,
        out_shape=jax.ShapeDtypeStruct((rows, columns), BF16),
        in_specs=[vmem] * 6 + [anywhere],
        out_specs=anywhere,
        scratch_shapes=[
            pltpu.VMEM((2, along_z, along_x, cores, depth, HD), BF16),
            pltpu.VMEM((rows, columns), BF16),
            pltpu.SemaphoreType.DMA((2, along_x)),
            pltpu.SemaphoreType.DMA((along_x,)),
        ],
        compiler_params=pltpu.CompilerParams(vmem_limit_bytes=VMEM_LIMIT),
    )(queries, keys, values, near, far, facts, weights)


def add_kernel(residual, summed, out):
    out[...] = (residual[...].astype(F32) + summed[...].astype(F32)).astype(BF16)


def add(residual, summed):
    rows, width = residual.shape
    half = pl.BlockSpec((rows, width // 2), lambda i: (0, i))
    return pl.pallas_call(
        add_kernel,
        out_shape=jax.ShapeDtypeStruct(residual.shape, BF16),
        grid=(2,),
        in_specs=[half, half],
        out_specs=half,
        compiler_params=pltpu.CompilerParams(vmem_limit_bytes=VMEM_LIMIT),
    )(residual, summed)


def shards(passages, norm_gain, w_qkv, w_out, counts, owners, query_of):
    devices = lax.axis_size("cand")
    parts = lax.axis_size("mp")
    me = lax.axis_index("mp")
    core = lax.rem(lax.axis_index("cand"), 2)
    along_x = devices // (2 * ALONG_Z)
    with jax.named_scope("weights_gathered"):
        copies = copies_by_head(w_qkv, w_out.T, 2 * along_x)
        from_x = lax.all_to_all(
            copies.reshape(-1, HD), "cand", 0, 0, tiled=True, axis_index_groups=x_groups()
        ).reshape(along_x, 2, -1, HD)
        weights = lax.all_gather(from_x, "cand", axis_index_groups=z_groups())
        weights = weights.reshape((ALONG_Z, 2) + from_x.shape)
    with jax.named_scope("passages_handed_over"):
        inner, outer, kept = pick(jnp.stack([owners, counts, query_of]), passages)
        from_x, inner, outer = lax.optimization_barrier((from_x, inner, outer))
        inner, outer = to_sibling(inner), to_outer(outer)
    with jax.named_scope("passages_packed"):
        packed, facts = pack(inner, kept, outer)
    with jax.named_scope("features_gathered"):
        half = packed.shape[0] // 2
        third, fourth = opposed(packed, 2), opposed(packed, -2)
        first, second = opposed(packed, 1), opposed(packed, -1)
        first, second, third, fourth = lax.optimization_barrier((first, second, third, fourth))
        fifth, sixth = opposed(third, 1), opposed(fourth, -1)
        last = (opposed(third[:half], 2), opposed(fourth[half:], -2))
        pieces = [packed, first, second, third, fourth, fifth, sixth, *last]
    away = (jnp.arange(parts, dtype=jnp.int32) - me) * (1 - 2 * core)
    away = lax.rem(away + parts, parts)
    place = jnp.where(away < parts // 2, 2 * away, 2 * parts - 1 - 2 * away)
    place = jnp.concatenate([place, me[None]]).astype(jnp.int32)
    gain = norm_gain.reshape(along_x, 1, -1)
    queries, keys, values, residual, sent = project(
        place, pieces, gain, weights, facts, devices // 2
    )
    with jax.named_scope("interaction_gathered"):
        near = lax.all_to_all(
            sent, "cand", 0, 0, tiled=True, axis_index_groups=same_core_groups()
        )
        far = to_sibling(near)
    partial = attend(queries, keys, values, near, far, facts, weights)
    with jax.named_scope("heads_summed"):
        summed = lax.psum_scatter(partial, "mp", scatter_dimension=0, tiled=True)
    return add(residual, summed)


def solution(mesh):
    in_specs = (
        P("cand", None, "mp"),
        P(),
        P(None, "cand", "mp"),
        P("mp", "cand"),
        P("cand"),
        P("cand"),
        P("cand"),
    )
    out_specs = P(("cand", "mp"), None)
    return jax.shard_map(shards, mesh=mesh, in_specs=in_specs, out_specs=out_specs, check_vma=False)
```

```python
import math

import jax
import jax.numpy as jnp
from jax import lax
from jax.experimental import pallas as pl
from jax.experimental.pallas import tpu as pltpu
from jax.sharding import PartitionSpec as P

HD = 128
EPS = 1e-05
NEGATIVE = -1e30
VMEM_LIMIT = 48 * 1024 * 1024
F32 = jnp.float32
BF16 = jnp.bfloat16
NT = (((1,), (1,)), ((), ()))


def along(shard, axis, by):
    length = lax.axis_size(axis)
    return lax.ppermute(shard, axis, [(i, (i + by) % length) for i in range(length)])


def to_sibling(shard):
    length = lax.axis_size("cand")
    return lax.ppermute(shard, "cand", [(i, i ^ 1) for i in range(length)])


def same_core_groups():
    length = lax.axis_size("cand")
    return [list(range(core, length, 2)) for core in range(2)]


ALONG_Z = 8


def x_groups():
    length = lax.axis_size("cand")
    step = 2 * ALONG_Z
    return [list(range(first, length, step)) for first in range(step)]


def z_groups():
    length = lax.axis_size("cand")
    step = 2 * ALONG_Z
    return [list(range(x, x + step)) for x in range(0, length, step)]


def to_outer(shard):
    length = lax.axis_size("cand")
    pairs = [(i, (i + (1 if i % 2 else length - 1)) % length) for i in range(length)]
    return lax.ppermute(shard, "cand", pairs)


def opposed(shard, by):
    chips, parts = lax.axis_size("cand"), lax.axis_size("mp")
    pairs = []
    for device in range(chips):
        signed = by if device % 2 == 0 else -by
        for part in range(parts):
            pairs.append((device * parts + part, device * parts + (part + signed) % parts))
    return lax.ppermute(shard, ("cand", "mp"), pairs)


def pick_kernel(table, passages, inner, outer, kept):
    me = lax.axis_index("cand")
    devices = lax.axis_size("cand")
    slots, length, width = passages.shape
    row = lax.broadcasted_iota(jnp.int32, (16, width), 0)
    lane = lax.broadcasted_iota(jnp.int32, (16, width), 1)
    number = [jnp.int32(0)] * 3
    core = lax.rem(me, 2)
    inward = jnp.where(core == 0, 1, devices - 1)
    outward = jnp.where(core == 0, devices - 1, 1)
    for slot in range(slots):
        ahead = lax.rem(table[0, slot] - me + devices, devices)
        facts = jnp.where(lane < width // 2, table[1, slot], table[2, slot]).astype(F32)
        tail = passages[slot, length - 16 :, :].astype(F32)
        tail = jnp.where(row == 15, facts, tail).astype(BF16)
        for which, (wanted, target) in enumerate(((inward, inner), (outward, outer), (0, kept))):
            hit = ahead == wanted
            place = jnp.minimum(number[which], target.shape[0] - 1)

            @pl.when(hit)
            def _():
                target[place, : length - 16, :] = passages[slot, : length - 16, :]
                target[place, length - 16 :, :] = tail

            number[which] = number[which] + hit.astype(jnp.int32)


def pick(table, passages):
    slots, length, width = passages.shape
    smem = pl.BlockSpec(memory_space=pltpu.SMEM)
    vmem = pl.BlockSpec(memory_space=pltpu.VMEM)
    shape = lambda n: jax.ShapeDtypeStruct((n, length, width), BF16)
    return pl.pallas_call(
        pick_kernel,
        out_shape=(shape(2), shape(2), shape(slots - 4)),
        in_specs=[smem, vmem],
        out_specs=(vmem, vmem, vmem),
        compiler_params=pltpu.CompilerParams(vmem_limit_bytes=VMEM_LIMIT),
    )(table, passages)


def copy_kernel(w_qkv, w_out, copies):
    depth = w_qkv.shape[1]
    for copy in range(copies.shape[0]):
        for part in range(3):
            copies[copy, part * depth : (part + 1) * depth, :] = w_qkv[part]
        copies[copy, 3 * depth :, :] = w_out[...]


def copied(w_qkv, w_out, number):
    vmem = pl.BlockSpec(memory_space=pltpu.VMEM)
    depth = 3 * w_qkv.shape[1] + w_out.shape[0]
    return pl.pallas_call(
        copy_kernel,
        out_shape=jax.ShapeDtypeStruct((number, depth, w_qkv.shape[2]), BF16),
        in_specs=[vmem, vmem],
        out_specs=vmem,
        compiler_params=pltpu.CompilerParams(vmem_limit_bytes=VMEM_LIMIT),
    )(w_qkv, w_out)


def pack_kernel(inner, kept, outer, packed, facts):
    rows = packed.shape[0]
    length = kept.shape[1]
    first = lax.rem(lax.axis_index("cand"), 2) == 0
    blocks = (
        [jnp.where(first, outer[i], inner[i]) for i in range(outer.shape[0])]
        + [kept[i] for i in range(kept.shape[0])]
        + [jnp.where(first, inner[i], outer[i]) for i in range(inner.shape[0])]
    )
    position = lax.broadcasted_iota(jnp.int32, (rows, length), 0)
    offset = lax.broadcasted_iota(jnp.int32, (rows, length), 1)
    start = jnp.zeros((1, length), jnp.int32)
    total = jnp.zeros(packed.shape, F32)
    for slot, block in enumerate(blocks):
        fact = block[length - 16 :, :].astype(F32)[15:16, :]
        facts[slot : slot + 1, :] = fact
        count = fact[:, :length].astype(jnp.int32)
        chosen = (position == start + offset) & (offset < count)
        total = total + jnp.dot(
            chosen.astype(F32).astype(BF16), block, preferred_element_type=F32
        )
        start = start + count
    packed[...] = total.astype(BF16)


def pack(inner, kept, outer):
    slots = inner.shape[0] + kept.shape[0] + outer.shape[0]
    length, width = kept.shape[1:]
    vmem = pl.BlockSpec(memory_space=pltpu.VMEM)
    return pl.pallas_call(
        pack_kernel,
        out_shape=(
            jax.ShapeDtypeStruct((slots * length // 2, width), BF16),
            jax.ShapeDtypeStruct((slots, width), F32),
        ),
        in_specs=[vmem] * 3,
        out_specs=(vmem, vmem),
        compiler_params=pltpu.CompilerParams(vmem_limit_bytes=VMEM_LIMIT),
    )(inner, kept, outer)


def project_kernel(place, *refs):
    pieces, gain, weights, facts = refs[:9], *refs[9:12]
    queries, keys, values, residual, sent, rows_in, total, squares = refs[12:]
    step = pl.program_id(0)
    rows = rows_in.shape[0]
    width = rows_in.shape[1] // 2
    half = rows // 2
    for side in range(2):
        lanes = slice(side * width, (side + 1) * width)
        wanted = place[2 * step + side]
        for number in range(7):

            @pl.when(wanted == number)
            def _():
                rows_in[:, lanes] = pieces[number][...]

        @pl.when(wanted == 7)
        def _():
            rows_in[:half, lanes] = pieces[7][...]
            rows_in[half:, lanes] = pieces[8][...]

    share = residual.shape[0]
    residual[...] = rows_in[pl.ds(pl.multiple_of(place[8] * share, share), share), :]
    x = rows_in[...].astype(F32)
    square = jnp.sum(x * x, axis=1, keepdims=True)
    scaled = (x * gain[0]).astype(BF16)
    depth = weights.shape[3] // 3
    columns = weights.shape[4]
    product = jnp.concatenate(
        [
            jnp.dot(
                scaled,
                weights[:, :, 0, part * depth : (part + 1) * depth, :].reshape(-1, columns),
                preferred_element_type=F32,
            )
            for part in range(3)
        ],
        axis=1,
    )

    @pl.when(step == 0)
    def _():
        total[...] = product
        squares[...] = square

    @pl.when(step > 0)
    def _():
        total[...] += product
        squares[...] += square

    @pl.when(step == 3)
    def _():
        inverse = lax.rsqrt(squares[...] / (8 * width) + EPS)
        done = [
            (total[:, part * columns : (part + 1) * columns] * inverse).astype(BF16)
            for part in range(3)
        ]
        queries[...], keys[...], values[...] = done
        slots = facts.shape[0]
        slot_of = lax.broadcasted_iota(jnp.int32, (2 * slots, rows), 0) % slots
        position = lax.broadcasted_iota(jnp.int32, (2 * slots, rows), 1)
        start = jnp.zeros((1, rows), jnp.int32)
        first = jnp.zeros((2 * slots, rows), jnp.int32)
        asked = jnp.zeros((2 * slots, HD), jnp.int32)
        for slot in range(slots):
            here = slot_of == slot
            first = jnp.where(here, start, first)
            asked = jnp.where(
                here[:, :HD],
                facts[slot : slot + 1, width // 2 : width // 2 + HD].astype(jnp.int32),
                asked,
            )
            start = start + facts[slot : slot + 1, :rows].astype(jnp.int32)
        chosen = (first == position).astype(F32).astype(BF16)
        mark = (asked == position[:, :HD]).astype(F32).astype(BF16)
        key_rows = jnp.dot(chosen, done[1], preferred_element_type=F32).astype(BF16)
        value_rows = jnp.dot(chosen, done[2], preferred_element_type=F32).astype(BF16)
        for copy in range(sent.shape[0] // (2 * slots)):
            there = slice(copy * 2 * slots, (copy + 1) * 2 * slots)
            sent[there, :columns] = key_rows
            sent[there, columns : 2 * columns] = value_rows
            sent[there, 2 * columns :] = mark


def project(place, pieces, gain, weights, facts, copies):
    rows, width = pieces[0].shape
    along_z, cores, along_x = weights.shape[:3]
    columns = 2 * HD
    whole = lambda array: pl.BlockSpec(array.shape, lambda r, place: (0,) * array.ndim)
    out = lambda *shape: (
        jax.ShapeDtypeStruct(shape, BF16),
        pl.BlockSpec(shape, lambda r, place: (0, 0)),
    )
    outs = [out(rows, columns)] * 3
    outs.append(
        (
            jax.ShapeDtypeStruct((rows // 8, 8 * width), BF16),
            pl.BlockSpec((rows // 8, 2 * width), lambda r, place: (0, r)),
        )
    )
    outs.append(out(copies * facts.shape[0], 2 * columns + HD))
    weight = pl.BlockSpec(
        (along_z, cores, 1, 192, columns), lambda r, place: (0, 0, r, 0, 0)
    )
    return pl.pallas_call(
        project_kernel,
        out_shape=tuple(o[0] for o in outs),
        grid_spec=pltpu.PrefetchScalarGridSpec(
            num_scalar_prefetch=1,
            grid=(along_x,),
            in_specs=[whole(piece) for piece in pieces]
            + [
                pl.BlockSpec((1, 1, 2 * width), lambda r, place: (r, 0, 0)),
                weight,
                whole(facts),
            ],
            out_specs=tuple(o[1] for o in outs),
            scratch_shapes=[
                pltpu.VMEM((rows, 2 * width), BF16),
                pltpu.VMEM((rows, 3 * columns), F32),
                pltpu.VMEM((rows, 1), F32),
            ],
        ),
        compiler_params=pltpu.CompilerParams(vmem_limit_bytes=VMEM_LIMIT),
    )(place, *pieces, gain, weights, facts)


def attend_kernel(*refs):
    queries, keys, values, near, far, facts, weights, out, held, done, arrived, left = refs
    rows, columns = near.shape[0], 2 * HD
    along_z, cores, along_x, depth, _ = held.shape
    width = along_z * cores * depth
    fetches = [
        pltpu.make_async_copy(
            weights.at[:, :, x, pl.ds(3 * depth, depth), :], held.at[:, :, x], arrived.at[x]
        )
        for x in range(along_x)
    ]
    for fetch in fetches:
        fetch.start()
    slots = facts.shape[0]
    half = facts.shape[1] // 2
    here = lax.axis_index("cand") // 2 * slots
    down = lax.broadcasted_iota(jnp.int32, (rows, rows), 0)
    across = lax.broadcasted_iota(jnp.int32, (rows, rows), 1)
    slot_down = jnp.zeros((rows, rows), jnp.int32)
    slot_across = jnp.zeros((rows, rows), jnp.int32)
    end = jnp.zeros((1, rows), jnp.int32)
    for slot in range(slots):
        end = end + facts[slot : slot + 1, :rows].astype(jnp.int32)
        if slot < slots - 1:
            slot_down = slot_down + (down >= end).astype(jnp.int32)
            slot_across = slot_across + (across >= end).astype(jnp.int32)
    asked = jnp.zeros((rows, HD), jnp.int32)
    for slot in range(slots):
        asked = jnp.where(
            slot_down[:, :HD] == slot,
            facts[slot : slot + 1, half : half + HD].astype(jnp.int32),
            asked,
        )
    local = ((slot_down == slot_across) & (down < end) & (across < end)) | (down == across)
    mark = (asked == across[:, :HD]).astype(F32).astype(BF16)
    same = lambda other: lax.dot_general(
        mark, other[:, 2 * columns :], NT, preferred_element_type=F32
    ) > 0.5
    masks = [local, same(near) & (across != here + slot_down), same(far)]
    scale = 1.0 / math.sqrt(HD)
    heads = []
    for head in range(columns // HD):
        lanes = slice(head * HD, (head + 1) * HD)
        value_lanes = slice(columns + head * HD, columns + (head + 1) * HD)
        query = queries[:, lanes]
        scores = [
            jnp.where(
                mask,
                lax.dot_general(query, key, NT, preferred_element_type=F32) * scale,
                NEGATIVE,
            )
            for mask, key in zip(masks, (keys[:, lanes], near[:, lanes], far[:, lanes]))
        ]
        peak = jnp.maximum(jnp.maximum(scores[0], scores[1]), scores[2])
        peak = jnp.max(peak, axis=1, keepdims=True)
        raised = [jnp.exp(score - peak) for score in scores]
        bottom = jnp.sum(raised[0] + raised[1] + raised[2], axis=1, keepdims=True)
        top = jnp.zeros((rows, HD), F32)
        for part, value in zip(
            raised, (values[:, lanes], near[:, value_lanes], far[:, value_lanes])
        ):
            top = top + jnp.dot(part.astype(BF16), value, preferred_element_type=F32)
        heads.append(jnp.where(down[:, :HD] < end[:, :HD], top / bottom, 0.0).astype(BF16))
    attended = jnp.concatenate(heads, axis=1)
    leaving = []
    for x in range(along_x):
        fetches[x].wait()
        for z in range(0, along_z, 2):
            block = held[z : z + 2, :, x].reshape(-1, columns)
            at = x * width + z * cores * depth
            done[:, at : at + 2 * cores * depth] = lax.dot_general(
                attended, block, NT, preferred_element_type=F32
            ).astype(BF16)
        lanes = pl.ds(x * width, width)
        leaving.append(pltpu.make_async_copy(done.at[:, lanes], out.at[:, lanes], left.at[x]))
        leaving[x].start()
    for copy in leaving:
        copy.wait()


def attend(queries, keys, values, near, far, facts, weights):
    along_z, cores, along_x, depth, inner = weights.shape
    depth = depth // 4
    rows = queries.shape[0]
    columns = along_z * along_x * cores * depth
    vmem = pl.BlockSpec(memory_space=pltpu.VMEM)
    anywhere = pl.BlockSpec(memory_space=pl.ANY)
    return pl.pallas_call(
        attend_kernel,
        out_shape=jax.ShapeDtypeStruct((rows, columns), BF16),
        in_specs=[vmem] * 6 + [anywhere],
        out_specs=anywhere,
        scratch_shapes=[
            pltpu.VMEM((along_z, cores, along_x, depth, inner), BF16),
            pltpu.VMEM((rows, columns), BF16),
            pltpu.SemaphoreType.DMA((along_x,)),
            pltpu.SemaphoreType.DMA((along_x,)),
        ],
        compiler_params=pltpu.CompilerParams(vmem_limit_bytes=VMEM_LIMIT),
    )(queries, keys, values, near, far, facts, weights)


def add_kernel(residual, summed, out):
    out[...] = (residual[...].astype(F32) + summed[...].astype(F32)).astype(BF16)


def add(residual, summed):
    rows, width = residual.shape
    half = pl.BlockSpec((rows, width // 2), lambda i: (0, i))
    return pl.pallas_call(
        add_kernel,
        out_shape=jax.ShapeDtypeStruct(residual.shape, BF16),
        grid=(2,),
        in_specs=[half, half],
        out_specs=half,
        compiler_params=pltpu.CompilerParams(vmem_limit_bytes=VMEM_LIMIT),
    )(residual, summed)


def shards(passages, norm_gain, w_qkv, w_out, counts, owners, query_of):
    devices = lax.axis_size("cand")
    parts = lax.axis_size("mp")
    me = lax.axis_index("mp")
    core = lax.rem(lax.axis_index("cand"), 2)
    along_x = devices // (2 * ALONG_Z)
    with jax.named_scope("weights_gathered"):
        copies = copied(w_qkv, w_out.T, along_x)
        from_x = lax.all_to_all(
            copies.reshape(-1, 2 * HD), "cand", 0, 0, tiled=True, axis_index_groups=x_groups()
        ).reshape(copies.shape)
        weights = lax.all_gather(from_x, "cand", axis_index_groups=z_groups())
        weights = weights.reshape((ALONG_Z, 2) + from_x.shape)
    with jax.named_scope("passages_handed_over"):
        inner, outer, kept = pick(jnp.stack([owners, counts, query_of]), passages)
        from_x, inner, outer = lax.optimization_barrier((from_x, inner, outer))
        inner, outer = to_sibling(inner), to_outer(outer)
    with jax.named_scope("passages_packed"):
        packed, facts = pack(inner, kept, outer)
    with jax.named_scope("features_gathered"):
        half = packed.shape[0] // 2
        third, fourth = opposed(packed, 2), opposed(packed, -2)
        first, second = opposed(packed, 1), opposed(packed, -1)
        first, second, third, fourth = lax.optimization_barrier((first, second, third, fourth))
        fifth, sixth = opposed(third, 1), opposed(fourth, -1)
        last = (opposed(third[:half], 2), opposed(fourth[half:], -2))
        pieces = [packed, first, second, third, fourth, fifth, sixth, *last]
    away = (jnp.arange(parts, dtype=jnp.int32) - me) * (1 - 2 * core)
    away = lax.rem(away + parts, parts)
    place = jnp.where(away < parts // 2, 2 * away, 2 * parts - 1 - 2 * away)
    place = jnp.concatenate([place, me[None]]).astype(jnp.int32)
    gain = norm_gain.reshape(along_x, 1, -1)
    queries, keys, values, residual, sent = project(
        place, pieces, gain, weights, facts, devices // 2
    )
    with jax.named_scope("interaction_gathered"):
        near = lax.all_to_all(
            sent, "cand", 0, 0, tiled=True, axis_index_groups=same_core_groups()
        )
        far = to_sibling(near)
    partial = attend(queries, keys, values, near, far, facts, weights)
    with jax.named_scope("heads_summed"):
        summed = lax.psum_scatter(partial, "mp", scatter_dimension=0, tiled=True)
    return add(residual, summed)


def solution(mesh):
    in_specs = (
        P("cand", None, "mp"),
        P(),
        P(None, "cand", "mp"),
        P("mp", "cand"),
        P("cand"),
        P("cand"),
        P("cand"),
    )
    out_specs = P(("cand", "mp"), None)
    return jax.shard_map(shards, mesh=mesh, in_specs=in_specs, out_specs=out_specs, check_vma=False)
```

```python
import math

import jax
import jax.numpy as jnp
from jax import lax
from jax.experimental import pallas as pl
from jax.experimental.pallas import tpu as pltpu
from jax.sharding import PartitionSpec as P

HD = 128
EPS = 1e-05
NEGATIVE = -1e30
VMEM_LIMIT = 48 * 1024 * 1024
F32 = jnp.float32
BF16 = jnp.bfloat16
NT = (((1,), (1,)), ((), ()))


def along(shard, axis, by):
    length = lax.axis_size(axis)
    return lax.ppermute(shard, axis, [(i, (i + by) % length) for i in range(length)])


def to_sibling(shard):
    length = lax.axis_size("cand")
    return lax.ppermute(shard, "cand", [(i, i ^ 1) for i in range(length)])


def same_core_groups():
    length = lax.axis_size("cand")
    return [list(range(core, length, 2)) for core in range(2)]


ALONG_Z = 8


def x_groups():
    length = lax.axis_size("cand")
    step = 2 * ALONG_Z
    return [list(range(first, length, step)) for first in range(step)]


def z_groups():
    length = lax.axis_size("cand")
    step = 2 * ALONG_Z
    return [list(range(x, x + step)) for x in range(0, length, step)]


def to_outer(shard):
    length = lax.axis_size("cand")
    pairs = [(i, (i + (1 if i % 2 else length - 1)) % length) for i in range(length)]
    return lax.ppermute(shard, "cand", pairs)


def opposed(shard, by):
    chips, parts = lax.axis_size("cand"), lax.axis_size("mp")
    pairs = []
    for device in range(chips):
        signed = by if device % 2 == 0 else -by
        for part in range(parts):
            pairs.append((device * parts + part, device * parts + (part + signed) % parts))
    return lax.ppermute(shard, ("cand", "mp"), pairs)


def pick_kernel(table, passages, inner, outer, kept):
    me = lax.axis_index("cand")
    devices = lax.axis_size("cand")
    slots, length, width = passages.shape
    row = lax.broadcasted_iota(jnp.int32, (16, width), 0)
    lane = lax.broadcasted_iota(jnp.int32, (16, width), 1)
    number = [jnp.int32(0)] * 3
    core = lax.rem(me, 2)
    inward = jnp.where(core == 0, 1, devices - 1)
    outward = jnp.where(core == 0, devices - 1, 1)
    for slot in range(slots):
        ahead = lax.rem(table[0, slot] - me + devices, devices)
        facts = jnp.where(lane < width // 2, table[1, slot], table[2, slot]).astype(F32)
        tail = passages[slot, length - 16 :, :].astype(F32)
        tail = jnp.where(row == 15, facts, tail).astype(BF16)
        for which, (wanted, target) in enumerate(((inward, inner), (outward, outer), (0, kept))):
            hit = ahead == wanted
            place = jnp.minimum(number[which], target.shape[0] - 1)

            @pl.when(hit)
            def _():
                target[place, : length - 16, :] = passages[slot, : length - 16, :]
                target[place, length - 16 :, :] = tail

            number[which] = number[which] + hit.astype(jnp.int32)


def pick(table, passages):
    slots, length, width = passages.shape
    smem = pl.BlockSpec(memory_space=pltpu.SMEM)
    vmem = pl.BlockSpec(memory_space=pltpu.VMEM)
    shape = lambda n: jax.ShapeDtypeStruct((n, length, width), BF16)
    return pl.pallas_call(
        pick_kernel,
        out_shape=(shape(2), shape(2), shape(slots - 4)),
        in_specs=[smem, vmem],
        out_specs=(vmem, vmem, vmem),
        compiler_params=pltpu.CompilerParams(vmem_limit_bytes=VMEM_LIMIT),
    )(table, passages)


def copy_kernel(w_qkv, w_out, copies):
    depth = w_qkv.shape[1]
    for copy in range(copies.shape[0]):
        for part in range(3):
            copies[copy, part * depth : (part + 1) * depth, :] = w_qkv[part]
        copies[copy, 3 * depth :, :] = w_out[...]


def copied(w_qkv, w_out, number):
    vmem = pl.BlockSpec(memory_space=pltpu.VMEM)
    depth = 3 * w_qkv.shape[1] + w_out.shape[0]
    return pl.pallas_call(
        copy_kernel,
        out_shape=jax.ShapeDtypeStruct((number, depth, w_qkv.shape[2]), BF16),
        in_specs=[vmem, vmem],
        out_specs=vmem,
        compiler_params=pltpu.CompilerParams(vmem_limit_bytes=VMEM_LIMIT),
    )(w_qkv, w_out)


def pack_kernel(inner, kept, outer, packed, facts):
    rows = packed.shape[0]
    length = kept.shape[1]
    first = lax.rem(lax.axis_index("cand"), 2) == 0
    blocks = (
        [jnp.where(first, outer[i], inner[i]) for i in range(outer.shape[0])]
        + [kept[i] for i in range(kept.shape[0])]
        + [jnp.where(first, inner[i], outer[i]) for i in range(inner.shape[0])]
    )
    position = lax.broadcasted_iota(jnp.int32, (rows, length), 0)
    offset = lax.broadcasted_iota(jnp.int32, (rows, length), 1)
    start = jnp.zeros((1, length), jnp.int32)
    total = jnp.zeros(packed.shape, F32)
    for slot, block in enumerate(blocks):
        fact = block[length - 16 :, :].astype(F32)[15:16, :]
        facts[slot : slot + 1, :] = fact
        count = fact[:, :length].astype(jnp.int32)
        chosen = (position == start + offset) & (offset < count)
        total = total + jnp.dot(
            chosen.astype(F32).astype(BF16), block, preferred_element_type=F32
        )
        start = start + count
    packed[...] = total.astype(BF16)


def pack(inner, kept, outer):
    slots = inner.shape[0] + kept.shape[0] + outer.shape[0]
    length, width = kept.shape[1:]
    vmem = pl.BlockSpec(memory_space=pltpu.VMEM)
    return pl.pallas_call(
        pack_kernel,
        out_shape=(
            jax.ShapeDtypeStruct((slots * length // 2, width), BF16),
            jax.ShapeDtypeStruct((slots, width), F32),
        ),
        in_specs=[vmem] * 3,
        out_specs=(vmem, vmem),
        compiler_params=pltpu.CompilerParams(vmem_limit_bytes=VMEM_LIMIT),
    )(inner, kept, outer)


def hold_kernel(source, held):
    held[...] = source[...]


def hold(array):
    vmem = pl.BlockSpec(memory_space=pltpu.VMEM)
    return pl.pallas_call(
        hold_kernel,
        out_shape=jax.ShapeDtypeStruct(array.shape, array.dtype),
        in_specs=[vmem],
        out_specs=vmem,
        compiler_params=pltpu.CompilerParams(vmem_limit_bytes=VMEM_LIMIT),
    )(array)


def project_kernel(place, *refs):
    pieces, gain, weights, facts = refs[:9], *refs[9:12]
    queries, keys, values, residual, sent, rows_in, total, squares = refs[12:]
    step = pl.program_id(0)
    rows = rows_in.shape[0]
    width = rows_in.shape[1] // 2
    half = rows // 2
    for side in range(2):
        lanes = slice(side * width, (side + 1) * width)
        wanted = place[2 * step + side]
        for number in range(7):

            @pl.when(wanted == number)
            def _():
                rows_in[:, lanes] = pieces[number][...]

        @pl.when(wanted == 7)
        def _():
            rows_in[:half, lanes] = pieces[7][...]
            rows_in[half:, lanes] = pieces[8][...]

    share = residual.shape[0]
    residual[...] = rows_in[pl.ds(pl.multiple_of(place[8] * share, share), share), :]
    x = rows_in[...].astype(F32)
    square = jnp.sum(x * x, axis=1, keepdims=True)
    scaled = (x * gain[step]).astype(BF16)
    depth = weights.shape[3] // 3
    columns = weights.shape[4]
    product = jnp.concatenate(
        [
            jnp.dot(
                scaled,
                weights[:, :, 0, part * depth : (part + 1) * depth, :].reshape(-1, columns),
                preferred_element_type=F32,
            )
            for part in range(3)
        ],
        axis=1,
    )

    @pl.when(step == 0)
    def _():
        total[...] = product
        squares[...] = square

    @pl.when(step > 0)
    def _():
        total[...] += product
        squares[...] += square

    @pl.when(step == 3)
    def _():
        inverse = lax.rsqrt(squares[...] / (8 * width) + EPS)
        done = [
            (total[:, part * columns : (part + 1) * columns] * inverse).astype(BF16)
            for part in range(3)
        ]
        queries[...], keys[...], values[...] = done
        slots = facts.shape[0]
        slot_of = lax.broadcasted_iota(jnp.int32, (2 * slots, rows), 0) % slots
        position = lax.broadcasted_iota(jnp.int32, (2 * slots, rows), 1)
        start = jnp.zeros((1, rows), jnp.int32)
        first = jnp.zeros((2 * slots, rows), jnp.int32)
        asked = jnp.zeros((2 * slots, HD), jnp.int32)
        for slot in range(slots):
            here = slot_of == slot
            first = jnp.where(here, start, first)
            asked = jnp.where(
                here[:, :HD],
                facts[slot : slot + 1, width // 2 : width // 2 + HD].astype(jnp.int32),
                asked,
            )
            start = start + facts[slot : slot + 1, :rows].astype(jnp.int32)
        chosen = (first == position).astype(F32).astype(BF16)
        mark = (asked == position[:, :HD]).astype(F32).astype(BF16)
        key_rows = jnp.dot(chosen, done[1], preferred_element_type=F32).astype(BF16)
        value_rows = jnp.dot(chosen, done[2], preferred_element_type=F32).astype(BF16)
        for copy in range(sent.shape[0] // (2 * slots)):
            there = slice(copy * 2 * slots, (copy + 1) * 2 * slots)
            sent[there, :columns] = key_rows
            sent[there, columns : 2 * columns] = value_rows
            sent[there, 2 * columns :] = mark


def project(place, pieces, gain, weights, facts, copies):
    rows, width = pieces[0].shape
    along_z, cores, along_x = weights.shape[:3]
    columns = 2 * HD
    resident = pl.BlockSpec(memory_space=pltpu.VMEM)
    out = lambda *shape: (
        jax.ShapeDtypeStruct(shape, BF16),
        pl.BlockSpec(shape, lambda r, place: (0, 0)),
    )
    outs = [out(rows, columns)] * 3
    outs.append(
        (
            jax.ShapeDtypeStruct((rows // 8, 8 * width), BF16),
            pl.BlockSpec((rows // 8, 2 * width), lambda r, place: (0, r)),
        )
    )
    outs.append(out(copies * facts.shape[0], 2 * columns + HD))
    weight = pl.BlockSpec(
        (along_z, cores, 1, 192, columns), lambda r, place: (0, 0, r, 0, 0)
    )
    return pl.pallas_call(
        project_kernel,
        out_shape=tuple(o[0] for o in outs),
        grid_spec=pltpu.PrefetchScalarGridSpec(
            num_scalar_prefetch=1,
            grid=(along_x,),
            in_specs=[resident for _ in pieces]
            + [
                resident,
                weight,
                resident,
            ],
            out_specs=tuple(o[1] for o in outs),
            scratch_shapes=[
                pltpu.VMEM((rows, 2 * width), BF16),
                pltpu.VMEM((rows, 3 * columns), F32),
                pltpu.VMEM((rows, 1), F32),
            ],
        ),
        compiler_params=pltpu.CompilerParams(vmem_limit_bytes=VMEM_LIMIT),
    )(place, *pieces, gain, weights, facts)


def attend_kernel(*refs):
    queries, keys, values, near, far, facts, weights, out, held, done, arrived, left = refs
    rows, columns = near.shape[0], 2 * HD
    along_z, cores, along_x, depth, _ = held.shape
    width = along_z * cores * depth
    fetches = [
        pltpu.make_async_copy(
            weights.at[:, :, x, pl.ds(3 * depth, depth), :], held.at[:, :, x], arrived.at[x]
        )
        for x in range(along_x)
    ]
    for fetch in fetches:
        fetch.start()
    slots = facts.shape[0]
    half = facts.shape[1] // 2
    here = lax.axis_index("cand") // 2 * slots
    down = lax.broadcasted_iota(jnp.int32, (rows, rows), 0)
    across = lax.broadcasted_iota(jnp.int32, (rows, rows), 1)
    slot_down = jnp.zeros((rows, rows), jnp.int32)
    slot_across = jnp.zeros((rows, rows), jnp.int32)
    end = jnp.zeros((1, rows), jnp.int32)
    for slot in range(slots):
        end = end + facts[slot : slot + 1, :rows].astype(jnp.int32)
        if slot < slots - 1:
            slot_down = slot_down + (down >= end).astype(jnp.int32)
            slot_across = slot_across + (across >= end).astype(jnp.int32)
    asked = jnp.zeros((rows, HD), jnp.int32)
    for slot in range(slots):
        asked = jnp.where(
            slot_down[:, :HD] == slot,
            facts[slot : slot + 1, half : half + HD].astype(jnp.int32),
            asked,
        )
    local = ((slot_down == slot_across) & (down < end) & (across < end)) | (down == across)
    mark = (asked == across[:, :HD]).astype(F32).astype(BF16)
    same = lambda other: lax.dot_general(
        mark, other[:, 2 * columns :], NT, preferred_element_type=F32
    ) > 0.5
    masks = [local, same(near) & (across != here + slot_down), same(far)]
    scale = 1.0 / math.sqrt(HD)
    heads = []
    for head in range(columns // HD):
        lanes = slice(head * HD, (head + 1) * HD)
        value_lanes = slice(columns + head * HD, columns + (head + 1) * HD)
        query = queries[:, lanes]
        scores = [
            jnp.where(
                mask,
                lax.dot_general(query, key, NT, preferred_element_type=F32) * scale,
                NEGATIVE,
            )
            for mask, key in zip(masks, (keys[:, lanes], near[:, lanes], far[:, lanes]))
        ]
        peak = jnp.maximum(jnp.maximum(scores[0], scores[1]), scores[2])
        peak = jnp.max(peak, axis=1, keepdims=True)
        raised = [jnp.exp(score - peak) for score in scores]
        bottom = jnp.sum(raised[0] + raised[1] + raised[2], axis=1, keepdims=True)
        top = jnp.zeros((rows, HD), F32)
        for part, value in zip(
            raised, (values[:, lanes], near[:, value_lanes], far[:, value_lanes])
        ):
            top = top + jnp.dot(part.astype(BF16), value, preferred_element_type=F32)
        heads.append(jnp.where(down[:, :HD] < end[:, :HD], top / bottom, 0.0).astype(BF16))
    attended = jnp.concatenate(heads, axis=1)
    leaving = []
    for x in range(along_x):
        fetches[x].wait()
        for z in range(0, along_z, 2):
            block = held[z : z + 2, :, x].reshape(-1, columns)
            at = x * width + z * cores * depth
            done[:, at : at + 2 * cores * depth] = lax.dot_general(
                attended, block, NT, preferred_element_type=F32
            ).astype(BF16)
        lanes = pl.ds(x * width, width)
        leaving.append(pltpu.make_async_copy(done.at[:, lanes], out.at[:, lanes], left.at[x]))
        leaving[x].start()
    for copy in leaving:
        copy.wait()


def attend(queries, keys, values, near, far, facts, weights):
    along_z, cores, along_x, depth, inner = weights.shape
    depth = depth // 4
    rows = queries.shape[0]
    columns = along_z * along_x * cores * depth
    vmem = pl.BlockSpec(memory_space=pltpu.VMEM)
    anywhere = pl.BlockSpec(memory_space=pl.ANY)
    return pl.pallas_call(
        attend_kernel,
        out_shape=jax.ShapeDtypeStruct((rows, columns), BF16),
        in_specs=[vmem] * 6 + [anywhere],
        out_specs=anywhere,
        scratch_shapes=[
            pltpu.VMEM((along_z, cores, along_x, depth, inner), BF16),
            pltpu.VMEM((rows, columns), BF16),
            pltpu.SemaphoreType.DMA((along_x,)),
            pltpu.SemaphoreType.DMA((along_x,)),
        ],
        compiler_params=pltpu.CompilerParams(vmem_limit_bytes=VMEM_LIMIT),
    )(queries, keys, values, near, far, facts, weights)


def add_kernel(residual, summed, out):
    out[...] = (residual[...].astype(F32) + summed[...].astype(F32)).astype(BF16)


def add(residual, summed):
    rows, width = residual.shape
    half = pl.BlockSpec((rows, width // 2), lambda i: (0, i))
    return pl.pallas_call(
        add_kernel,
        out_shape=jax.ShapeDtypeStruct(residual.shape, BF16),
        grid=(2,),
        in_specs=[half, half],
        out_specs=half,
        compiler_params=pltpu.CompilerParams(vmem_limit_bytes=VMEM_LIMIT),
    )(residual, summed)


def shards(passages, norm_gain, w_qkv, w_out, counts, owners, query_of):
    devices = lax.axis_size("cand")
    parts = lax.axis_size("mp")
    me = lax.axis_index("mp")
    core = lax.rem(lax.axis_index("cand"), 2)
    along_x = devices // (2 * ALONG_Z)
    with jax.named_scope("weights_gathered"):
        copies = copied(w_qkv, w_out.T, along_x)
        from_x = lax.all_to_all(
            copies.reshape(-1, 2 * HD), "cand", 0, 0, tiled=True, axis_index_groups=x_groups()
        ).reshape(copies.shape)
        weights = lax.all_gather(from_x, "cand", axis_index_groups=z_groups())
        weights = weights.reshape((ALONG_Z, 2) + from_x.shape)
    with jax.named_scope("passages_handed_over"):
        inner, outer, kept = pick(jnp.stack([owners, counts, query_of]), passages)
        from_x, inner, outer = lax.optimization_barrier((from_x, inner, outer))
        inner, outer = to_sibling(inner), to_outer(outer)
    with jax.named_scope("passages_packed"):
        packed, facts = pack(inner, kept, outer)
    with jax.named_scope("features_gathered"):
        half = packed.shape[0] // 2
        third, fourth = opposed(packed, 2), opposed(packed, -2)
        first, second = opposed(packed, 1), opposed(packed, -1)
        gain = hold(norm_gain.reshape(along_x, 1, -1))
        first, second, third, fourth, gain = lax.optimization_barrier(
            (first, second, third, fourth, gain)
        )
        fifth, sixth = opposed(third, 1), opposed(fourth, -1)
        last = (opposed(third[:half], 2), opposed(fourth[half:], -2))
        pieces = [packed, first, second, third, fourth, fifth, sixth, *last]
    away = (jnp.arange(parts, dtype=jnp.int32) - me) * (1 - 2 * core)
    away = lax.rem(away + parts, parts)
    place = jnp.where(away < parts // 2, 2 * away, 2 * parts - 1 - 2 * away)
    place = jnp.concatenate([place, me[None]]).astype(jnp.int32)
    queries, keys, values, residual, sent = project(
        place, pieces, gain, weights, facts, devices // 2
    )
    with jax.named_scope("interaction_gathered"):
        near = lax.all_to_all(
            sent, "cand", 0, 0, tiled=True, axis_index_groups=same_core_groups()
        )
        far = to_sibling(near)
    partial = attend(queries, keys, values, near, far, facts, weights)
    with jax.named_scope("heads_summed"):
        summed = lax.psum_scatter(partial, "mp", scatter_dimension=0, tiled=True)
    return add(residual, summed)


def solution(mesh):
    in_specs = (
        P("cand", None, "mp"),
        P(),
        P(None, "cand", "mp"),
        P("mp", "cand"),
        P("cand"),
        P("cand"),
        P("cand"),
    )
    out_specs = P(("cand", "mp"), None)
    return jax.shard_map(shards, mesh=mesh, in_specs=in_specs, out_specs=out_specs, check_vma=False)
```

```python
import math

import jax
import jax.numpy as jnp
from jax import lax
from jax.experimental import pallas as pl
from jax.experimental.pallas import tpu as pltpu
from jax.sharding import PartitionSpec as P

HD = 128
EPS = 1e-05
NEGATIVE = -1e30
VMEM_LIMIT = 48 * 1024 * 1024
F32 = jnp.float32
BF16 = jnp.bfloat16
NT = (((1,), (1,)), ((), ()))


def along(shard, axis, by):
    length = lax.axis_size(axis)
    return lax.ppermute(shard, axis, [(i, (i + by) % length) for i in range(length)])


def to_sibling(shard):
    length = lax.axis_size("cand")
    return lax.ppermute(shard, "cand", [(i, i ^ 1) for i in range(length)])


def same_core_groups():
    length = lax.axis_size("cand")
    return [list(range(core, length, 2)) for core in range(2)]


ALONG_Z = 8


def x_groups():
    length = lax.axis_size("cand")
    step = 2 * ALONG_Z
    return [list(range(first, length, step)) for first in range(step)]


def z_groups():
    length = lax.axis_size("cand")
    step = 2 * ALONG_Z
    return [list(range(x, x + step)) for x in range(0, length, step)]


def to_outer(shard):
    length = lax.axis_size("cand")
    pairs = [(i, (i + (1 if i % 2 else length - 1)) % length) for i in range(length)]
    return lax.ppermute(shard, "cand", pairs)


def opposed(shard, by):
    chips, parts = lax.axis_size("cand"), lax.axis_size("mp")
    pairs = []
    for device in range(chips):
        signed = by if device % 2 == 0 else -by
        for part in range(parts):
            pairs.append((device * parts + part, device * parts + (part + signed) % parts))
    return lax.ppermute(shard, ("cand", "mp"), pairs)


def pick_kernel(table, passages, inner, outer, kept):
    me = lax.axis_index("cand")
    devices = lax.axis_size("cand")
    slots, length, width = passages.shape
    row = lax.broadcasted_iota(jnp.int32, (16, width), 0)
    lane = lax.broadcasted_iota(jnp.int32, (16, width), 1)
    number = [jnp.int32(0)] * 3
    core = lax.rem(me, 2)
    inward = jnp.where(core == 0, 1, devices - 1)
    outward = jnp.where(core == 0, devices - 1, 1)
    for slot in range(slots):
        ahead = lax.rem(table[0, slot] - me + devices, devices)
        facts = jnp.where(lane < width // 2, table[1, slot], table[2, slot]).astype(F32)
        tail = passages[slot, length - 16 :, :].astype(F32)
        tail = jnp.where(row == 15, facts, tail).astype(BF16)
        for which, (wanted, target) in enumerate(((inward, inner), (outward, outer), (0, kept))):
            hit = ahead == wanted
            place = jnp.minimum(number[which], target.shape[0] - 1)

            @pl.when(hit)
            def _():
                target[place, : length - 16, :] = passages[slot, : length - 16, :]
                target[place, length - 16 :, :] = tail

            number[which] = number[which] + hit.astype(jnp.int32)


def pick(table, passages):
    slots, length, width = passages.shape
    smem = pl.BlockSpec(memory_space=pltpu.SMEM)
    vmem = pl.BlockSpec(memory_space=pltpu.VMEM)
    shape = lambda n: jax.ShapeDtypeStruct((n, length, width), BF16)
    return pl.pallas_call(
        pick_kernel,
        out_shape=(shape(2), shape(2), shape(slots - 4)),
        in_specs=[smem, vmem],
        out_specs=(vmem, vmem, vmem),
        compiler_params=pltpu.CompilerParams(vmem_limit_bytes=VMEM_LIMIT),
    )(table, passages)


def copy_kernel(w_qkv, w_out, copies):
    depth = w_qkv.shape[1]
    for copy in range(copies.shape[0]):
        for part in range(3):
            copies[copy, part * depth : (part + 1) * depth, :] = w_qkv[part]
        copies[copy, 3 * depth :, :] = w_out[...]


def copied(w_qkv, w_out, number):
    vmem = pl.BlockSpec(memory_space=pltpu.VMEM)
    depth = 3 * w_qkv.shape[1] + w_out.shape[0]
    return pl.pallas_call(
        copy_kernel,
        out_shape=jax.ShapeDtypeStruct((number, depth, w_qkv.shape[2]), BF16),
        in_specs=[vmem, vmem],
        out_specs=vmem,
        compiler_params=pltpu.CompilerParams(vmem_limit_bytes=VMEM_LIMIT),
    )(w_qkv, w_out)


def pack_kernel(inner, kept, outer, packed, facts):
    rows = packed.shape[0]
    length = kept.shape[1]
    first = lax.rem(lax.axis_index("cand"), 2) == 0
    blocks = (
        [jnp.where(first, outer[i], inner[i]) for i in range(outer.shape[0])]
        + [kept[i] for i in range(kept.shape[0])]
        + [jnp.where(first, inner[i], outer[i]) for i in range(inner.shape[0])]
    )
    position = lax.broadcasted_iota(jnp.int32, (rows, length), 0)
    offset = lax.broadcasted_iota(jnp.int32, (rows, length), 1)
    start = jnp.zeros((1, length), jnp.int32)
    total = jnp.zeros(packed.shape, F32)
    for slot, block in enumerate(blocks):
        fact = block[length - 16 :, :].astype(F32)[15:16, :]
        facts[slot : slot + 1, :] = fact
        count = fact[:, :length].astype(jnp.int32)
        chosen = (position == start + offset) & (offset < count)
        total = total + jnp.dot(
            chosen.astype(F32).astype(BF16), block, preferred_element_type=F32
        )
        start = start + count
    packed[...] = total.astype(BF16)


def pack(inner, kept, outer):
    slots = inner.shape[0] + kept.shape[0] + outer.shape[0]
    length, width = kept.shape[1:]
    vmem = pl.BlockSpec(memory_space=pltpu.VMEM)
    return pl.pallas_call(
        pack_kernel,
        out_shape=(
            jax.ShapeDtypeStruct((slots * length // 2, width), BF16),
            jax.ShapeDtypeStruct((slots, width), F32),
        ),
        in_specs=[vmem] * 3,
        out_specs=(vmem, vmem),
        compiler_params=pltpu.CompilerParams(vmem_limit_bytes=VMEM_LIMIT),
    )(inner, kept, outer)


def hold_kernel(source, held):
    held[...] = source[...]


def hold(array):
    vmem = pl.BlockSpec(memory_space=pltpu.VMEM)
    return pl.pallas_call(
        hold_kernel,
        out_shape=jax.ShapeDtypeStruct(array.shape, array.dtype),
        in_specs=[vmem],
        out_specs=vmem,
        compiler_params=pltpu.CompilerParams(vmem_limit_bytes=VMEM_LIMIT),
    )(array)


def project_kernel(place, *refs):
    pieces, gain, weights, facts = refs[:9], *refs[9:12]
    queries, keys, values, residual, sent, rows_in, total, squares = refs[12:]
    step = pl.program_id(0)
    rows = rows_in.shape[0]
    width = rows_in.shape[1] // 2
    half = rows // 2
    for side in range(2):
        lanes = slice(side * width, (side + 1) * width)
        wanted = place[2 * step + side]
        for number in range(7):

            @pl.when(wanted == number)
            def _():
                rows_in[:, lanes] = pieces[number][...]

        @pl.when(wanted == 7)
        def _():
            rows_in[:half, lanes] = pieces[7][...]
            rows_in[half:, lanes] = pieces[8][...]

    share = residual.shape[0]
    residual[...] = rows_in[pl.ds(pl.multiple_of(place[8] * share, share), share), :]
    x = rows_in[...].astype(F32)
    square = jnp.sum(x * x, axis=1, keepdims=True)
    scaled = (x * gain[step]).astype(BF16)
    depth = weights.shape[3] // 3
    columns = weights.shape[4]
    product = jnp.concatenate(
        [
            jnp.dot(
                scaled,
                weights[:, :, 0, part * depth : (part + 1) * depth, :].reshape(-1, columns),
                preferred_element_type=F32,
            )
            for part in range(3)
        ],
        axis=1,
    )

    @pl.when(step == 0)
    def _():
        total[...] = product
        squares[...] = square

    @pl.when(step > 0)
    def _():
        total[...] += product
        squares[...] += square

    @pl.when(step == 3)
    def _():
        inverse = lax.rsqrt(squares[...] / (8 * width) + EPS)
        done = [
            (total[:, part * columns : (part + 1) * columns] * inverse).astype(BF16)
            for part in range(3)
        ]
        queries[...], keys[...], values[...] = done
        slots = facts.shape[0]
        slot_of = lax.broadcasted_iota(jnp.int32, (2 * slots, rows), 0) % slots
        position = lax.broadcasted_iota(jnp.int32, (2 * slots, rows), 1)
        start = jnp.zeros((1, rows), jnp.int32)
        first = jnp.zeros((2 * slots, rows), jnp.int32)
        asked = jnp.zeros((2 * slots, HD), jnp.int32)
        for slot in range(slots):
            here = slot_of == slot
            first = jnp.where(here, start, first)
            asked = jnp.where(
                here[:, :HD],
                facts[slot : slot + 1, width // 2 : width // 2 + HD].astype(jnp.int32),
                asked,
            )
            start = start + facts[slot : slot + 1, :rows].astype(jnp.int32)
        chosen = (first == position).astype(F32).astype(BF16)
        mark = (asked == position[:, :HD]).astype(F32).astype(BF16)
        key_rows = jnp.dot(chosen, done[1], preferred_element_type=F32).astype(BF16)
        value_rows = jnp.dot(chosen, done[2], preferred_element_type=F32).astype(BF16)
        for copy in range(sent.shape[0] // (2 * slots)):
            there = slice(copy * 2 * slots, (copy + 1) * 2 * slots)
            sent[there, :columns] = key_rows
            sent[there, columns : 2 * columns] = value_rows
            sent[there, 2 * columns :] = mark


def project(place, pieces, gain, weights, facts, copies):
    rows, width = pieces[0].shape
    along_z, cores, along_x = weights.shape[:3]
    columns = 2 * HD
    resident = pl.BlockSpec(memory_space=pltpu.VMEM)
    out = lambda *shape: (
        jax.ShapeDtypeStruct(shape, BF16),
        pl.BlockSpec(shape, lambda r, place: (0, 0)),
    )
    outs = [out(rows, columns)] * 3
    outs.append(
        (
            jax.ShapeDtypeStruct((rows // 8, 8 * width), BF16),
            pl.BlockSpec((rows // 8, 2 * width), lambda r, place: (0, r)),
        )
    )
    outs.append(out(copies * facts.shape[0], 2 * columns + HD))
    weight = pl.BlockSpec(
        (along_z, cores, 1, 192, columns), lambda r, place: (0, 0, r, 0, 0)
    )
    return pl.pallas_call(
        project_kernel,
        out_shape=tuple(o[0] for o in outs),
        grid_spec=pltpu.PrefetchScalarGridSpec(
            num_scalar_prefetch=1,
            grid=(along_x,),
            in_specs=[resident for _ in pieces]
            + [
                resident,
                weight,
                resident,
            ],
            out_specs=tuple(o[1] for o in outs),
            scratch_shapes=[
                pltpu.VMEM((rows, 2 * width), BF16),
                pltpu.VMEM((rows, 3 * columns), F32),
                pltpu.VMEM((rows, 1), F32),
            ],
        ),
        compiler_params=pltpu.CompilerParams(vmem_limit_bytes=VMEM_LIMIT),
    )(place, *pieces, gain, weights, facts)


def attend_kernel(*refs):
    queries, keys, values, near, far, facts, residual, weights, out, held, done, arrived, left = refs
    share = residual.shape[0]
    own = pl.ds(pl.multiple_of(lax.axis_index("mp") * share, share), share)
    rows, columns = near.shape[0], 2 * HD
    along_z, cores, along_x, depth, _ = held.shape
    width = along_z * cores * depth
    fetches = [
        pltpu.make_async_copy(
            weights.at[:, :, x, pl.ds(3 * depth, depth), :], held.at[:, :, x], arrived.at[x]
        )
        for x in range(along_x)
    ]
    for fetch in fetches:
        fetch.start()
    slots = facts.shape[0]
    half = facts.shape[1] // 2
    here = lax.axis_index("cand") // 2 * slots
    down = lax.broadcasted_iota(jnp.int32, (rows, rows), 0)
    across = lax.broadcasted_iota(jnp.int32, (rows, rows), 1)
    slot_down = jnp.zeros((rows, rows), jnp.int32)
    slot_across = jnp.zeros((rows, rows), jnp.int32)
    end = jnp.zeros((1, rows), jnp.int32)
    for slot in range(slots):
        end = end + facts[slot : slot + 1, :rows].astype(jnp.int32)
        if slot < slots - 1:
            slot_down = slot_down + (down >= end).astype(jnp.int32)
            slot_across = slot_across + (across >= end).astype(jnp.int32)
    asked = jnp.zeros((rows, HD), jnp.int32)
    for slot in range(slots):
        asked = jnp.where(
            slot_down[:, :HD] == slot,
            facts[slot : slot + 1, half : half + HD].astype(jnp.int32),
            asked,
        )
    local = ((slot_down == slot_across) & (down < end) & (across < end)) | (down == across)
    mark = (asked == across[:, :HD]).astype(F32).astype(BF16)
    same = lambda other: lax.dot_general(
        mark, other[:, 2 * columns :], NT, preferred_element_type=F32
    ) > 0.5
    masks = [local, same(near) & (across != here + slot_down), same(far)]
    scale = 1.0 / math.sqrt(HD)
    heads = []
    for head in range(columns // HD):
        lanes = slice(head * HD, (head + 1) * HD)
        value_lanes = slice(columns + head * HD, columns + (head + 1) * HD)
        query = queries[:, lanes]
        scores = [
            jnp.where(
                mask,
                lax.dot_general(query, key, NT, preferred_element_type=F32) * scale,
                NEGATIVE,
            )
            for mask, key in zip(masks, (keys[:, lanes], near[:, lanes], far[:, lanes]))
        ]
        peak = jnp.maximum(jnp.maximum(scores[0], scores[1]), scores[2])
        peak = jnp.max(peak, axis=1, keepdims=True)
        raised = [jnp.exp(score - peak) for score in scores]
        bottom = jnp.sum(raised[0] + raised[1] + raised[2], axis=1, keepdims=True)
        top = jnp.zeros((rows, HD), F32)
        for part, value in zip(
            raised, (values[:, lanes], near[:, value_lanes], far[:, value_lanes])
        ):
            top = top + jnp.dot(part.astype(BF16), value, preferred_element_type=F32)
        heads.append(jnp.where(down[:, :HD] < end[:, :HD], top / bottom, 0.0).astype(BF16))
    attended = jnp.concatenate(heads, axis=1)
    leaving = []
    for x in range(along_x):
        fetches[x].wait()
        for z in range(0, along_z, 2):
            block = held[z : z + 2, :, x].reshape(-1, columns)
            at = x * width + z * cores * depth
            done[:, at : at + 2 * cores * depth] = lax.dot_general(
                attended, block, NT, preferred_element_type=F32
            ).astype(BF16)
        lanes = pl.ds(x * width, width)
        mixed = done[own, lanes].astype(F32) + residual[:, lanes].astype(F32)
        done[own, lanes] = mixed.astype(BF16)
        leaving.append(pltpu.make_async_copy(done.at[:, lanes], out.at[:, lanes], left.at[x]))
        leaving[x].start()
    for copy in leaving:
        copy.wait()


def attend(queries, keys, values, near, far, facts, residual, weights):
    along_z, cores, along_x, depth, inner = weights.shape
    depth = depth // 4
    rows = queries.shape[0]
    columns = along_z * along_x * cores * depth
    vmem = pl.BlockSpec(memory_space=pltpu.VMEM)
    anywhere = pl.BlockSpec(memory_space=pl.ANY)
    return pl.pallas_call(
        attend_kernel,
        out_shape=jax.ShapeDtypeStruct((rows, columns), BF16),
        in_specs=[vmem] * 7 + [anywhere],
        out_specs=anywhere,
        scratch_shapes=[
            pltpu.VMEM((along_z, cores, along_x, depth, inner), BF16),
            pltpu.VMEM((rows, columns), BF16),
            pltpu.SemaphoreType.DMA((along_x,)),
            pltpu.SemaphoreType.DMA((along_x,)),
        ],
        compiler_params=pltpu.CompilerParams(vmem_limit_bytes=VMEM_LIMIT),
    )(queries, keys, values, near, far, facts, residual, weights)


def shards(passages, norm_gain, w_qkv, w_out, counts, owners, query_of):
    devices = lax.axis_size("cand")
    parts = lax.axis_size("mp")
    me = lax.axis_index("mp")
    core = lax.rem(lax.axis_index("cand"), 2)
    along_x = devices // (2 * ALONG_Z)
    with jax.named_scope("weights_gathered"):
        copies = copied(w_qkv, w_out.T, along_x)
        from_x = lax.all_to_all(
            copies.reshape(-1, 2 * HD), "cand", 0, 0, tiled=True, axis_index_groups=x_groups()
        ).reshape(copies.shape)
        weights = lax.all_gather(from_x, "cand", axis_index_groups=z_groups())
        weights = weights.reshape((ALONG_Z, 2) + from_x.shape)
    with jax.named_scope("passages_handed_over"):
        inner, outer, kept = pick(jnp.stack([owners, counts, query_of]), passages)
        from_x, inner, outer = lax.optimization_barrier((from_x, inner, outer))
        inner, outer = to_sibling(inner), to_outer(outer)
    with jax.named_scope("passages_packed"):
        packed, facts = pack(inner, kept, outer)
    with jax.named_scope("features_gathered"):
        half = packed.shape[0] // 2
        third, fourth = opposed(packed, 2), opposed(packed, -2)
        first, second = opposed(packed, 1), opposed(packed, -1)
        gain = hold(norm_gain.reshape(along_x, 1, -1))
        first, second, third, fourth, gain = lax.optimization_barrier(
            (first, second, third, fourth, gain)
        )
        fifth, sixth = opposed(third, 1), opposed(fourth, -1)
        last = (opposed(third[:half], 2), opposed(fourth[half:], -2))
        pieces = [packed, first, second, third, fourth, fifth, sixth, *last]
    away = (jnp.arange(parts, dtype=jnp.int32) - me) * (1 - 2 * core)
    away = lax.rem(away + parts, parts)
    place = jnp.where(away < parts // 2, 2 * away, 2 * parts - 1 - 2 * away)
    place = jnp.concatenate([place, me[None]]).astype(jnp.int32)
    queries, keys, values, residual, sent = project(
        place, pieces, gain, weights, facts, devices // 2
    )
    with jax.named_scope("interaction_gathered"):
        near = lax.all_to_all(
            sent, "cand", 0, 0, tiled=True, axis_index_groups=same_core_groups()
        )
        far = to_sibling(near)
    partial = attend(queries, keys, values, near, far, facts, residual, weights)
    with jax.named_scope("heads_summed"):
        return lax.psum_scatter(partial, "mp", scatter_dimension=0, tiled=True)


def solution(mesh):
    in_specs = (
        P("cand", None, "mp"),
        P(),
        P(None, "cand", "mp"),
        P("mp", "cand"),
        P("cand"),
        P("cand"),
        P("cand"),
    )
    out_specs = P(("cand", "mp"), None)
    return jax.shard_map(shards, mesh=mesh, in_specs=in_specs, out_specs=out_specs, check_vma=False)
```

```python
import math

import jax
import jax.numpy as jnp
from jax import lax
from jax.experimental import pallas as pl
from jax.experimental.pallas import tpu as pltpu
from jax.sharding import PartitionSpec as P

HD = 128
EPS = 1e-05
NEGATIVE = -1e30
VMEM_LIMIT = 48 * 1024 * 1024
F32 = jnp.float32
BF16 = jnp.bfloat16
NT = (((1,), (1,)), ((), ()))


def along(shard, axis, by):
    length = lax.axis_size(axis)
    return lax.ppermute(shard, axis, [(i, (i + by) % length) for i in range(length)])


def to_sibling(shard):
    length = lax.axis_size("cand")
    return lax.ppermute(shard, "cand", [(i, i ^ 1) for i in range(length)])


def same_core_groups():
    length = lax.axis_size("cand")
    return [list(range(core, length, 2)) for core in range(2)]


ALONG_Z = 8


def x_groups():
    length = lax.axis_size("cand")
    step = 2 * ALONG_Z
    return [list(range(first, length, step)) for first in range(step)]


def z_groups():
    length = lax.axis_size("cand")
    step = 2 * ALONG_Z
    return [list(range(x, x + step)) for x in range(0, length, step)]


def to_outer(shard):
    length = lax.axis_size("cand")
    pairs = [(i, (i + (1 if i % 2 else length - 1)) % length) for i in range(length)]
    return lax.ppermute(shard, "cand", pairs)


def opposed(shard, by):
    chips, parts = lax.axis_size("cand"), lax.axis_size("mp")
    pairs = []
    for device in range(chips):
        signed = by if device % 2 == 0 else -by
        for part in range(parts):
            pairs.append((device * parts + part, device * parts + (part + signed) % parts))
    return lax.ppermute(shard, ("cand", "mp"), pairs)


def pick_kernel(table, passages, inner, outer, kept):
    me = lax.axis_index("cand")
    devices = lax.axis_size("cand")
    slots, length, width = passages.shape
    row = lax.broadcasted_iota(jnp.int32, (16, width), 0)
    lane = lax.broadcasted_iota(jnp.int32, (16, width), 1)
    number = [jnp.int32(0)] * 3
    core = lax.rem(me, 2)
    inward = jnp.where(core == 0, 1, devices - 1)
    outward = jnp.where(core == 0, devices - 1, 1)
    for slot in range(slots):
        ahead = lax.rem(table[0, slot] - me + devices, devices)
        facts = jnp.where(lane < width // 2, table[1, slot], table[2, slot]).astype(F32)
        tail = passages[slot, length - 16 :, :].astype(F32)
        tail = jnp.where(row == 15, facts, tail).astype(BF16)
        for which, (wanted, target) in enumerate(((inward, inner), (outward, outer), (0, kept))):
            hit = ahead == wanted
            place = jnp.minimum(number[which], target.shape[0] - 1)

            @pl.when(hit)
            def _():
                target[place, : length - 16, :] = passages[slot, : length - 16, :]
                target[place, length - 16 :, :] = tail

            number[which] = number[which] + hit.astype(jnp.int32)


def pick(table, passages):
    slots, length, width = passages.shape
    smem = pl.BlockSpec(memory_space=pltpu.SMEM)
    vmem = pl.BlockSpec(memory_space=pltpu.VMEM)
    shape = lambda n: jax.ShapeDtypeStruct((n, length, width), BF16)
    return pl.pallas_call(
        pick_kernel,
        out_shape=(shape(2), shape(2), shape(slots - 4)),
        in_specs=[smem, vmem],
        out_specs=(vmem, vmem, vmem),
        compiler_params=pltpu.CompilerParams(vmem_limit_bytes=VMEM_LIMIT),
    )(table, passages)


def copy_kernel(w_qkv, w_out, copies):
    depth = w_qkv.shape[1]
    for copy in range(copies.shape[0]):
        for part in range(3):
            copies[copy, part * depth : (part + 1) * depth, :] = w_qkv[part]
        copies[copy, 3 * depth :, :] = w_out[...]


def copied(w_qkv, w_out, number):
    vmem = pl.BlockSpec(memory_space=pltpu.VMEM)
    depth = 3 * w_qkv.shape[1] + w_out.shape[0]
    return pl.pallas_call(
        copy_kernel,
        out_shape=jax.ShapeDtypeStruct((number, depth, w_qkv.shape[2]), BF16),
        in_specs=[vmem, vmem],
        out_specs=vmem,
        compiler_params=pltpu.CompilerParams(vmem_limit_bytes=VMEM_LIMIT),
    )(w_qkv, w_out)


def pack_kernel(inner, kept, outer, packed, facts):
    rows = packed.shape[0]
    length = kept.shape[1]
    first = lax.rem(lax.axis_index("cand"), 2) == 0
    blocks = (
        [jnp.where(first, outer[i], inner[i]) for i in range(outer.shape[0])]
        + [kept[i] for i in range(kept.shape[0])]
        + [jnp.where(first, inner[i], outer[i]) for i in range(inner.shape[0])]
    )
    position = lax.broadcasted_iota(jnp.int32, (rows, length), 0)
    offset = lax.broadcasted_iota(jnp.int32, (rows, length), 1)
    start = jnp.zeros((1, length), jnp.int32)
    total = jnp.zeros(packed.shape, F32)
    for slot, block in enumerate(blocks):
        fact = block[length - 16 :, :].astype(F32)[15:16, :]
        facts[slot : slot + 1, :] = fact
        count = fact[:, :length].astype(jnp.int32)
        chosen = (position == start + offset) & (offset < count)
        total = total + jnp.dot(
            chosen.astype(F32).astype(BF16), block, preferred_element_type=F32
        )
        start = start + count
    packed[...] = total.astype(BF16)


def pack(inner, kept, outer):
    slots = inner.shape[0] + kept.shape[0] + outer.shape[0]
    length, width = kept.shape[1:]
    vmem = pl.BlockSpec(memory_space=pltpu.VMEM)
    return pl.pallas_call(
        pack_kernel,
        out_shape=(
            jax.ShapeDtypeStruct((slots * length // 2, width), BF16),
            jax.ShapeDtypeStruct((slots, width), F32),
        ),
        in_specs=[vmem] * 3,
        out_specs=(vmem, vmem),
        compiler_params=pltpu.CompilerParams(vmem_limit_bytes=VMEM_LIMIT),
    )(inner, kept, outer)


def hold_kernel(source, held):
    held[...] = source[...]


def hold(array):
    vmem = pl.BlockSpec(memory_space=pltpu.VMEM)
    return pl.pallas_call(
        hold_kernel,
        out_shape=jax.ShapeDtypeStruct(array.shape, array.dtype),
        in_specs=[vmem],
        out_specs=vmem,
        compiler_params=pltpu.CompilerParams(vmem_limit_bytes=VMEM_LIMIT),
    )(array)


def project_kernel(place, *refs):
    pieces, (gain, facts, weights), outs = refs[:9], refs[9:12], refs[12:17]
    queries, keys, values, residual, sent = outs
    scaled, final, kept, held, arrived = refs[17:]
    rows, width = pieces[0].shape
    parts, share = kept.shape[:2]
    along_z, _, along_x, depth, columns = held.shape
    depth = depth // 3
    fetches = [
        pltpu.make_async_copy(
            weights.at[:, :, x, pl.ds(0, 3 * depth), :], held.at[:, :, x], arrived.at[x]
        )
        for x in range(along_x)
    ]
    for fetch in fetches:
        fetch.start()
    final[: rows // 2, :] = pieces[7][...]
    final[rows // 2 :, :] = pieces[8][...]
    row = pl.ds(pl.multiple_of(place[8] * share, share), share)
    square = jnp.zeros((rows, HD), F32)
    for number, source in enumerate((*pieces[:7], final)):
        at = place[number]
        kept[at] = source[row, :]
        x = source[...].astype(F32)
        scaled[at] = (x * gain[at]).astype(BF16)
        x = x * x
        for lane in range(0, width, HD):
            square = square + x[:, lane : lane + HD]
    for part in range(parts):
        residual[:, part * width : (part + 1) * width] = kept[part]
    totals = [jnp.zeros((rows, columns), F32) for _ in range(3)]
    for x in range(along_x):
        fetches[x].wait()
        for side in range(2):
            strip = slice(side * along_z // 2, (side + 1) * along_z // 2)
            for part in range(3):
                block = held[strip, :, x, part * depth : (part + 1) * depth, :]
                totals[part] = totals[part] + jnp.dot(
                    scaled[2 * x + side],
                    block.reshape(-1, columns),
                    preferred_element_type=F32,
                )
    inverse = lax.rsqrt(jnp.sum(square, axis=1, keepdims=True) / (parts * width) + EPS)
    done = [(total * inverse).astype(BF16) for total in totals]
    queries[...], keys[...], values[...] = done
    slots = facts.shape[0]
    slot_of = lax.broadcasted_iota(jnp.int32, (2 * slots, rows), 0) % slots
    position = lax.broadcasted_iota(jnp.int32, (2 * slots, rows), 1)
    start = jnp.zeros((1, rows), jnp.int32)
    first = jnp.zeros((2 * slots, rows), jnp.int32)
    asked = jnp.zeros((2 * slots, HD), jnp.int32)
    for slot in range(slots):
        here = slot_of == slot
        first = jnp.where(here, start, first)
        asked = jnp.where(
            here[:, :HD],
            facts[slot : slot + 1, width // 2 : width // 2 + HD].astype(jnp.int32),
            asked,
        )
        start = start + facts[slot : slot + 1, :rows].astype(jnp.int32)
    chosen = (first == position).astype(F32).astype(BF16)
    mark = (asked == position[:, :HD]).astype(F32).astype(BF16)
    key_rows = jnp.dot(chosen, done[1], preferred_element_type=F32).astype(BF16)
    value_rows = jnp.dot(chosen, done[2], preferred_element_type=F32).astype(BF16)
    for copy in range(sent.shape[0] // (2 * slots)):
        there = slice(copy * 2 * slots, (copy + 1) * 2 * slots)
        sent[there, :columns] = key_rows
        sent[there, columns : 2 * columns] = value_rows
        sent[there, 2 * columns :] = mark


def project(place, pieces, gain, weights, facts, copies):
    rows, width = pieces[0].shape
    along_z, cores, along_x, depth, columns = weights.shape
    depth = 3 * depth // 4
    parts = gain.shape[0]
    vmem = pl.BlockSpec(memory_space=pltpu.VMEM)
    shape = lambda *sizes: jax.ShapeDtypeStruct(sizes, BF16)
    return pl.pallas_call(
        project_kernel,
        out_shape=(
            shape(rows, columns),
            shape(rows, columns),
            shape(rows, columns),
            shape(rows // parts, parts * width),
            shape(copies * facts.shape[0], 2 * columns + HD),
        ),
        in_specs=[pl.BlockSpec(memory_space=pltpu.SMEM)]
        + [vmem] * 11
        + [pl.BlockSpec(memory_space=pl.ANY)],
        out_specs=(vmem,) * 5,
        scratch_shapes=[
            pltpu.VMEM((parts, rows, width), BF16),
            pltpu.VMEM((rows, width), BF16),
            pltpu.VMEM((parts, rows // parts, width), BF16),
            pltpu.VMEM((along_z, cores, along_x, depth, columns), BF16),
            pltpu.SemaphoreType.DMA((along_x,)),
        ],
        compiler_params=pltpu.CompilerParams(vmem_limit_bytes=VMEM_LIMIT),
    )(place, *pieces, gain, facts, weights)


def attend_kernel(*refs):
    queries, keys, values, near, far, facts, residual, weights, out, held, done, arrived, left = refs
    share = residual.shape[0]
    own = pl.ds(pl.multiple_of(lax.axis_index("mp") * share, share), share)
    rows, columns = near.shape[0], 2 * HD
    along_z, cores, along_x, depth, _ = held.shape
    width = along_z * cores * depth
    fetches = [
        pltpu.make_async_copy(
            weights.at[:, :, x, pl.ds(3 * depth, depth), :], held.at[:, :, x], arrived.at[x]
        )
        for x in range(along_x)
    ]
    for fetch in fetches:
        fetch.start()
    slots = facts.shape[0]
    half = facts.shape[1] // 2
    here = lax.axis_index("cand") // 2 * slots
    down = lax.broadcasted_iota(jnp.int32, (rows, rows), 0)
    across = lax.broadcasted_iota(jnp.int32, (rows, rows), 1)
    slot_down = jnp.zeros((rows, rows), jnp.int32)
    slot_across = jnp.zeros((rows, rows), jnp.int32)
    end = jnp.zeros((1, rows), jnp.int32)
    for slot in range(slots):
        end = end + facts[slot : slot + 1, :rows].astype(jnp.int32)
        if slot < slots - 1:
            slot_down = slot_down + (down >= end).astype(jnp.int32)
            slot_across = slot_across + (across >= end).astype(jnp.int32)
    asked = jnp.zeros((rows, HD), jnp.int32)
    for slot in range(slots):
        asked = jnp.where(
            slot_down[:, :HD] == slot,
            facts[slot : slot + 1, half : half + HD].astype(jnp.int32),
            asked,
        )
    local = ((slot_down == slot_across) & (down < end) & (across < end)) | (down == across)
    mark = (asked == across[:, :HD]).astype(F32).astype(BF16)
    same = lambda other: lax.dot_general(
        mark, other[:, 2 * columns :], NT, preferred_element_type=F32
    ) > 0.5
    masks = [local, same(near) & (across != here + slot_down), same(far)]
    scale = 1.0 / math.sqrt(HD)
    heads = []
    for head in range(columns // HD):
        lanes = slice(head * HD, (head + 1) * HD)
        value_lanes = slice(columns + head * HD, columns + (head + 1) * HD)
        query = queries[:, lanes]
        scores = [
            jnp.where(
                mask,
                lax.dot_general(query, key, NT, preferred_element_type=F32) * scale,
                NEGATIVE,
            )
            for mask, key in zip(masks, (keys[:, lanes], near[:, lanes], far[:, lanes]))
        ]
        peak = jnp.maximum(jnp.maximum(scores[0], scores[1]), scores[2])
        peak = jnp.max(peak, axis=1, keepdims=True)
        raised = [jnp.exp(score - peak) for score in scores]
        bottom = jnp.sum(raised[0] + raised[1] + raised[2], axis=1, keepdims=True)
        top = jnp.zeros((rows, HD), F32)
        for part, value in zip(
            raised, (values[:, lanes], near[:, value_lanes], far[:, value_lanes])
        ):
            top = top + jnp.dot(part.astype(BF16), value, preferred_element_type=F32)
        heads.append(jnp.where(down[:, :HD] < end[:, :HD], top / bottom, 0.0).astype(BF16))
    attended = jnp.concatenate(heads, axis=1)
    leaving = []
    for x in range(along_x):
        fetches[x].wait()
        for z in range(0, along_z, 2):
            block = held[z : z + 2, :, x].reshape(-1, columns)
            at = x * width + z * cores * depth
            done[:, at : at + 2 * cores * depth] = lax.dot_general(
                attended, block, NT, preferred_element_type=F32
            ).astype(BF16)
        lanes = pl.ds(x * width, width)
        mixed = done[own, lanes].astype(F32) + residual[:, lanes].astype(F32)
        done[own, lanes] = mixed.astype(BF16)
        leaving.append(pltpu.make_async_copy(done.at[:, lanes], out.at[:, lanes], left.at[x]))
        leaving[x].start()
    for copy in leaving:
        copy.wait()


def attend(queries, keys, values, near, far, facts, residual, weights):
    along_z, cores, along_x, depth, inner = weights.shape
    depth = depth // 4
    rows = queries.shape[0]
    columns = along_z * along_x * cores * depth
    vmem = pl.BlockSpec(memory_space=pltpu.VMEM)
    anywhere = pl.BlockSpec(memory_space=pl.ANY)
    return pl.pallas_call(
        attend_kernel,
        out_shape=jax.ShapeDtypeStruct((rows, columns), BF16),
        in_specs=[vmem] * 7 + [anywhere],
        out_specs=anywhere,
        scratch_shapes=[
            pltpu.VMEM((along_z, cores, along_x, depth, inner), BF16),
            pltpu.VMEM((rows, columns), BF16),
            pltpu.SemaphoreType.DMA((along_x,)),
            pltpu.SemaphoreType.DMA((along_x,)),
        ],
        compiler_params=pltpu.CompilerParams(vmem_limit_bytes=VMEM_LIMIT),
    )(queries, keys, values, near, far, facts, residual, weights)


def shards(passages, norm_gain, w_qkv, w_out, counts, owners, query_of):
    devices = lax.axis_size("cand")
    parts = lax.axis_size("mp")
    me = lax.axis_index("mp")
    core = lax.rem(lax.axis_index("cand"), 2)
    along_x = devices // (2 * ALONG_Z)
    with jax.named_scope("weights_gathered"):
        copies = copied(w_qkv, w_out.T, along_x)
        from_x = lax.all_to_all(
            copies.reshape(-1, 2 * HD), "cand", 0, 0, tiled=True, axis_index_groups=x_groups()
        ).reshape(copies.shape)
        weights = lax.all_gather(from_x, "cand", axis_index_groups=z_groups())
        weights = weights.reshape((ALONG_Z, 2) + from_x.shape)
    with jax.named_scope("passages_handed_over"):
        inner, outer, kept = pick(jnp.stack([owners, counts, query_of]), passages)
        from_x, inner, outer = lax.optimization_barrier((from_x, inner, outer))
        inner, outer = to_sibling(inner), to_outer(outer)
    with jax.named_scope("passages_packed"):
        packed, facts = pack(inner, kept, outer)
    with jax.named_scope("features_gathered"):
        half = packed.shape[0] // 2
        third, fourth = opposed(packed, 2), opposed(packed, -2)
        first, second = opposed(packed, 1), opposed(packed, -1)
        gain = hold(norm_gain.reshape(parts, 1, -1))
        first, second, third, fourth, gain = lax.optimization_barrier(
            (first, second, third, fourth, gain)
        )
        fifth, sixth = opposed(third, 1), opposed(fourth, -1)
        last = (opposed(third[:half], 2), opposed(fourth[half:], -2))
        pieces = [packed, first, second, third, fourth, fifth, sixth, *last]
    away = jnp.array([0, -1, 1, -2, 2, -3, 3, 4, 0], jnp.int32)
    place = lax.rem(me + parts + away * (1 - 2 * core), parts).astype(jnp.int32)
    queries, keys, values, residual, sent = project(
        place, pieces, gain, weights, facts, devices // 2
    )
    with jax.named_scope("interaction_gathered"):
        near = lax.all_to_all(
            sent, "cand", 0, 0, tiled=True, axis_index_groups=same_core_groups()
        )
        far = to_sibling(near)
    partial = attend(queries, keys, values, near, far, facts, residual, weights)
    with jax.named_scope("heads_summed"):
        return lax.psum_scatter(partial, "mp", scatter_dimension=0, tiled=True)


def solution(mesh):
    in_specs = (
        P("cand", None, "mp"),
        P(),
        P(None, "cand", "mp"),
        P("mp", "cand"),
        P("cand"),
        P("cand"),
        P("cand"),
    )
    out_specs = P(("cand", "mp"), None)
    return jax.shard_map(shards, mesh=mesh, in_specs=in_specs, out_specs=out_specs, check_vma=False)
```

```python
import math

import jax
import jax.numpy as jnp
from jax import lax
from jax.experimental import pallas as pl
from jax.experimental.pallas import tpu as pltpu
from jax.sharding import PartitionSpec as P

HD = 128
EPS = 1e-05
NEGATIVE = -1e30
VMEM_LIMIT = 48 * 1024 * 1024
F32 = jnp.float32
BF16 = jnp.bfloat16
NT = (((1,), (1,)), ((), ()))


def along(shard, axis, by):
    length = lax.axis_size(axis)
    return lax.ppermute(shard, axis, [(i, (i + by) % length) for i in range(length)])


def to_sibling(shard):
    length = lax.axis_size("cand")
    return lax.ppermute(shard, "cand", [(i, i ^ 1) for i in range(length)])


def same_core_groups():
    length = lax.axis_size("cand")
    return [list(range(core, length, 2)) for core in range(2)]


ALONG_Z = 8


def x_groups():
    length = lax.axis_size("cand")
    step = 2 * ALONG_Z
    return [list(range(first, length, step)) for first in range(step)]


def z_groups():
    length = lax.axis_size("cand")
    step = 2 * ALONG_Z
    return [list(range(x, x + step)) for x in range(0, length, step)]


def to_outer(shard):
    length = lax.axis_size("cand")
    pairs = [(i, (i + (1 if i % 2 else length - 1)) % length) for i in range(length)]
    return lax.ppermute(shard, "cand", pairs)


def opposed(shard, by):
    chips, parts = lax.axis_size("cand"), lax.axis_size("mp")
    pairs = []
    for device in range(chips):
        signed = by if device % 2 == 0 else -by
        for part in range(parts):
            pairs.append((device * parts + part, device * parts + (part + signed) % parts))
    return lax.ppermute(shard, ("cand", "mp"), pairs)


def pick_kernel(table, passages, inner, outer, kept):
    me = lax.axis_index("cand")
    devices = lax.axis_size("cand")
    slots, length, width = passages.shape
    row = lax.broadcasted_iota(jnp.int32, (16, width), 0)
    lane = lax.broadcasted_iota(jnp.int32, (16, width), 1)
    number = [jnp.int32(0)] * 3
    core = lax.rem(me, 2)
    inward = jnp.where(core == 0, 1, devices - 1)
    outward = jnp.where(core == 0, devices - 1, 1)
    for slot in range(slots):
        ahead = lax.rem(table[0, slot] - me + devices, devices)
        facts = jnp.where(lane < width // 2, table[1, slot], table[2, slot]).astype(F32)
        tail = passages[slot, length - 16 :, :].astype(F32)
        tail = jnp.where(row == 15, facts, tail).astype(BF16)
        for which, (wanted, target) in enumerate(((inward, inner), (outward, outer), (0, kept))):
            hit = ahead == wanted
            place = jnp.minimum(number[which], target.shape[0] - 1)

            @pl.when(hit)
            def _():
                target[place, : length - 16, :] = passages[slot, : length - 16, :]
                target[place, length - 16 :, :] = tail

            number[which] = number[which] + hit.astype(jnp.int32)


def pick(table, passages):
    slots, length, width = passages.shape
    smem = pl.BlockSpec(memory_space=pltpu.SMEM)
    vmem = pl.BlockSpec(memory_space=pltpu.VMEM)
    shape = lambda n: jax.ShapeDtypeStruct((n, length, width), BF16)
    return pl.pallas_call(
        pick_kernel,
        out_shape=(shape(2), shape(2), shape(slots - 4)),
        in_specs=[smem, vmem],
        out_specs=(vmem, vmem, vmem),
        compiler_params=pltpu.CompilerParams(vmem_limit_bytes=VMEM_LIMIT),
    )(table, passages)


def copy_kernel(w_qkv, w_out, copies):
    depth = w_qkv.shape[1]
    for copy in range(copies.shape[0]):
        for part in range(3):
            copies[copy, part * depth : (part + 1) * depth, :] = w_qkv[part]
        copies[copy, 3 * depth :, :] = w_out[...]


def copied(w_qkv, w_out, number):
    vmem = pl.BlockSpec(memory_space=pltpu.VMEM)
    depth = 3 * w_qkv.shape[1] + w_out.shape[0]
    return pl.pallas_call(
        copy_kernel,
        out_shape=jax.ShapeDtypeStruct((number, depth, w_qkv.shape[2]), BF16),
        in_specs=[vmem, vmem],
        out_specs=vmem,
        compiler_params=pltpu.CompilerParams(vmem_limit_bytes=VMEM_LIMIT),
    )(w_qkv, w_out)


def pack_kernel(inner, kept, outer, packed, facts):
    rows = packed.shape[0]
    length = kept.shape[1]
    first = lax.rem(lax.axis_index("cand"), 2) == 0
    blocks = (
        [jnp.where(first, outer[i], inner[i]) for i in range(outer.shape[0])]
        + [kept[i] for i in range(kept.shape[0])]
        + [jnp.where(first, inner[i], outer[i]) for i in range(inner.shape[0])]
    )
    position = lax.broadcasted_iota(jnp.int32, (rows, length), 0)
    offset = lax.broadcasted_iota(jnp.int32, (rows, length), 1)
    start = jnp.zeros((1, length), jnp.int32)
    total = jnp.zeros(packed.shape, F32)
    for slot, block in enumerate(blocks):
        fact = block[length - 16 :, :].astype(F32)[15:16, :]
        facts[slot : slot + 1, :] = fact
        count = fact[:, :length].astype(jnp.int32)
        chosen = (position == start + offset) & (offset < count)
        total = total + jnp.dot(
            chosen.astype(F32).astype(BF16), block, preferred_element_type=F32
        )
        start = start + count
    packed[...] = total.astype(BF16)


def pack(inner, kept, outer):
    slots = inner.shape[0] + kept.shape[0] + outer.shape[0]
    length, width = kept.shape[1:]
    vmem = pl.BlockSpec(memory_space=pltpu.VMEM)
    return pl.pallas_call(
        pack_kernel,
        out_shape=(
            jax.ShapeDtypeStruct((slots * length // 2, width), BF16),
            jax.ShapeDtypeStruct((slots, width), F32),
        ),
        in_specs=[vmem] * 3,
        out_specs=(vmem, vmem),
        compiler_params=pltpu.CompilerParams(vmem_limit_bytes=VMEM_LIMIT),
    )(inner, kept, outer)


def hold_kernel(source, held):
    held[...] = source[...]


def hold(array):
    vmem = pl.BlockSpec(memory_space=pltpu.VMEM)
    return pl.pallas_call(
        hold_kernel,
        out_shape=jax.ShapeDtypeStruct(array.shape, array.dtype),
        in_specs=[vmem],
        out_specs=vmem,
        compiler_params=pltpu.CompilerParams(vmem_limit_bytes=VMEM_LIMIT),
    )(array)


def project_kernel(place, *refs):
    pieces, (gain, facts, weights), outs = refs[:9], refs[9:12], refs[12:18]
    scaled, factor, keys, values, residual, sent = outs
    final, kept, held, arrived = refs[18:]
    rows, width = pieces[0].shape
    parts, share = kept.shape[:2]
    along_z, _, along_x, depth, columns = held.shape
    depth = depth // 2
    fetches = [
        pltpu.make_async_copy(
            weights.at[:, :, x, pl.ds(depth, 2 * depth), :], held.at[:, :, x], arrived.at[x]
        )
        for x in range(along_x)
    ]
    for fetch in fetches:
        fetch.start()
    final[: rows // 2, :] = pieces[7][...]
    final[rows // 2 :, :] = pieces[8][...]
    row = pl.ds(pl.multiple_of(place[8] * share, share), share)
    square = jnp.zeros((rows, HD), F32)
    for number, source in enumerate((*pieces[:7], final)):
        at = place[number]
        kept[at] = source[row, :]
        x = source[...].astype(F32)
        scaled[at] = (x * gain[at]).astype(BF16)
        x = x * x
        for lane in range(0, width, HD):
            square = square + x[:, lane : lane + HD]
    for part in range(parts):
        residual[:, part * width : (part + 1) * width] = kept[part]
    totals = [jnp.zeros((rows, columns), F32) for _ in range(2)]
    for x in range(along_x):
        fetches[x].wait()
        for side in range(2):
            strip = slice(side * along_z // 2, (side + 1) * along_z // 2)
            for part in range(2):
                block = held[strip, :, x, part * depth : (part + 1) * depth, :]
                totals[part] = totals[part] + jnp.dot(
                    scaled[2 * x + side],
                    block.reshape(-1, columns),
                    preferred_element_type=F32,
                )
    inverse = lax.rsqrt(jnp.sum(square, axis=1, keepdims=True) / (parts * width) + EPS)
    done = [(total * inverse).astype(BF16) for total in totals]
    keys[...], values[...] = done
    factor[...] = jnp.broadcast_to(inverse, factor.shape)
    slots = facts.shape[0]
    slot_of = lax.broadcasted_iota(jnp.int32, (2 * slots, rows), 0) % slots
    position = lax.broadcasted_iota(jnp.int32, (2 * slots, rows), 1)
    start = jnp.zeros((1, rows), jnp.int32)
    first = jnp.zeros((2 * slots, rows), jnp.int32)
    asked = jnp.zeros((2 * slots, HD), jnp.int32)
    for slot in range(slots):
        here = slot_of == slot
        first = jnp.where(here, start, first)
        asked = jnp.where(
            here[:, :HD],
            facts[slot : slot + 1, width // 2 : width // 2 + HD].astype(jnp.int32),
            asked,
        )
        start = start + facts[slot : slot + 1, :rows].astype(jnp.int32)
    chosen = (first == position).astype(F32).astype(BF16)
    mark = (asked == position[:, :HD]).astype(F32).astype(BF16)
    key_rows = jnp.dot(chosen, done[0], preferred_element_type=F32).astype(BF16)
    value_rows = jnp.dot(chosen, done[1], preferred_element_type=F32).astype(BF16)
    for copy in range(sent.shape[0] // (2 * slots)):
        there = slice(copy * 2 * slots, (copy + 1) * 2 * slots)
        sent[there, :columns] = key_rows
        sent[there, columns : 2 * columns] = value_rows
        sent[there, 2 * columns :] = mark


def project(place, pieces, gain, weights, facts, copies):
    rows, width = pieces[0].shape
    along_z, cores, along_x, depth, columns = weights.shape
    depth = depth // 2
    parts = gain.shape[0]
    vmem = pl.BlockSpec(memory_space=pltpu.VMEM)
    shape = lambda *sizes: jax.ShapeDtypeStruct(sizes, BF16)
    return pl.pallas_call(
        project_kernel,
        out_shape=(
            shape(parts, rows, width),
            jax.ShapeDtypeStruct((rows, columns), F32),
            shape(rows, columns),
            shape(rows, columns),
            shape(rows // parts, parts * width),
            shape(copies * facts.shape[0], 2 * columns + HD),
        ),
        in_specs=[pl.BlockSpec(memory_space=pltpu.SMEM)]
        + [vmem] * 11
        + [pl.BlockSpec(memory_space=pl.ANY)],
        out_specs=(vmem,) * 6,
        scratch_shapes=[
            pltpu.VMEM((rows, width), BF16),
            pltpu.VMEM((parts, rows // parts, width), BF16),
            pltpu.VMEM((along_z, cores, along_x, depth, columns), BF16),
            pltpu.SemaphoreType.DMA((along_x,)),
        ],
        compiler_params=pltpu.CompilerParams(vmem_limit_bytes=VMEM_LIMIT),
    )(place, *pieces, gain, facts, weights)


def query_kernel(scaled, factor, weights, queries, held, arrived):
    along_z, _, along_x, depth, columns = held.shape
    fetches = [
        pltpu.make_async_copy(
            weights.at[:, :, x, pl.ds(0, depth), :], held.at[:, :, x], arrived.at[x]
        )
        for x in range(along_x)
    ]
    for fetch in fetches:
        fetch.start()
    total = jnp.zeros(queries.shape, F32)
    for x in range(along_x):
        fetches[x].wait()
        for side in range(2):
            strip = slice(side * along_z // 2, (side + 1) * along_z // 2)
            total = total + jnp.dot(
                scaled[2 * x + side],
                held[strip, :, x].reshape(-1, columns),
                preferred_element_type=F32,
            )
    queries[...] = (total * factor[...]).astype(BF16)


def project_queries(scaled, factor, weights):
    along_z, cores, along_x, depth, columns = weights.shape
    vmem = pl.BlockSpec(memory_space=pltpu.VMEM)
    return pl.pallas_call(
        query_kernel,
        out_shape=jax.ShapeDtypeStruct(factor.shape, BF16),
        in_specs=[vmem, vmem, pl.BlockSpec(memory_space=pl.ANY)],
        out_specs=vmem,
        scratch_shapes=[
            pltpu.VMEM((along_z, cores, along_x, depth // 4, columns), BF16),
            pltpu.SemaphoreType.DMA((along_x,)),
        ],
        compiler_params=pltpu.CompilerParams(vmem_limit_bytes=VMEM_LIMIT),
    )(scaled, factor, weights)


def attend_kernel(*refs):
    queries, keys, values, near, far, facts, residual, weights, out, held, done, arrived, left = refs
    share = residual.shape[0]
    own = pl.ds(pl.multiple_of(lax.axis_index("mp") * share, share), share)
    rows, columns = near.shape[0], 2 * HD
    along_z, cores, along_x, depth, _ = held.shape
    width = along_z * cores * depth
    fetches = [
        pltpu.make_async_copy(
            weights.at[:, :, x, pl.ds(3 * depth, depth), :], held.at[:, :, x], arrived.at[x]
        )
        for x in range(along_x)
    ]
    for fetch in fetches:
        fetch.start()
    slots = facts.shape[0]
    half = facts.shape[1] // 2
    here = lax.axis_index("cand") // 2 * slots
    down = lax.broadcasted_iota(jnp.int32, (rows, rows), 0)
    across = lax.broadcasted_iota(jnp.int32, (rows, rows), 1)
    slot_down = jnp.zeros((rows, rows), jnp.int32)
    slot_across = jnp.zeros((rows, rows), jnp.int32)
    end = jnp.zeros((1, rows), jnp.int32)
    for slot in range(slots):
        end = end + facts[slot : slot + 1, :rows].astype(jnp.int32)
        if slot < slots - 1:
            slot_down = slot_down + (down >= end).astype(jnp.int32)
            slot_across = slot_across + (across >= end).astype(jnp.int32)
    asked = jnp.zeros((rows, HD), jnp.int32)
    for slot in range(slots):
        asked = jnp.where(
            slot_down[:, :HD] == slot,
            facts[slot : slot + 1, half : half + HD].astype(jnp.int32),
            asked,
        )
    local = ((slot_down == slot_across) & (down < end) & (across < end)) | (down == across)
    mark = (asked == across[:, :HD]).astype(F32).astype(BF16)
    same = lambda other: lax.dot_general(
        mark, other[:, 2 * columns :], NT, preferred_element_type=F32
    ) > 0.5
    masks = [local, same(near) & (across != here + slot_down), same(far)]
    scale = 1.0 / math.sqrt(HD)
    heads = []
    for head in range(columns // HD):
        lanes = slice(head * HD, (head + 1) * HD)
        value_lanes = slice(columns + head * HD, columns + (head + 1) * HD)
        query = queries[:, lanes]
        scores = [
            jnp.where(
                mask,
                lax.dot_general(query, key, NT, preferred_element_type=F32) * scale,
                NEGATIVE,
            )
            for mask, key in zip(masks, (keys[:, lanes], near[:, lanes], far[:, lanes]))
        ]
        peak = jnp.maximum(jnp.maximum(scores[0], scores[1]), scores[2])
        peak = jnp.max(peak, axis=1, keepdims=True)
        raised = [jnp.exp(score - peak) for score in scores]
        bottom = jnp.sum(raised[0] + raised[1] + raised[2], axis=1, keepdims=True)
        top = jnp.zeros((rows, HD), F32)
        for part, value in zip(
            raised, (values[:, lanes], near[:, value_lanes], far[:, value_lanes])
        ):
            top = top + jnp.dot(part.astype(BF16), value, preferred_element_type=F32)
        heads.append(jnp.where(down[:, :HD] < end[:, :HD], top / bottom, 0.0).astype(BF16))
    attended = jnp.concatenate(heads, axis=1)
    leaving = []
    for x in range(along_x):
        fetches[x].wait()
        for z in range(0, along_z, 2):
            block = held[z : z + 2, :, x].reshape(-1, columns)
            at = x * width + z * cores * depth
            done[:, at : at + 2 * cores * depth] = lax.dot_general(
                attended, block, NT, preferred_element_type=F32
            ).astype(BF16)
        lanes = pl.ds(x * width, width)
        mixed = done[own, lanes].astype(F32) + residual[:, lanes].astype(F32)
        done[own, lanes] = mixed.astype(BF16)
        leaving.append(pltpu.make_async_copy(done.at[:, lanes], out.at[:, lanes], left.at[x]))
        leaving[x].start()
    for copy in leaving:
        copy.wait()


def attend(queries, keys, values, near, far, facts, residual, weights):
    along_z, cores, along_x, depth, inner = weights.shape
    depth = depth // 4
    rows = queries.shape[0]
    columns = along_z * along_x * cores * depth
    vmem = pl.BlockSpec(memory_space=pltpu.VMEM)
    anywhere = pl.BlockSpec(memory_space=pl.ANY)
    return pl.pallas_call(
        attend_kernel,
        out_shape=jax.ShapeDtypeStruct((rows, columns), BF16),
        in_specs=[vmem] * 7 + [anywhere],
        out_specs=anywhere,
        scratch_shapes=[
            pltpu.VMEM((along_z, cores, along_x, depth, inner), BF16),
            pltpu.VMEM((rows, columns), BF16),
            pltpu.SemaphoreType.DMA((along_x,)),
            pltpu.SemaphoreType.DMA((along_x,)),
        ],
        compiler_params=pltpu.CompilerParams(vmem_limit_bytes=VMEM_LIMIT),
    )(queries, keys, values, near, far, facts, residual, weights)


def shards(passages, norm_gain, w_qkv, w_out, counts, owners, query_of):
    devices = lax.axis_size("cand")
    parts = lax.axis_size("mp")
    me = lax.axis_index("mp")
    core = lax.rem(lax.axis_index("cand"), 2)
    along_x = devices // (2 * ALONG_Z)
    with jax.named_scope("weights_gathered"):
        copies = copied(w_qkv, w_out.T, along_x)
        from_x = lax.all_to_all(
            copies.reshape(-1, 2 * HD), "cand", 0, 0, tiled=True, axis_index_groups=x_groups()
        ).reshape(copies.shape)
        weights = lax.all_gather(from_x, "cand", axis_index_groups=z_groups())
        weights = weights.reshape((ALONG_Z, 2) + from_x.shape)
    with jax.named_scope("passages_handed_over"):
        inner, outer, kept = pick(jnp.stack([owners, counts, query_of]), passages)
        from_x, inner, outer = lax.optimization_barrier((from_x, inner, outer))
        inner, outer = to_sibling(inner), to_outer(outer)
    with jax.named_scope("passages_packed"):
        packed, facts = pack(inner, kept, outer)
    with jax.named_scope("features_gathered"):
        half = packed.shape[0] // 2
        third, fourth = opposed(packed, 2), opposed(packed, -2)
        first, second = opposed(packed, 1), opposed(packed, -1)
        gain = hold(norm_gain.reshape(parts, 1, -1))
        first, second, third, fourth, gain = lax.optimization_barrier(
            (first, second, third, fourth, gain)
        )
        fifth, sixth = opposed(third, 1), opposed(fourth, -1)
        last = (opposed(third[:half], 2), opposed(fourth[half:], -2))
        pieces = [packed, first, second, third, fourth, fifth, sixth, *last]
    away = jnp.array([0, -1, 1, -2, 2, -3, 3, 4, 0], jnp.int32)
    place = lax.rem(me + parts + away * (1 - 2 * core), parts).astype(jnp.int32)
    scaled, factor, keys, values, residual, sent = project(
        place, pieces, gain, weights, facts, devices // 2
    )
    with jax.named_scope("interaction_gathered"):
        near = lax.all_to_all(
            sent, "cand", 0, 0, tiled=True, axis_index_groups=same_core_groups()
        )
        far = to_sibling(near)
    queries = project_queries(scaled, factor, weights)
    partial = attend(queries, keys, values, near, far, facts, residual, weights)
    with jax.named_scope("heads_summed"):
        return lax.psum_scatter(partial, "mp", scatter_dimension=0, tiled=True)


def solution(mesh):
    in_specs = (
        P("cand", None, "mp"),
        P(),
        P(None, "cand", "mp"),
        P("mp", "cand"),
        P("cand"),
        P("cand"),
        P("cand"),
    )
    out_specs = P(("cand", "mp"), None)
    return jax.shard_map(shards, mesh=mesh, in_specs=in_specs, out_specs=out_specs, check_vma=False)
```
